32 devices in a mesh: dp: 8 (over y, x, core), tensor: 4 (over z).
Axes of the slice: x: 2, y: 2, z: 4, core: 2. Of those that a mesh axis runs over, the one named last changes fastest.
Arguments:
- images: bfloat16 [24, 729, 1152], P('dp'), may hold values from -6 to 6
- counts: int32 [8], P('dp'), may hold values from 2 to 3, as said below
- cotangent: bfloat16 [24, 729, 1152], P('dp'), may hold values from -6 to 6
- query_w: bfloat16 [1152, 1152], P(None, 'tensor'), may hold values from -0.1875 to 0.1875
- query_b: float32 [1152], P('tensor'), may hold values from -3 to 3
- key_w: bfloat16 [1152, 1152], P(None, 'tensor'), may hold values from -0.1875 to 0.1875
- value_w: bfloat16 [1152, 1152], P(None, 'tensor'), may hold values from -0.1875 to 0.1875
- value_b: float32 [1152], P('tensor'), may hold values from -0.3 to 0.3
- out_w: bfloat16 [1152, 1152], P('tensor'), may hold values from -3 to 3
- out_b: float32 [1152], replicated, may hold values from -3 to 3
- norm1_gain: float32 [1152], replicated, may hold values from 0.25 to 1.75
- norm1_shift: float32 [1152], replicated, may hold values from -0.3 to 0.3
- norm2_gain: float32 [1152], replicated, may hold values from 0.25 to 1.75
- norm2_shift: float32 [1152], replicated, may hold values from -2 to 2
- expand_w: bfloat16 [1152, 4304], P(None, 'tensor'), may hold values from -0.1875 to 0.1875
- expand_b: float32 [4304], P('tensor'), may hold values from -3 to 3
- shrink_w: bfloat16 [4304, 1152], P('tensor'), may hold values from -0.09375 to 0.09375
- shrink_b: float32 [1152], replicated, may hold values from -3 to 3
Outputs:
- output: bfloat16 [24, 729, 1152], P('dp')
- input_grad: float32 [24, 729, 1152], P('dp')
- grad_query_w: float32 [1152, 1152], P('dp', 'tensor')
- grad_query_b: float32 [1152], P('tensor')
- grad_key_w: float32 [1152, 1152], P('dp', 'tensor')
- grad_value_w: float32 [1152, 1152], P('dp', 'tensor')
- grad_value_b: float32 [1152], P('tensor')
- grad_out_w: float32 [1152, 1152], P('tensor', 'dp')
- grad_out_b: float32 [1152], replicated
- grad_norm1_gain: float32 [1152], replicated
- grad_norm1_shift: float32 [1152], replicated
- grad_norm2_gain: float32 [1152], replicated
- grad_norm2_shift: float32 [1152], replicated
- grad_expand_w: float32 [1152, 4304], P('dp', 'tensor')
- grad_expand_b: float32 [4304], P('tensor')
- grad_shrink_w: float32 [4304, 1152], P('tensor', 'dp')
- grad_shrink_b: float32 [1152], replicated
- clipped_query_w: bfloat16 [1152, 1152], P(None, 'tensor')
- clipped_key_w: bfloat16 [1152, 1152], P(None, 'tensor')
The draws below stay inside these ranges and needn't reach their ends.
Inputs may be any that keep to these rules, and one draw needn't show every extreme that they name: Each dp index holds 3 image slots, the first counts of them live; in every draw some index has 3 live slots and another 3 - 1.
All inputs are finite; a program needn't handle non-finite values.
Results may differ from the reference program's by a relative error of at most 0.02.
Values may be sent and summed in bfloat16 or wider, within the bound.
A program may use at most 192 MiB of HBM per device.

```python
import jax
import jax.numpy as jnp
from jax import lax

D = 1152
HEADS = 16
HD = 72
FF = 4304
L = 729
SLOTS = 3
IMG_SLOTS = 24
N_DP = 8
N_TENSOR = 4


def draw_counts(key, part):
    first, second, third = jax.random.split(key, 3)
    dropped = (jax.random.randint(first, (N_DP,), 0, 10) < 3).astype(jnp.int32)
    result = SLOTS - dropped
    full_index = jax.random.randint(second, (), 0, N_DP)
    short_index = (full_index + 1 + jax.random.randint(third, (), 0, N_DP - 1)) % N_DP
    result = result.at[full_index].set(SLOTS)
    result = result.at[short_index].set(SLOTS - 1)
    return result.astype(jnp.int32)


def levels(own_key, dims, cuts, low, largest):
    def one(dim, blocks):
        heights = jax.random.uniform(jax.random.fold_in(jax.random.fold_in(own_key, 6), dim), (blocks,), jnp.float32, low / len(cuts), largest / len(cuts))
        return jnp.repeat(jnp.exp(heights), dims[dim] // blocks).reshape((-1,) + (1,) * (len(dims) - dim - 1))

    factor_of = one(*cuts[0])
    for cut in cuts[1:]:
        factor_of = factor_of * one(*cut)
    return factor_of


def noise(rng, dims, scale, reach, pieces=(), kind=jnp.bfloat16):
    level = levels(rng, dims, pieces, -0.22, 0.18) if pieces else 1.0
    entries = jax.random.normal(rng, dims, jnp.float32) * scale * level
    return jnp.minimum(jnp.maximum(entries, -reach), reach).astype(kind)


def setup_inputs(seed: int = 0) -> dict:
    keys = jax.random.split(jax.random.key(seed), 19)
    images = noise(keys[0], (IMG_SLOTS, L, D), 1.0, 6.0, ((0, 8),))
    counts = draw_counts(jax.random.fold_in(keys[18], 71), 0)
    cotangent = noise(keys[2], (IMG_SLOTS, L, D), 1.0, 6.0, ((0, 8),))
    query_w = noise(keys[3], (D, D), D ** -0.5, 0.1875, ((1, 4),))
    query_b = noise(keys[4], (D,), 0.5, 3.0, ((0, 4),), jnp.float32)
    key_w = noise(keys[5], (D, D), D ** -0.5, 0.1875, ((1, 4),))
    value_w = noise(keys[6], (D, D), D ** -0.5, 0.1875, ((1, 4),))
    value_b = noise(keys[7], (D,), 0.05, 0.3, ((0, 4),), jnp.float32)
    out_w = noise(keys[8], (D, D), (max(D // 256, 1)) ** -0.5, 3.0, ((0, 4),))
    out_b = noise(keys[9], (D,), 0.5, 3.0, (), jnp.float32)
    norm1_gain = jnp.clip(1.0 + 0.15 * jax.random.normal(keys[10], (D,), jnp.float32), 0.25, 1.75)
    norm1_shift = noise(keys[11], (D,), 0.05, 0.3, (), jnp.float32)
    norm2_gain = jnp.clip(1.0 + 0.15 * jax.random.normal(keys[12], (D,), jnp.float32), 0.25, 1.75)
    norm2_shift = noise(keys[13], (D,), 0.3, 2.0, (), jnp.float32)
    expand_w = noise(keys[14], (D, FF), D ** -0.5, 0.1875, ((1, 4),))
    expand_b = noise(keys[15], (FF,), 0.5, 3.0, ((0, 4),), jnp.float32)
    shrink_w = noise(keys[16], (FF, D), FF ** -0.5, 0.09375, ((0, 4),))
    shrink_b = noise(keys[17], (D,), 0.5, 3.0, (), jnp.float32)
    return dict(images=images, counts=counts, cotangent=cotangent, query_w=query_w, query_b=query_b, key_w=key_w, value_w=value_w, value_b=value_b, out_w=out_w, out_b=out_b, norm1_gain=norm1_gain, norm1_shift=norm1_shift, norm2_gain=norm2_gain, norm2_shift=norm2_shift, expand_w=expand_w, expand_b=expand_b, shrink_w=shrink_w, shrink_b=shrink_b)


norm_eps = 1e-06
clip_limit = 3.0
tanh_coef = 0.7978845608028654
cube_coef = 0.044715
highest = lax.Precision.HIGHEST

@jax.custom_vjp
def low(v):
    return lax.optimization_barrier(v.astype(jnp.bfloat16)).astype(jnp.float32)

@jax.custom_vjp
def low_back(v):
    return v

def low_keep(v):
    return (low(v), None)

def low_pass(kept, grad):
    return (grad,)

def back_keep(v):
    return (v, None)

def back_low(kept, grad):
    return (low(grad),)
low.defvjp(low_keep, low_pass)
low_back.defvjp(back_keep, back_low)

def layer_norm(values, gain, shift):
    centre = lax.optimization_barrier(jnp.mean(values, axis=-1, keepdims=True))
    centred = values - centre
    spread = lax.optimization_barrier(jnp.mean(centred * centred, axis=-1, keepdims=True))
    return centred * lax.rsqrt(spread + norm_eps) * gain + shift

def gelu_tanh(pre_act):
    return 0.5 * pre_act * (1.0 + jnp.tanh(tanh_coef * (pre_act + cube_coef * pre_act * pre_act * pre_act)))

def forward(inputs, query_w, query_b, key_w, value_w, value_b, out_w, out_b, norm1_gain, norm1_shift, norm2_gain, norm2_shift, expand_w, expand_b, shrink_w, shrink_b):
    slot_count, length, model_width = inputs.shape
    groups = N_TENSOR
    sub_width = model_width // groups
    sub_hidden = expand_w.shape[1] // groups
    score_scale = 1.0 / jnp.sqrt(jnp.float32(HD))
    flat = inputs.reshape(slot_count * length, model_width)
    first_in = low(layer_norm(flat, norm1_gain, norm1_shift))
    first_copies = low_back(jnp.broadcast_to(first_in, (groups,) + first_in.shape))

    def project(weight):
        parted = jnp.einsum('gtd,dgc->tgc', first_copies, weight.reshape(model_width, groups, sub_width), precision=highest)
        return parted.reshape(-1, model_width)
    queries = low(low_back(project(query_w)) + query_b)
    key_rows = low(low_back(project(key_w)))
    value_rows = low(low_back(project(value_w)) + value_b)

    def attend(slot_block):
        query_blk, key_blk, value_blk = slot_block
        scores = low_back(jnp.einsum('qhc,khc->hqk', query_blk, key_blk, precision=highest) * score_scale)
        row_top = lax.optimization_barrier(jnp.max(scores, axis=-1, keepdims=True))
        exponent = jnp.exp(scores - row_top)
        attn_prob = exponent / lax.optimization_barrier(jnp.sum(exponent, axis=-1, keepdims=True))
        mixture = jnp.einsum('hqk,khc->qhc', low(attn_prob), value_blk, precision=highest)
        return (mixture, lax.optimization_barrier(jnp.max(row_top, axis=(1, 2))))
    per_head = (slot_count, length, HEADS, HD)
    attended, head_tops = lax.map(jax.checkpoint(attend), (queries.reshape(per_head), key_rows.reshape(per_head), value_rows.reshape(per_head)))
    attended = low_back(low(attended.reshape(-1, model_width)))
    partial_out = jnp.einsum('tgc,gcd->gtd', attended.reshape(-1, groups, sub_width), out_w.reshape(groups, sub_width, model_width), precision=highest)
    midway = flat + low_back(lax.optimization_barrier(jnp.sum(low(partial_out), axis=0))) + out_b
    second_in = low(layer_norm(midway, norm2_gain, norm2_shift))
    second_copies = low_back(jnp.broadcast_to(second_in, (groups,) + second_in.shape))
    pre_prod = jnp.einsum('gtd,dgf->tgf', second_copies, expand_w.reshape(model_width, groups, sub_hidden), precision=highest)
    pre_act = low_back(pre_prod) + expand_b.reshape(groups, sub_hidden)
    activated = low(gelu_tanh(pre_act))
    partial_mlp = jnp.einsum('tgf,gfd->gtd', activated, shrink_w.reshape(groups, sub_hidden, model_width), precision=highest)
    result = midway + lax.optimization_barrier(jnp.sum(low(partial_mlp), axis=0)) + shrink_b
    return (result.reshape(inputs.shape), head_tops)

def reference(images, counts, cotangent, query_w, query_b, key_w, value_w, value_b, out_w, out_b, norm1_gain, norm1_shift, norm2_gain, norm2_shift, expand_w, expand_b, shrink_w, shrink_b):
    slot_index = jnp.arange(images.shape[0], dtype=jnp.int32)
    owner = (slot_index // SLOTS).astype(jnp.int32)
    live = (slot_index % SLOTS < counts[owner]).astype(jnp.float32)
    params = tuple((item.astype(jnp.float32) for item in (query_w, query_b, key_w, value_w, value_b, out_w, out_b, norm1_gain, norm1_shift, norm2_gain, norm2_shift, expand_w, expand_b, shrink_w, shrink_b)))
    inputs = images.astype(jnp.float32)
    result, vjp_fn, head_tops = jax.vjp(forward, inputs, *params, has_aux=True)
    weight = live[:, None, None]
    grads = vjp_fn(cotangent.astype(jnp.float32) * weight)
    output = (result * weight).astype(jnp.bfloat16)
    masked = jnp.where(live[:, None] > 0.0, head_tops, jnp.float32(-1e+30))
    logit_top = lax.optimization_barrier(jnp.max(masked, axis=0))
    factor = jnp.sqrt(clip_limit / jnp.maximum(logit_top, clip_limit))
    column_factor = jnp.repeat(factor, HD)
    clipped_query = (params[0] * column_factor).astype(jnp.bfloat16)
    clipped_key = (params[2] * column_factor).astype(jnp.bfloat16)
    return (output, grads[0], grads[1], grads[2], grads[3], grads[4], grads[5], grads[6], grads[7], grads[8], grads[9], grads[10], grads[11], grads[12], grads[13], grads[14], grads[15], clipped_query, clipped_key)
```

```python
import functools, math
import jax, jax.numpy as jnp
from jax import lax
from jax.experimental import pallas as pl
from jax.experimental.pallas import tpu as pltpu
from jax.sharding import PartitionSpec as P

HD=72; TOK=768
norm_eps=1e-06; clip_limit=3.0
SC=1/math.sqrt(HD); LOG2E=1.4426950408889634
RT=256
F32=jnp.float32; BF=jnp.bfloat16
tanh_coef=0.7978845608028654; cube_coef=0.044715
def nn(a,b): return jnp.dot(a,b,preferred_element_type=F32)
def nt(a,b): return lax.dot_general(a,b,(((1,),(1,)),((),())),preferred_element_type=F32)
def tn(a,b): return lax.dot_general(a,b,(((0,),(0,)),((),())),preferred_element_type=F32)
VM=pl.BlockSpec(memory_space=pltpu.VMEM)

def attn_fwd_kernel(length, first, W, qb, vb, acc_in, qkv, att, lse, tops, acc, *, heads):
    cw=heads*HD
    @pl.loop(0, TOK//RT)
    def _(i):
        rows=pl.ds(pl.multiple_of(i*RT,RT),RT)
        t=nn(first[rows,:], W[:, :3*cw])
        q=(t[:, :cw]+qb[...]).astype(BF); k=t[:, cw:2*cw].astype(BF); v=(t[:,2*cw:]+vb[...]).astype(BF)
        for h in range(heads):
            qkv[h,rows,:]=q[:,h*HD:(h+1)*HD]
            qkv[heads+h,rows,:]=k[:,h*HD:(h+1)*HD]
            qkv[2*heads+h,rows,:]=v[:,h*HD:(h+1)*HD]
    tops[...]=jnp.full(tops.shape,-1e30,F32)
    @pl.loop(0, TOK//RT)
    def _(i):
        rows=pl.ds(pl.multiple_of(i*RT,RT),RT)
        rid=lax.broadcasted_iota(jnp.int32,(RT,1),0)+i*RT
        cid=lax.broadcasted_iota(jnp.int32,(1,TOK),1)
        outs=[]
        for h in range(heads):
            s=nt(qkv[h,rows,:], qkv[heads+h])
            s=jnp.where(cid<length, s, -1e30)
            m=jnp.max(s,axis=1,keepdims=True)
            e=jnp.exp2((s-m)*(SC*LOG2E))
            l=jnp.sum(e,axis=1,keepdims=True)
            o=nn(e.astype(BF), qkv[2*heads+h])*(1.0/l)
            outs.append(o.astype(BF))
            lse[h,rows,:]=m*(SC*LOG2E)+jnp.log2(l)
            tops[h:h+1,:]=jnp.maximum(tops[h:h+1,:], jnp.max(jnp.where(rid<length,m,-1e30))*SC)
        a=jnp.concatenate(outs,axis=1)
        att[rows,:]=a
        acc[rows,:]=acc_in[rows,:]+nt(a, W[:,3*cw:])

def attn_fwd(first, W, qb, vb, acc, length):
    D=first.shape[1]; cw=W.shape[1]//4; heads=cw//HD
    return pl.pallas_call(functools.partial(attn_fwd_kernel,length,heads=heads),
        out_shape=(jax.ShapeDtypeStruct((3*heads,TOK,HD),BF),jax.ShapeDtypeStruct((TOK,cw),BF),
                   jax.ShapeDtypeStruct((heads,TOK,1),F32),jax.ShapeDtypeStruct((heads,128),F32),jax.ShapeDtypeStruct((TOK,D),F32)),
        in_specs=[VM]*5,out_specs=(VM,)*5,
        input_output_aliases={4:4},
        compiler_params=pltpu.CompilerParams(vmem_limit_bytes=48*2**20),
        cost_estimate=pl.CostEstimate(flops=2*TOK*(D*cw*4+heads*2*TOK*HD*3),bytes_accessed=20*2**20,transcendentals=heads*TOK*TOK),
        name="attn_fwd")(first,W,qb,vb,acc)

def mlp_kernel(second, secondT, gout, goutT, E, ST, eb, mlp_in, sec_in, gE, gST, geb, mlp, sec, act_s, gpre_s):
    geb[...]=jnp.zeros_like(geb)
    @pl.loop(0, TOK//RT)
    def _(i):
        rows=pl.ds(pl.multiple_of(i*RT,RT),RT)
        u=nn(second[rows,:],E[...])+eb[...]
        ga=nn(gout[rows,:],ST[...])
        u2=u*u
        t=jnp.tanh(u*(tanh_coef+(tanh_coef*cube_coef)*u2))
        hu=0.5*(1.0+t)
        act=(u*hu).astype(BF)
        act_s[rows,:]=act
        slope=hu+u*(0.5*tanh_coef)*(1.0-t*t)*(1.0+(3.0*cube_coef)*u2)
        gp=ga*slope
        geb[...]+=jnp.sum(gp,axis=0,keepdims=True)
        gpl=gp.astype(BF)
        gpre_s[rows,:]=gpl
        mlp[rows,:]=mlp_in[rows,:]+nt(act,ST[...])
        sec[rows,:]=sec_in[rows,:]+nt(gpl,E[...])
    @pl.loop(0, secondT.shape[0]//384)
    def _(i):
        rows=pl.ds(pl.multiple_of(i*384,128),384)
        gE[rows,:]=nn(secondT[rows,:],gpre_s[...]).astype(BF)
        gST[rows,:]=nn(goutT[rows,:],act_s[...]).astype(BF)

def mlp_call(second,secondT,gout,goutT,E,ST,eb,mlp,sec):
    D=second.shape[1]; F=E.shape[1]
    return pl.pallas_call(mlp_kernel,
        out_shape=(jax.ShapeDtypeStruct((D,F),BF),jax.ShapeDtypeStruct((D,F),BF),jax.ShapeDtypeStruct((1,F),F32),
                   jax.ShapeDtypeStruct((TOK,D),F32),jax.ShapeDtypeStruct((TOK,D),F32)),
        in_specs=[VM]*9,out_specs=(VM,)*5,
        input_output_aliases={7:3,8:4},
        scratch_shapes=[pltpu.VMEM((TOK,F),BF),pltpu.VMEM((TOK,F),BF)],
        compiler_params=pltpu.CompilerParams(vmem_limit_bytes=56*2**20),
        cost_estimate=pl.CostEstimate(flops=2*6*TOK*D*F,bytes_accessed=30*2**20,transcendentals=TOK*F),
        name="mlp")(second,secondT,gout,goutT,E,ST,eb,mlp,sec)

def attn_bwd_kernel(length, gmid, gmidT, firstT, W, qkv, att, lse, acc_in, gW, gqb, gvb, acc, ga_s, d_s, dk_s, dv_s, *, heads):
    cw=heads*HD
    @pl.loop(0, TOK//RT)
    def _(i):
        rows=pl.ds(pl.multiple_of(i*RT,RT),RT)
        g=nn(gmid[rows,:], W[:,3*cw:]).astype(BF)
        for h in range(heads):
            ga_s[h,rows,:]=g[:,h*HD:(h+1)*HD]
    gqb[...]=jnp.zeros_like(gqb)
    dk_s[...]=jnp.zeros_like(dk_s); dv_s[...]=jnp.zeros_like(dv_s)
    @pl.loop(0, TOK//RT)
    def _(i):
        rows=pl.ds(pl.multiple_of(i*RT,RT),RT)
        cid=lax.broadcasted_iota(jnp.int32,(1,TOK),1)
        dqs=[]
        for h in range(heads):
            q=qkv[h,rows,:]; k=qkv[heads+h]; v=qkv[2*heads+h]; g=ga_s[h,rows,:]
            s=nt(q,k)
            p=jnp.exp2(s*(SC*LOG2E)-lse[h,rows,:])
            p=jnp.where(cid<length,p,0.0)
            dp=nt(g,v)
            dd=jnp.sum(g.astype(F32)*att[rows,h*HD:(h+1)*HD].astype(F32),axis=1,keepdims=True)
            ds=(p*(dp-dd)).astype(BF)
            dqs.append(nn(ds,k)*SC)
            dk_s[h]+=tn(ds,q)
            dv_s[h]+=tn(p.astype(BF),g)
        dq=jnp.concatenate(dqs,axis=1)
        gqb[...]+=jnp.sum(dq,axis=0,keepdims=True)
        d_s[rows,:cw]=dq.astype(BF)
    dk=jnp.concatenate([dk_s[h]*SC for h in range(heads)],axis=1)
    d_s[:,cw:2*cw]=dk.astype(BF)
    dv=jnp.concatenate([dv_s[h] for h in range(heads)],axis=1)
    gvb[...]=jnp.sum(dv,axis=0,keepdims=True)
    d_s[:,2*cw:]=dv.astype(BF)
    @pl.loop(0, TOK//RT)
    def _(i):
        rows=pl.ds(pl.multiple_of(i*RT,RT),RT)
        acc[rows,:]=acc_in[rows,:]+nt(d_s[rows,:],W[:,:3*cw])
    @pl.loop(0, firstT.shape[0]//384)
    def _(i):
        rows=pl.ds(pl.multiple_of(i*384,128),384)
        gW[rows,:3*cw]=nn(firstT[rows,:],d_s[...]).astype(BF)
        gW[rows,3*cw:]=nn(gmidT[rows,:],att[...]).astype(BF)

def attn_bwd(gmid,gmidT,firstT,W,qkv,att,lse,acc,length):
    D=gmid.shape[1]; cw=W.shape[1]//4; heads=cw//HD
    return pl.pallas_call(functools.partial(attn_bwd_kernel,length,heads=heads),
        out_shape=(jax.ShapeDtypeStruct((D,4*cw),BF),jax.ShapeDtypeStruct((1,cw),F32),jax.ShapeDtypeStruct((1,cw),F32),jax.ShapeDtypeStruct((TOK,D),F32)),
        in_specs=[VM]*8,out_specs=(VM,)*4,
        input_output_aliases={7:3},
        scratch_shapes=[pltpu.VMEM((heads,TOK,HD),BF),pltpu.VMEM((TOK,3*cw),BF),pltpu.VMEM((heads,TOK,HD),F32),pltpu.VMEM((heads,TOK,HD),F32)],
        compiler_params=pltpu.CompilerParams(vmem_limit_bytes=56*2**20),
        cost_estimate=pl.CostEstimate(flops=2*TOK*(D*cw*8+heads*5*TOK*HD*3),bytes_accessed=25*2**20,transcendentals=heads*TOK*TOK),
        name="attn_bwd")(gmid,gmidT,firstT,W,qkv,att,lse,acc)


def normalize(values):
    centre = jnp.mean(values, axis=-1, keepdims=True)
    centred = values - centre
    spread = jnp.mean(centred * centred, axis=-1, keepdims=True)
    inverse = lax.rsqrt(spread + norm_eps)
    return centred * inverse, inverse


def norm_back(grad_norm, normed, inverse, gain):
    scaled = grad_norm * gain
    first_mean = jnp.mean(scaled, axis=-1, keepdims=True)
    second_mean = jnp.mean(scaled * normed, axis=-1, keepdims=True)
    grad_input = inverse * (scaled - first_mean - normed * second_mean)
    return grad_input, jnp.sum(grad_norm * normed, axis=0), jnp.sum(grad_norm, axis=0)


def slot_table(d, groups):
    z = lax.axis_index("tensor")
    middle = 1 + d % 2
    return jnp.where(z == 0, 0, jnp.where(z == groups - 1, 1, 2)), (z == 0) | (z == groups - 1) | (z == middle)


def spread_general(own, groups):
    d, count = lax.axis_index("dp"), lax.axis_size("dp")
    rows = own.shape[0] // count
    piece = lax.dynamic_slice_in_dim(own, d * rows, rows, 0)
    piece = lax.all_gather(piece, "tensor")
    whole = lax.all_gather(piece, "dp", axis=1, tiled=True)
    return [whole[i] for i in range(groups)]


def collect_general(parts):
    part = lax.psum_scatter(jnp.stack(parts), "dp", scatter_dimension=1, tiled=True)
    return lax.psum_scatter(part, "tensor", scatter_dimension=0, tiled=True)[0].astype(F32)


def share_general(mine, d, groups):
    every = lax.all_gather(mine, "tensor")
    return jnp.stack([every[0], every[groups - 1], lax.dynamic_index_in_dim(every, 1 + d % 2, 0, keepdims=False)])


def shards(images, counts, cotangent, query_w, query_b, key_w, value_w, value_b, out_w, out_b, norm1_gain, norm1_shift,
           norm2_gain, norm2_shift, expand_w, expand_b, shrink_w, shrink_b):
    slots, length, width = images.shape
    groups = lax.axis_size("tensor")
    d, z = lax.axis_index("dp"), lax.axis_index("tensor")
    cw, fw = query_w.shape[1], expand_w.shape[1]
    heads = cw // HD
    slot, used = slot_table(d, groups)
    live = jnp.where(used & (slot < counts[0]), 1.0, 0.0).astype(F32)
    pad = lambda a: jnp.pad(a, ((0, TOK - length), (0, 0)))
    x = pad(lax.dynamic_index_in_dim(images, slot, 0, keepdims=False)).astype(F32)
    gout = pad(lax.dynamic_index_in_dim(cotangent, slot, 0, keepdims=False)) * live.astype(BF)
    gout_t = gout.T

    attn_own = jnp.concatenate([query_w, key_w, value_w, out_w.T], axis=1)
    mlp_own = jnp.concatenate([expand_w, shrink_w.T], axis=1)
    attn_ws = spread_general(attn_own, groups)
    mlp_ws = spread_general(mlp_own, groups)
    biases = lax.all_gather(jnp.concatenate([query_b, value_b, expand_b]), "tensor")
    shard_of = list(range(groups))

    normed1, inverse1 = normalize(x)
    first = (normed1 * norm1_gain + norm1_shift).astype(BF)
    first_t = first.T
    acc = x + out_b
    kept, tops = [], []
    for k in range(groups):
        b = biases[k]
        qkv, att, lse, top, acc = attn_fwd(first, attn_ws[k], b[None, :cw], b[None, cw:2 * cw], acc, length)
        kept.append((qkv, att, lse))
        tops.append(top[:, 0])
    midway = acc
    normed2, inverse2 = normalize(midway)
    second = (normed2 * norm2_gain + norm2_shift).astype(BF)
    second_t = second.T
    mlp = midway + shrink_b
    sec = jnp.zeros((TOK, width), F32)
    grad_mlp, geb = [], []
    for k in range(groups):
        w = mlp_ws[k]
        g_e, g_s, g_b, mlp, sec = mlp_call(second, second_t, gout, gout_t, w[:, :fw], w[:, fw:], biases[k][None, 2 * cw:], mlp, sec)
        grad_mlp.append(jnp.concatenate([g_e, g_s], axis=1))
        geb.append(g_b[0])
    output = (mlp[:length] * live).astype(BF)
    back2, gn2g, gn2s = norm_back(sec, normed2, inverse2, norm2_gain)
    gout32 = gout.astype(F32)
    gmid = gout32 + back2
    gmid_low = gmid.astype(BF)
    gmid_t = gmid_low.T
    acc = jnp.zeros((TOK, width), F32)
    grad_attn, gqb, gvb = [], [], []
    for k in range(groups):
        g_w, g_q, g_v, acc = attn_bwd(gmid_low, gmid_t, first_t, attn_ws[k], *kept[k], acc, length)
        grad_attn.append(g_w)
        gqb.append(g_q[0])
        gvb.append(g_v[0])
    back1, gn1g, gn1s = norm_back(acc, normed1, inverse1, norm1_gain)
    input_grad = ((gmid + back1) * live)[:length].astype(BF)

    outputs = share_general(output, d, groups)
    input_grads = share_general(input_grad, d, groups).astype(F32)
    sum_attn = collect_general(grad_attn)
    sum_mlp = collect_general(grad_mlp)
    vector = jnp.concatenate([jnp.stack(gqb + gvb, 0).reshape(-1), jnp.stack(geb).reshape(-1), jnp.sum(gmid, axis=0), jnp.sum(gout32, axis=0), gn1g, gn1s, gn2g, gn2s])
    vector = lax.psum(vector, ("dp", "tensor"))
    part = lambda start, size: lax.dynamic_slice_in_dim(vector, start, size, 0)
    whole, hidden = cw * groups, fw * groups
    tail = [vector[2 * whole + hidden + i * width:][:width] for i in range(6)]
    logit_top = lax.pmax(jnp.where(live > 0.0, jnp.stack(tops), -1e30), ("dp", "tensor"))
    logit_top = lax.dynamic_index_in_dim(logit_top, z, 0, keepdims=False)
    factor = jnp.sqrt(clip_limit / jnp.maximum(logit_top, clip_limit))
    column_factor = jnp.repeat(factor, HD)
    clipped_query = (query_w.astype(F32) * column_factor).astype(BF)
    clipped_key = (key_w.astype(F32) * column_factor).astype(BF)
    return (outputs, input_grads, sum_attn[:, :cw], part(z * cw, cw), sum_attn[:, cw:2 * cw], sum_attn[:, 2 * cw:3 * cw], part(whole + z * cw, cw),
            sum_attn[:, 3 * cw:].T, tail[0], tail[2], tail[3], tail[4], tail[5], sum_mlp[:, :fw], part(2 * whole + z * fw, fw), sum_mlp[:, fw:].T,
            tail[1], clipped_query, clipped_key)


def solution(mesh):
    columns, rows, vector = P(None, "tensor"), P("tensor", None), P("tensor")
    whole = P("dp", None, None)
    return jax.shard_map(
        shards, mesh=mesh,
        in_specs=(whole, P("dp"), whole, columns, vector, columns, columns, vector, rows, P(), P(), P(), P(), P(), columns, vector, rows, P()),
        out_specs=(whole, whole, P("dp", "tensor"), vector, P("dp", "tensor"), P("dp", "tensor"), vector, P("tensor", "dp"), P(), P(), P(), P(), P(),
                   P("dp", "tensor"), vector, P("tensor", "dp"), P(), columns, columns),
        check_vma=False)
```

```python
import functools
import math

import jax
import jax.numpy as jnp
from jax import lax
from jax.experimental import pallas as pl
from jax.experimental.pallas import tpu as pltpu
from jax.sharding import PartitionSpec as P

HD = 72
TOK = 768
RT = 256
SC = 1 / math.sqrt(HD)
LOG2E = 1.4426950408889634
F32 = jnp.float32
BF = jnp.bfloat16
norm_eps = 1e-06
clip_limit = 3.0
tanh_coef = 0.7978845608028654
cube_coef = 0.044715
VM = pl.BlockSpec(memory_space=pltpu.VMEM)
HB = pl.BlockSpec(memory_space=pl.ANY)
MESH = pl.DeviceIdType.MESH


def nn(a, b):
    return jnp.dot(a, b, preferred_element_type=F32)


def nt(a, b):
    return lax.dot_general(a, b, (((1,), (1,)), ((), ())), preferred_element_type=F32)


def tn(a, b):
    return lax.dot_general(a, b, (((0,), (0,)), ((), ())), preferred_element_type=F32)


def shape(dims, dtype):
    return jax.ShapeDtypeStruct(dims, dtype)


def cut_rows(rows):
    first = (rows // 2 + 15) // 16 * 16
    return first, rows - first


class Plan:
    def __init__(self, number):
        self.number, self.ins, self.outs, self.copies = number, [], [], []

    def take(self, array):
        self.ins.append(array)
        return ("in", len(self.ins) - 1)

    def give(self, dims, dtype=BF):
        self.outs.append(shape(dims, dtype))
        return ("out", len(self.outs) - 1)

    def copy(self, start, until, src, src_row, dst, dst_row, size, dp=0, z=0, sends=None):
        self.copies.append((start, until, src, src_row, dst, dst_row, size, dp, z, sends))


class Bound:
    def __init__(self, plan, ins, outs, send_sem, recv_sem):
        self.plan, self.refs, self.sems = plan, {"in": ins, "out": outs}, (send_sem, recv_sem)
        self.d, self.z = lax.axis_index("dp"), lax.axis_index("tensor")

    def barrier(self, more=()):
        masks = sorted({(c[7], c[8]) for c in self.plan.copies if c[7] or c[8]} | set(more))
        if masks:
            sem = pltpu.get_barrier_semaphore()
            for dp, z in masks:
                pl.semaphore_signal(sem, inc=1, device_id=(self.d ^ dp, self.z ^ z), device_id_type=MESH)
            pl.semaphore_wait(sem, len(masks))

    def place(self, handle, row, size):
        ref = self.refs[handle[0]][handle[1]]
        row = pl.multiple_of(row(self.d), 16) if callable(row) else row
        return ref.at[pl.ds(row, size), :]

    def tick(self, t, last=False):
        todo = list(enumerate(self.plan.copies))
        for i, c in todo:
            if c[1] == t or (last and c[1] is None):
                self.one(i, c, False)
        for i, c in todo:
            if c[0] == t:
                self.one(i, c, True)

    def one(self, i, c, start):
        _, _, src, src_row, dst, dst_row, size, dp, z, sends = c
        s, r = self.sems
        a, b = self.place(src, src_row, size), self.place(dst, dst_row, size)
        if not dp and not z:
            copy = pltpu.make_async_copy(a, b, s.at[i])
            copy.start() if start else copy.wait()
            return
        copy = pltpu.make_async_remote_copy(src_ref=a, dst_ref=b, send_sem=s.at[i], recv_sem=r.at[i], device_id=(self.d ^ dp, self.z ^ z), device_id_type=MESH)
        if sends is None:
            copy.start() if start else copy.wait()
            return
        core = self.d % 2

        def any_of(z_here):
            hit = None
            for zz, cc in sends:
                this = z_here == zz
                if cc is not None:
                    this = this & (core == cc)
                hit = this if hit is None else hit | this
            return hit

        if start:
            pl.when(any_of(self.z))(copy.start)
        else:
            pl.when(any_of(self.z))(copy.wait_send)
            pl.when(any_of(self.z ^ z))(copy.wait_recv)


def plan_args(plan):
    n = max(len(plan.copies), 1)
    return [HB] * len(plan.ins), (HB,) * len(plan.outs), [pltpu.SemaphoreType.DMA((n,)), pltpu.SemaphoreType.DMA((n,))]


def params(plan, mib):
    if plan.copies:
        return pltpu.CompilerParams(vmem_limit_bytes=mib * 2**20, collective_id=plan.number, has_side_effects=True)
    return pltpu.CompilerParams(vmem_limit_bytes=mib * 2**20)


def block_rows(lhs, rhs, half, write):
    if half is None:
        @pl.loop(0, lhs.shape[0] // 384)
        def _(t):
            place = pl.ds(pl.multiple_of(t * 384, 128), 384)
            write(place, nn(lhs[place, :], rhs[...]))
    else:
        rows = lhs.shape[0] // 8
        d = lax.axis_index("dp")

        @pl.loop(0, 2)
        def _(t):
            r = 4 * t + 1 - half
            both = [lhs[pl.ds(pl.multiple_of((d ^ q) * rows, 16), rows), :] for q in (r, r + 2)]
            write(pl.ds(pl.multiple_of(t * 2 * rows, 16), 2 * rows), nn(jnp.concatenate(both, axis=0), rhs[...]))


def core_copy(src, dst, sems):
    d, z = lax.axis_index("dp"), lax.axis_index("tensor")
    return pltpu.make_async_remote_copy(src_ref=src, dst_ref=dst, send_sem=sems.at[0], recv_sem=sems.at[1], device_id=(d ^ 1, z), device_id_type=MESH)


def attn_fwd_kernel(length, heads, plan, first, qb, vb, acc_in, W_ref, *rest):
    ni, no = len(plan.ins), len(plan.outs)
    ins, (qkv, att, lse, tops, acc), rest = rest[:ni], rest[ni:ni + 5], rest[ni + 5:]
    outs, (W, sem, s_sem, r_sem) = rest[:no], rest[no:]
    net = Bound(plan, ins, outs, s_sem, r_sem)
    load = pltpu.make_async_copy(W_ref, W, sem)
    load.start()
    net.barrier()
    net.tick(0)
    load.wait()
    cw = heads * HD

    @pl.loop(0, TOK // RT)
    def _(i):
        rows = pl.ds(pl.multiple_of(i * RT, RT), RT)
        t = nn(first[rows, :], W[:, :3 * cw])
        q = (t[:, :cw] + qb[...]).astype(BF)
        k = t[:, cw:2 * cw].astype(BF)
        v = (t[:, 2 * cw:] + vb[...]).astype(BF)
        for h in range(heads):
            qkv[h, rows, :] = q[:, h * HD:(h + 1) * HD]
            qkv[heads + h, rows, :] = k[:, h * HD:(h + 1) * HD]
            qkv[2 * heads + h, rows, :] = v[:, h * HD:(h + 1) * HD]

    tops[...] = jnp.full(tops.shape, -1e30, F32)

    @pl.loop(0, TOK // RT)
    def _(i):
        for t in range(TOK // RT):
            pl.when(i == t)(functools.partial(net.tick, t + 1))
        rows = pl.ds(pl.multiple_of(i * RT, RT), RT)
        rid = lax.broadcasted_iota(jnp.int32, (RT, 1), 0) + i * RT
        cid = lax.broadcasted_iota(jnp.int32, (1, TOK), 1)
        res = []
        for h in range(heads):
            s = nt(qkv[h, rows, :], qkv[heads + h])
            s = jnp.where(cid < length, s, -1e30)
            m = jnp.max(s, axis=1, keepdims=True)
            e = jnp.exp2((s - m) * (SC * LOG2E))
            l = jnp.sum(e, axis=1, keepdims=True)
            o = nn(e.astype(BF), qkv[2 * heads + h]) * (1.0 / l)
            res.append(o.astype(BF))
            lse[h, rows, :] = m * (SC * LOG2E) + jnp.log2(l)
            tops[h:h + 1, :] = jnp.maximum(tops[h:h + 1, :], jnp.max(jnp.where(rid < length, m, -1e30)) * SC)
        a = jnp.concatenate(res, axis=1)
        att[rows, :] = a
        acc[rows, :] = acc_in[rows, :] + nt(a, W[:, 3 * cw:])

    net.tick(4)
    net.tick(5)
    net.tick(6, True)


def attn_fwd(plan, first, W, qb, vb, acc, length):
    D = first.shape[1]
    cw = W.shape[1] // 4
    heads = cw // HD
    in_p, out_p, sems = plan_args(plan)
    got = pl.pallas_call(
        functools.partial(attn_fwd_kernel, length, heads, plan),
        out_shape=(shape((3 * heads, TOK, HD), BF), shape((TOK, cw), BF), shape((heads, TOK, 1), F32), shape((heads, 128), F32), shape((TOK, D), F32), *plan.outs),
        in_specs=[VM] * 4 + [HB] + in_p,
        out_specs=(VM,) * 5 + out_p,
        scratch_shapes=[pltpu.VMEM((D, 4 * cw), BF), pltpu.SemaphoreType.DMA] + sems,
        compiler_params=params(plan, 44),
        cost_estimate=pl.CostEstimate(flops=2 * TOK * (D * cw * 4 + heads * 2 * TOK * HD * 6), bytes_accessed=25 * 2**20, transcendentals=heads * TOK * TOK),
        name="attn_fwd",
    )(first, qb, vb, acc, W, *plan.ins)
    return got[:5], got[5:]


def mlp_kernel(fw, split, plan, second, secondT, gout, goutT, eb, mlp_in, sec_in, W_ref, *rest):
    ni, no = len(plan.ins), len(plan.outs)
    ins, (G, geb, mlp, sec), rest = rest[:ni], rest[ni:ni + 4], rest[ni + 4:]
    outs, (W, E, ST, act_s, gpre_s, out_s, peer_s, sem, c_sem, s_sem, r_sem) = rest[:no], rest[no:]
    net = Bound(plan, ins, outs, s_sem, r_sem)
    load = pltpu.make_async_copy(W_ref, W, sem)
    load.start()
    if split:
        net.barrier([(1, 0)])
    net.tick(0)
    load.wait()
    cut = fw // 128 * 128
    tail = fw - cut
    E[:, :cut] = W[:, :cut]
    ST[:, :cut] = W[:, cut:2 * cut]
    last = W[:, 2 * cut:]
    blank = jnp.zeros((last.shape[0], 128 - tail), BF)
    E[:, cut:] = jnp.concatenate([last[:, :tail], blank], axis=1)
    ST[:, cut:] = jnp.concatenate([last[:, tail:], blank], axis=1)
    geb[...] = jnp.zeros_like(geb)

    @pl.loop(0, TOK // RT)
    def _(i):
        for t in range(1, TOK // RT):
            pl.when(i == t)(functools.partial(net.tick, t))
        rows = pl.ds(pl.multiple_of(i * RT, RT), RT)
        u = nn(second[rows, :], E[...]) + eb[...]
        ga = nn(gout[rows, :], ST[...])
        u2 = u * u
        t = jnp.tanh(u * (tanh_coef + (tanh_coef * cube_coef) * u2))
        hu = 0.5 * (1.0 + t)
        act_s[rows, :] = (u * hu).astype(BF)
        slope = hu + u * (0.5 * tanh_coef) * (1.0 - t * t) * (1.0 + (3.0 * cube_coef) * u2)
        gp = ga * slope
        geb[...] += jnp.sum(gp, axis=0, keepdims=True)
        gpre_s[rows, :] = gp.astype(BF)

    net.tick(3)

    def write_e(dst, peer):
        def write(place, v):
            a, b = v[:, :cut], v[:, cut:fw]
            if peer is not None:
                a = a + peer[place, :cut].astype(F32)
                b = b + peer[place, 2 * cut:2 * cut + tail].astype(F32)
            dst[place, :cut] = a.astype(BF)
            dst[place, 2 * cut:2 * cut + tail] = b.astype(BF)
        return write

    def write_s(dst, peer):
        def write(place, v):
            a, b = v[:, :cut], v[:, cut:fw]
            if peer is not None:
                a = a + peer[place, cut:2 * cut].astype(F32)
                b = b + peer[place, 2 * cut + tail:].astype(F32)
            dst[place, cut:2 * cut] = a.astype(BF)
            dst[place, 2 * cut + tail:] = b.astype(BF)
        return write

    if split:
        block_rows(secondT, gpre_s, 0, write_e(out_s, None))
        block_rows(goutT, act_s, 0, write_s(out_s, None))
        exchange = core_copy(out_s, peer_s, c_sem)
        exchange.start()

    @pl.loop(0, TOK // RT)
    def _(i):
        rows = pl.ds(pl.multiple_of(i * RT, RT), RT)
        mlp[rows, :] = mlp_in[rows, :] + nt(act_s[rows, :], ST[...])
        sec[rows, :] = sec_in[rows, :] + nt(gpre_s[rows, :], E[...])

    net.tick(4)
    if split:
        exchange.wait()
    peer = peer_s if split else None
    block_rows(secondT, gpre_s, 1 if split else None, write_e(G, peer))
    block_rows(goutT, act_s, 1 if split else None, write_s(G, peer))
    net.tick(5)
    net.tick(6, True)


def mlp_call(plan, second, secondT, gout, goutT, W, eb, mlp, sec, split):
    D = second.shape[1]
    fw = W.shape[1] // 2
    wide = fw // 128 * 128 + 128
    eb = jnp.pad(eb, ((0, 0), (0, wide - fw)))
    in_p, out_p, sems = plan_args(plan)
    side = pltpu.VMEM((D // 2, 2 * fw) if split else (16, 128), BF)
    got = pl.pallas_call(
        functools.partial(mlp_kernel, fw, split, plan),
        out_shape=(shape((D // (1 + split), 2 * fw), BF), shape((1, wide), F32), shape((TOK, D), F32), shape((TOK, D), F32), *plan.outs),
        in_specs=[VM] * 7 + [HB] + in_p,
        out_specs=(VM,) * 4 + out_p,
        scratch_shapes=[pltpu.VMEM((D, 2 * fw), BF)] + [pltpu.VMEM((D, wide), BF)] * 2 + [pltpu.VMEM((TOK, wide), BF)] * 2 + [side, side] + [pltpu.SemaphoreType.DMA, pltpu.SemaphoreType.DMA((2,))] + sems,
        compiler_params=params(plan, 56) if plan.copies or not split else pltpu.CompilerParams(vmem_limit_bytes=56 * 2**20, collective_id=plan.number, has_side_effects=True),
        cost_estimate=pl.CostEstimate(flops=2 * 9 * TOK * D * fw, bytes_accessed=35 * 2**20, transcendentals=TOK * fw),
        name="mlp",
    )(second, secondT, gout, goutT, eb, mlp, sec, W, *plan.ins)
    return got[:4], got[4:]


def attn_bwd_kernel(length, heads, split, plan, gmid, gmidT, firstT, qkv, att, lse, acc_in, W_ref, *rest):
    ni, no = len(plan.ins), len(plan.outs)
    ins, (G, gqb, gvb, acc), rest = rest[:ni], rest[ni:ni + 4], rest[ni + 4:]
    outs, (W, ga_s, d_s, dk_s, dv_s, out_s, peer_s, sem, c_sem, s_sem, r_sem) = rest[:no], rest[no:]
    net = Bound(plan, ins, outs, s_sem, r_sem)
    load = pltpu.make_async_copy(W_ref, W, sem)
    load.start()
    if split:
        net.barrier([(1, 0)])
    net.tick(0)
    load.wait()
    cw = heads * HD

    @pl.loop(0, TOK // RT)
    def _(i):
        rows = pl.ds(pl.multiple_of(i * RT, RT), RT)
        g = nn(gmid[rows, :], W[:, 3 * cw:]).astype(BF)
        for h in range(heads):
            ga_s[h, rows, :] = g[:, h * HD:(h + 1) * HD]

    gqb[...] = jnp.zeros_like(gqb)
    dk_s[...] = jnp.zeros_like(dk_s)
    dv_s[...] = jnp.zeros_like(dv_s)

    @pl.loop(0, TOK // RT)
    def _(i):
        rows = pl.ds(pl.multiple_of(i * RT, RT), RT)
        cid = lax.broadcasted_iota(jnp.int32, (1, TOK), 1)
        dqs = []
        for h in range(heads):
            q, k, v, g = qkv[h, rows, :], qkv[heads + h], qkv[2 * heads + h], ga_s[h, rows, :]
            s = nt(q, k)
            p = jnp.exp2(s * (SC * LOG2E) - lse[h, rows, :])
            p = jnp.where(cid < length, p, 0.0)
            dp = nt(g, v)
            dd = jnp.sum(g.astype(F32) * att[rows, h * HD:(h + 1) * HD].astype(F32), axis=1, keepdims=True)
            ds = (p * (dp - dd)).astype(BF)
            dqs.append(nn(ds, k) * SC)
            dk_s[h] += tn(ds, q)
            dv_s[h] += tn(p.astype(BF), g)
        dq = jnp.concatenate(dqs, axis=1)
        gqb[...] += jnp.sum(dq, axis=0, keepdims=True)
        d_s[rows, :cw] = dq.astype(BF)

    dk = jnp.concatenate([dk_s[h] * SC for h in range(heads)], axis=1)
    d_s[:, cw:2 * cw] = dk.astype(BF)
    dv = jnp.concatenate([dv_s[h] for h in range(heads)], axis=1)
    gvb[...] = jnp.sum(dv, axis=0, keepdims=True)
    d_s[:, 2 * cw:] = dv.astype(BF)

    def write(dst, peer, lo, hi):
        def put(place, v):
            if peer is not None:
                v = v + peer[place, lo:hi].astype(F32)
            dst[place, lo:hi] = v.astype(BF)
        return put

    if split:
        block_rows(firstT, d_s, 0, write(out_s, None, 0, 3 * cw))
        block_rows(gmidT, att, 0, write(out_s, None, 3 * cw, 4 * cw))
        exchange = core_copy(out_s, peer_s, c_sem)
        exchange.start()

    @pl.loop(0, TOK // RT)
    def _(i):
        rows = pl.ds(pl.multiple_of(i * RT, RT), RT)
        acc[rows, :] = acc_in[rows, :] + nt(d_s[rows, :], W[:, :3 * cw])

    if split:
        exchange.wait()
    peer = peer_s if split else None
    block_rows(firstT, d_s, 1 if split else None, write(G, peer, 0, 3 * cw))
    block_rows(gmidT, att, 1 if split else None, write(G, peer, 3 * cw, 4 * cw))
    net.tick(6, True)


def attn_bwd(plan, gmid, gmidT, firstT, W, qkv, att, lse, acc, length, split):
    D = gmid.shape[1]
    cw = W.shape[1] // 4
    heads = cw // HD
    in_p, out_p, sems = plan_args(plan)
    side = pltpu.VMEM((D // 2, 4 * cw) if split else (16, 128), BF)
    got = pl.pallas_call(
        functools.partial(attn_bwd_kernel, length, heads, split, plan),
        out_shape=(shape((D // (1 + split), 4 * cw), BF), shape((1, cw), F32), shape((1, cw), F32), shape((TOK, D), F32), *plan.outs),
        in_specs=[VM] * 7 + [HB] + in_p,
        out_specs=(VM,) * 4 + out_p,
        scratch_shapes=[pltpu.VMEM((D, 4 * cw), BF), pltpu.VMEM((heads, TOK, HD), BF), pltpu.VMEM((TOK, 3 * cw), BF), pltpu.VMEM((heads, TOK, HD), F32), pltpu.VMEM((heads, TOK, HD), F32), side, side, pltpu.SemaphoreType.DMA, pltpu.SemaphoreType.DMA((2,))] + sems,
        compiler_params=params(plan, 52) if plan.copies or not split else pltpu.CompilerParams(vmem_limit_bytes=52 * 2**20, collective_id=plan.number, has_side_effects=True),
        cost_estimate=pl.CostEstimate(flops=2 * TOK * (D * cw * 8 + heads * 5 * TOK * HD * 6), bytes_accessed=30 * 2**20, transcendentals=heads * TOK * TOK),
        name="attn_bwd",
    )(gmid, gmidT, firstT, qkv, att, lse, acc, W, *plan.ins)
    return got[:4], got[4:]


def normalize(values):
    centre = jnp.mean(values, axis=-1, keepdims=True)
    centred = values - centre
    spread = jnp.mean(centred * centred, axis=-1, keepdims=True)
    inverse = lax.rsqrt(spread + norm_eps)
    return centred * inverse, inverse


def norm_back(grad_norm, normed, inverse, gain):
    scaled = grad_norm * gain
    first_mean = jnp.mean(scaled, axis=-1, keepdims=True)
    second_mean = jnp.mean(scaled * normed, axis=-1, keepdims=True)
    grad_input = inverse * (scaled - first_mean - normed * second_mean)
    return grad_input, jnp.sum(grad_norm * normed, axis=0), jnp.sum(grad_norm, axis=0)


def slot_table(d, groups):
    z = lax.axis_index("tensor")
    middle = 1 + d % 2
    return jnp.where(z == 0, 0, jnp.where(z == groups - 1, 1, 2)), (z == 0) | (z == groups - 1) | (z == middle)


class General:
    split = 0

    def __init__(self, groups, attn_own, mlp_own):
        self.groups = groups
        self.attn, self.mlp = self.spread(attn_own), self.spread(mlp_own)

    def vectors(self, own):
        every = lax.all_gather(own, "tensor")
        return [every[i] for i in range(self.groups)]

    def spread(self, own):
        d, count = lax.axis_index("dp"), lax.axis_size("dp")
        rows = own.shape[0] // count
        piece = lax.dynamic_slice_in_dim(own, d * rows, rows, 0)
        piece = lax.all_gather(piece, "tensor")
        whole = lax.all_gather(piece, "dp", axis=1, tiled=True)
        return [whole[i] for i in range(self.groups)]

    def plan(self, name):
        return Plan(0)

    def done(self, name, got):
        pass

    def reduce(self, parts):
        part = lax.psum_scatter(jnp.stack(parts), "dp", scatter_dimension=1, tiled=True)
        return lax.psum_scatter(part, "tensor", scatter_dimension=0, tiled=True)[0].astype(F32)

    def collect(self, grad_attn, grad_mlp):
        return self.reduce(grad_attn), self.reduce(grad_mlp)

    def by_index(self, items):
        return jnp.stack(items)

    def give(self, mine):
        self.mine = mine

    def gathered(self):
        return self.share(self.mine)

    def share(self, mine):
        every = lax.all_gather(mine, "tensor")
        middle = 1 + lax.axis_index("dp") % 2
        return jnp.stack([every[0], every[self.groups - 1], lax.dynamic_index_in_dim(every, middle, 0, keepdims=False)])


BOTH_UP = ((0, None),)
HOPS = {
    "u1": (1, ((0, None),)), "u2": (3, ((1, None),)), "u3": (1, ((2, None),)),
    "w1": (1, ((3, None),)), "w2": (3, ((2, None),)), "w3": (1, ((1, None),)),
    "v1": (3, ((1, 0), (2, 1))), "v2": (1, ((2, 0), (1, 1))), "v3": (1, ((1, 0), (2, 1))),
}
HOP_FROM = {"u1": "me", "u2": "u1", "u3": "u2", "w1": "me", "w2": "w1", "w3": "w2", "v1": "me", "v2": "v1", "v3": "me"}


class Line:
    split = 1
    groups = 4
    work = {
        "A0": ("z a1", "z a2", "g a1"),
        "A1": ("g a2", "z a3", "z m1", "zl m2"),
        "A2": ("g a3", "zh m2"),
        "A3": ("g m1", "z m3"),
        "M0": ("g m2",),
        "M1": ("g m3", "r1 m0"),
        "M2": ("r2 m0", "r1 m1"),
        "M3": ("r3 m0", "r2 m1", "r1 m2"),
        "B3": ("r3 m1", "r2 m2", "r1 m3", "h u1 0", "h w1 0", "h v1 0", "h v3 0", "h v1 1", "h v3 1"),
        "B2": ("r3 m2", "r2 m3", "r1 b3", "h u2 0", "h w2 0", "h u1 1", "h w1 1", "h v2 0", "h v2 1"),
        "B1": ("r3 m3", "r2 b3", "r1 b2", "h u3 0", "h w3 0", "h u2 1", "h w2 1"),
        "B0": ("r3 b3", "r2 b2", "r1 b1", "h u3 1", "h w3 1"),
    }

    def __init__(self, groups, attn_own, mlp_own):
        d = lax.axis_index("dp")
        self.rows = attn_own.shape[0] // 8
        self.one, self.two = cut_rows(self.rows)
        self.attn, self.mlp = [attn_own, None, None, None], [mlp_own, None, None, None]
        self.piece = {}
        for name, own in (("a", attn_own), ("m", mlp_own)):
            self.piece[name + "0"] = lax.dynamic_slice_in_dim(own, d * self.rows, self.rows, 0)
        self.state, self.hops = {}, {}

    def vectors(self, own):
        return [own] + [lax.ppermute(own, "tensor", [(i, i ^ k) for i in range(4)]) for k in (1, 2, 3)]

    def plan(self, name):
        plan = Plan(list(self.work).index(name))
        self.made = made = []
        rows, one, two = self.rows, self.one, self.two
        fresh = {}
        for job in self.work[name]:
            kind, what, *more = job.split()
            if kind == "z":
                k = int(what[1])
                src = self.piece[what[0] + ("2" if k == 3 else "0")]
                out = plan.give(src.shape)
                plan.copy(0, 2 if "g " + what in self.work[name] else None, plan.take(src), 0, out, 0, rows, z=1 if k == 3 else k)
                fresh[what] = out
                made.append((self.piece, what))
            elif kind in ("zl", "zh"):
                src = self.piece[what[0] + "0"]
                lo, size = (0, two) if kind == "zl" else (two, one)
                out = plan.give((size, src.shape[1]))
                plan.copy(0, None, plan.take(src), lo, out, 0, size, z=2)
                made.append((self.piece, what + kind))
            elif kind == "g":
                t = (2, 3, 4) if what in fresh else (0, 2, 4) if name[0] == "M" else (0, 2, 3)
                src = fresh[what] if what in fresh else plan.take(self.piece[what])
                out = plan.give((rows * 8, self.piece[what[0] + "0"].shape[1]))
                at = lambda mask, off=0: lambda d: (d ^ mask) * rows + off
                plan.copy(t[0], None, src, 0, out, at(0), rows)
                for mask in (2, 4, 1):
                    plan.copy(t[0], t[1], src, 0, out, at(0), rows, dp=mask)
                plan.copy(t[1], t[2], out, at(2), out, at(2), one, dp=4)
                plan.copy(t[1], t[2], out, at(4, one), out, at(4, one), two, dp=2)
                for mask in (2, 4):
                    plan.copy(t[1], None, out, at(mask), out, at(mask), rows, dp=1)
                plan.copy(t[2], None, out, at(6), out, at(6), rows, dp=1)
                made.append((self.attn if what[0] == "a" else self.mlp, int(what[1])))
            elif kind == "r1":
                s = self.state[what]
                columns = s["h"].shape[1]
                h, ax, by = plan.take(s["h"]), plan.give((2 * one, columns)), plan.give((2 * two, columns))
                plan.copy(0, None, h, rows, ax, 0, one, dp=2)
                plan.copy(0, None, h, 3 * rows, ax, one, one, dp=2)
                plan.copy(0, None, h, 2 * rows + one, by, 0, two, dp=4)
                plan.copy(0, None, h, 3 * rows + one, by, two, two, dp=4)
                made += [(s, "ax"), (s, "by")]
            elif kind == "r2":
                s = self.state[what]
                src = self.second(s)
                t, ay, bx = plan.take(src), plan.give((one, src.shape[1])), plan.give((two, src.shape[1]))
                plan.copy(0, None, t, 0, ay, 0, one, dp=4)
                plan.copy(0, None, t, one, bx, 0, two, dp=2)
                made += [(s, "ay"), (s, "bx")]
            elif kind == "r3":
                s, k = self.state[what], int(what[1])
                s["whole"] = self.third(s)
                if k:
                    src = s["whole"].astype(BF)
                    plan.copy(0, None, plan.take(src), 0, plan.give(src.shape), 0, rows, z=k)
                    made.append((s, "z"))
            elif kind == "h":
                half = int(more[0])
                mask, sends = HOPS[what]
                begin = HOP_FROM[what]
                src = self.mine if begin == "me" else self.hops[begin, half]
                size = self.mine.shape[0] // 2
                plan.copy(0, None, plan.take(src), half * size if begin == "me" else 0, plan.give((size, src.shape[1])), 0, size, z=mask, sends=sends)
                made.append((self.hops, (what, half)))
        return plan

    def done(self, name, got):
        for (store, key), value in zip(self.made, got, strict=True):
            store[key] = value
        if name == "A2":
            self.piece["m2"] = jnp.concatenate([self.piece.pop("m2zl"), self.piece.pop("m2zh")])

    def summed(self, name, h):
        self.state[name] = {"h": h}

    def h(self, s, q, lo, hi):
        return s["h"][q * self.rows + lo:q * self.rows + hi].astype(F32)

    def second(self, s):
        one, two = self.one, self.two
        return jnp.concatenate([self.h(s, 2, 0, one) + s["ax"][one:].astype(F32), self.h(s, 1, one, self.rows) + s["by"][two:].astype(F32)]).astype(BF)

    def third(self, s):
        one, two = self.one, self.two
        a = self.h(s, 0, 0, one) + s["ax"][:one].astype(F32) + s["ay"].astype(F32)
        b = self.h(s, 0, one, self.rows) + s["by"][:two].astype(F32) + s["bx"].astype(F32)
        return jnp.concatenate([a, b])

    def dp(self, a, m):
        return lax.ppermute(a, "dp", [(i, i ^ m) for i in range(8)])

    def collect(self, grad_attn, grad_mlp):
        rows, one, two = self.rows, self.one, self.two
        out = []
        for name in ("b", "m"):
            total = None
            for k in range(4):
                s = self.state[name + str(k)]
                if "ax" not in s:
                    s["ax"] = self.dp(jnp.concatenate([s["h"][rows:rows + one], s["h"][3 * rows:3 * rows + one]]), 2)
                    s["by"] = self.dp(jnp.concatenate([s["h"][2 * rows + one:3 * rows], s["h"][3 * rows + one:]]), 4)
                if "ay" not in s:
                    t = self.second(s)
                    s["ay"], s["bx"] = self.dp(t[:one], 4), self.dp(t[one:], 2)
                if "whole" not in s:
                    s["whole"] = self.third(s)
                if k and "z" not in s:
                    s["z"] = lax.ppermute(s["whole"].astype(BF), "tensor", [(i, i ^ k) for i in range(4)])
                part = s["z"].astype(F32) if k else s["whole"]
                total = part if total is None else total + part
            out.append(total)
        return out

    def by_index(self, items):
        return jnp.take(jnp.stack(items), lax.axis_index("tensor") ^ jnp.arange(4), axis=0)

    def give(self, mine):
        self.mine = jnp.pad(mine, ((0, -mine.shape[0] % 32), (0, 0)))

    def select(self, a, g):
        z, c = lax.axis_index("tensor"), lax.axis_index("dp") % 2
        near = jnp.where(c == 0, z, 3 - z)

        def pick(who, options):
            out = options[3]
            for i in (2, 1, 0):
                out = jnp.where(who == i, options[i], out)
            return out

        return jnp.stack([pick(z, [a, g["u1"], g["u2"], g["u3"]]), pick(z, [g["w3"], g["w2"], g["w1"], a]), pick(near, [g["v3"], a, g["v1"], g["v2"]])])

    def gathered(self):
        size = self.mine.shape[0] // 2
        return jnp.concatenate([self.select(self.mine[h * size:(h + 1) * size], {n: self.hops[n, h] for n in HOPS}) for h in (0, 1)], axis=1)

    def share(self, mine):
        rows = -(-mine.shape[0] // 3 // 16) * 16
        result = []
        for start in range(0, mine.shape[0], rows):
            have = {"me": mine[start:start + rows]}
            for name in ("u1", "w1", "v1", "v3", "u2", "w2", "v2", "u3", "w3"):
                mask, sends = HOPS[name]
                pairs = [(i * 4 + s, i * 4 + (s ^ mask)) for i in range(8) for s, c in sends if c is None or c == i % 2]
                have[name] = lax.ppermute(have[HOP_FROM[name]], ("dp", "tensor"), pairs)
            result.append(self.select(have["me"], have))
        return jnp.concatenate(result, axis=1)


def shards(images, counts, cotangent, query_w, query_b, key_w, value_w, value_b, out_w, out_b, norm1_gain, norm1_shift,
           norm2_gain, norm2_shift, expand_w, expand_b, shrink_w, shrink_b):
    slots, length, width = images.shape
    groups = lax.axis_size("tensor")
    d, z = lax.axis_index("dp"), lax.axis_index("tensor")
    cw, fw = query_w.shape[1], expand_w.shape[1]
    cut = fw // 128 * 128
    slot, used = slot_table(d, groups)
    live = jnp.where(used & (slot < counts[0]), 1.0, 0.0).astype(F32)
    pad = lambda a: jnp.pad(a, ((0, TOK - length), (0, 0)))

    attn_own = jnp.concatenate([query_w, key_w, value_w, out_w.T], axis=1)
    shrink_t = shrink_w.T
    mlp_own = jnp.concatenate([expand_w[:, :cut], shrink_t[:, :cut], expand_w[:, cut:], shrink_t[:, cut:]], axis=1)
    net = (Line if (groups, lax.axis_size("dp")) == (4, 8) else General)(groups, attn_own, mlp_own)
    split = net.split
    biases = net.vectors(jnp.concatenate([query_b, value_b, expand_b]))

    x = pad(lax.dynamic_index_in_dim(images, slot, 0, keepdims=False)).astype(F32)
    gout = pad(lax.dynamic_index_in_dim(cotangent, slot, 0, keepdims=False)) * live.astype(BF)
    gout_t = gout.T
    normed1, inverse1 = normalize(x)
    first = (normed1 * norm1_gain + norm1_shift).astype(BF)
    first_t = first.T
    acc = x + out_b
    kept, tops = [], []
    for k in range(groups):
        b = biases[k]
        plan = net.plan(f"A{k}")
        (qkv, att, lse, top, acc), got = attn_fwd(plan, first, net.attn[k], b[None, :cw], b[None, cw:2 * cw], acc, length)
        net.done(f"A{k}", got)
        kept.append((qkv, att, lse))
        tops.append(top[:, 0])
    midway = acc
    normed2, inverse2 = normalize(midway)
    second = (normed2 * norm2_gain + norm2_shift).astype(BF)
    second_t = second.T
    mlp = midway + shrink_b
    sec = jnp.zeros((TOK, width), F32)
    grad_mlp, geb = [], []
    for k in range(groups):
        plan = net.plan(f"M{k}")
        (grad, g_b, mlp, sec), got = mlp_call(plan, second, second_t, gout, gout_t, net.mlp[k], biases[k][None, 2 * cw:], mlp, sec, split)
        net.done(f"M{k}", got)
        if split:
            net.summed(f"m{k}", grad)
        grad_mlp.append(grad)
        geb.append(g_b[0, :fw])
    net.give((mlp[:length] * live).astype(BF))
    back2, gn2g, gn2s = norm_back(sec, normed2, inverse2, norm2_gain)
    gout32 = gout.astype(F32)
    gmid = gout32 + back2
    gmid_low = gmid.astype(BF)
    gmid_t = gmid_low.T
    acc = jnp.zeros((TOK, width), F32)
    grad_attn, gqb, gvb = [None] * groups, [None] * groups, [None] * groups
    for k in reversed(range(groups)):
        plan = net.plan(f"B{k}")
        (grad, g_q, g_v, acc), got = attn_bwd(plan, gmid_low, gmid_t, first_t, net.attn[k], *kept[k], acc, length, split)
        net.done(f"B{k}", got)
        if split:
            net.summed(f"b{k}", grad)
        grad_attn[k], gqb[k], gvb[k] = grad, g_q[0], g_v[0]
    back1, gn1g, gn1s = norm_back(acc, normed1, inverse1, norm1_gain)
    input_grad = ((gmid + back1) * live)[:length].astype(BF)

    outputs = net.gathered()[:, :length]
    input_grads = net.share(input_grad).astype(F32)
    sum_attn, sum_mlp = net.collect(grad_attn, grad_mlp)
    flat = lambda items: net.by_index(items).reshape(-1)
    vector = jnp.concatenate([flat(gqb), flat(gvb), flat(geb), jnp.sum(gmid, axis=0), jnp.sum(gout32, axis=0), gn1g, gn1s, gn2g, gn2s])
    vector = lax.psum(vector, ("dp", "tensor"))
    part = lambda start, size: lax.dynamic_slice_in_dim(vector, start, size, 0)
    whole, hidden = cw * groups, fw * groups
    tail = [vector[2 * whole + hidden + i * width:][:width] for i in range(6)]
    logit_top = lax.pmax(jnp.where(live > 0.0, net.by_index(tops), -1e30), ("dp", "tensor"))
    logit_top = lax.dynamic_index_in_dim(logit_top, z, 0, keepdims=False)
    factor = jnp.sqrt(clip_limit / jnp.maximum(logit_top, clip_limit))
    column_factor = jnp.repeat(factor, HD)
    clipped_query = (query_w.astype(F32) * column_factor).astype(BF)
    clipped_key = (key_w.astype(F32) * column_factor).astype(BF)
    unpack = lambda a, i: jnp.concatenate([a[:, i * cut:(i + 1) * cut], a[:, 2 * cut + i * (fw - cut):][:, :fw - cut]], axis=1)
    return (outputs, input_grads, sum_attn[:, :cw], part(z * cw, cw), sum_attn[:, cw:2 * cw], sum_attn[:, 2 * cw:3 * cw], part(whole + z * cw, cw),
            sum_attn[:, 3 * cw:].T, tail[0], tail[2], tail[3], tail[4], tail[5], unpack(sum_mlp, 0), part(2 * whole + z * fw, fw), unpack(sum_mlp, 1).T,
            tail[1], clipped_query, clipped_key)


def solution(mesh):
    columns, rows, vector = P(None, "tensor"), P("tensor", None), P("tensor")
    whole = P("dp", None, None)
    return jax.shard_map(
        shards, mesh=mesh,
        in_specs=(whole, P("dp"), whole, columns, vector, columns, columns, vector, rows, P(), P(), P(), P(), P(), columns, vector, rows, P()),
        out_specs=(whole, whole, P("dp", "tensor"), vector, P("dp", "tensor"), P("dp", "tensor"), vector, P("tensor", "dp"), P(), P(), P(), P(), P(),
                   P("dp", "tensor"), vector, P("tensor", "dp"), P(), columns, columns),
        check_vma=False)
```

```python
import functools
import math

import jax
import jax.numpy as jnp
from jax import lax
from jax.experimental import pallas as pl
from jax.experimental.pallas import tpu as pltpu
from jax.sharding import PartitionSpec as P

HD = 72
TOK = 768
RT = 256
SC = 1 / math.sqrt(HD)
LOG2E = 1.4426950408889634
F32 = jnp.float32
BF = jnp.bfloat16
norm_eps = 1e-06
clip_limit = 3.0
tanh_coef = 0.7978845608028654
cube_coef = 0.044715
VM = pl.BlockSpec(memory_space=pltpu.VMEM)
HB = pl.BlockSpec(memory_space=pl.ANY)
MESH = pl.DeviceIdType.MESH


def nn(a, b):
    return jnp.dot(a, b, preferred_element_type=F32)


def nt(a, b):
    return lax.dot_general(a, b, (((1,), (1,)), ((), ())), preferred_element_type=F32)


def tn(a, b):
    return lax.dot_general(a, b, (((0,), (0,)), ((), ())), preferred_element_type=F32)


def shape(dims, dtype):
    return jax.ShapeDtypeStruct(dims, dtype)


def cut_rows(rows):
    first = (rows // 2 + 15) // 16 * 16
    return first, rows - first


class Plan:
    def __init__(self, number):
        self.number, self.ins, self.outs, self.copies = number, [], [], []

    def take(self, array):
        self.ins.append(array)
        return ("in", len(self.ins) - 1)

    def give(self, dims, dtype=BF):
        self.outs.append(shape(dims, dtype))
        return ("out", len(self.outs) - 1)

    def copy(self, start, until, src, src_row, dst, dst_row, size, dp=0, z=0, sends=None):
        self.copies.append((start, until, src, src_row, dst, dst_row, size, dp, z, sends))


class Bound:
    def __init__(self, plan, ins, outs, send_sem, recv_sem):
        self.plan, self.refs, self.sems = plan, {"in": ins, "out": outs}, (send_sem, recv_sem)
        self.d, self.z = lax.axis_index("dp"), lax.axis_index("tensor")

    def barrier(self, more=()):
        masks = sorted({(c[7], c[8]) for c in self.plan.copies if c[7] or c[8]} | set(more))
        if masks:
            sem = pltpu.get_barrier_semaphore()
            for dp, z in masks:
                pl.semaphore_signal(sem, inc=1, device_id=(self.d ^ dp, self.z ^ z), device_id_type=MESH)
            pl.semaphore_wait(sem, len(masks))

    def place(self, handle, row, size):
        ref = self.refs[handle[0]][handle[1]]
        row = pl.multiple_of(row(self.d), 16) if callable(row) else row
        return ref.at[pl.ds(row, size), :]

    def tick(self, t, last=False):
        todo = list(enumerate(self.plan.copies))
        for i, c in todo:
            if c[1] == t or (last and c[1] is None):
                self.one(i, c, False)
        for i, c in todo:
            if c[0] == t:
                self.one(i, c, True)

    def one(self, i, c, start):
        _, _, src, src_row, dst, dst_row, size, dp, z, sends = c
        s, r = self.sems
        a, b = self.place(src, src_row, size), self.place(dst, dst_row, size)
        if not dp and not z:
            copy = pltpu.make_async_copy(a, b, s.at[i])
            copy.start() if start else copy.wait()
            return
        copy = pltpu.make_async_remote_copy(src_ref=a, dst_ref=b, send_sem=s.at[i], recv_sem=r.at[i], device_id=(self.d ^ dp, self.z ^ z), device_id_type=MESH)
        if sends is None:
            copy.start() if start else copy.wait()
            return
        core = self.d % 2

        def any_of(z_here):
            hit = None
            for zz, cc in sends:
                this = z_here == zz
                if cc is not None:
                    this = this & (core == cc)
                hit = this if hit is None else hit | this
            return hit

        if start:
            pl.when(any_of(self.z))(copy.start)
        else:
            pl.when(any_of(self.z))(copy.wait_send)
            pl.when(any_of(self.z ^ z))(copy.wait_recv)


def plan_args(plan):
    n = max(len(plan.copies), 1)
    return [HB] * len(plan.ins), (HB,) * len(plan.outs), [pltpu.SemaphoreType.DMA((n,)), pltpu.SemaphoreType.DMA((n,))]


def params(plan, mib):
    if plan.copies:
        return pltpu.CompilerParams(vmem_limit_bytes=mib * 2**20, collective_id=plan.number, has_side_effects=True)
    return pltpu.CompilerParams(vmem_limit_bytes=mib * 2**20)


def block_rows(lhs, rhs, half, write):
    if half is None:
        @pl.loop(0, lhs.shape[0] // 384)
        def _(t):
            place = pl.ds(pl.multiple_of(t * 384, 128), 384)
            write(place, nn(lhs[place, :], rhs[...]))
    else:
        rows = lhs.shape[0] // 8
        d = lax.axis_index("dp")

        @pl.loop(0, 2)
        def _(t):
            r = 4 * t + 1 - half
            both = [lhs[pl.ds(pl.multiple_of((d ^ q) * rows, 16), rows), :] for q in (r, r + 2)]
            write(pl.ds(pl.multiple_of(t * 2 * rows, 16), 2 * rows), nn(jnp.concatenate(both, axis=0), rhs[...]))


def core_copy(src, dst, sems):
    d, z = lax.axis_index("dp"), lax.axis_index("tensor")
    return pltpu.make_async_remote_copy(src_ref=src, dst_ref=dst, send_sem=sems.at[0], recv_sem=sems.at[1], device_id=(d ^ 1, z), device_id_type=MESH)


def attn_fwd_kernel(length, heads, plan, first, qb, vb, acc_in, W_ref, *rest):
    ni, no = len(plan.ins), len(plan.outs)
    ins, (qkv, att, lse, tops, acc), rest = rest[:ni], rest[ni:ni + 5], rest[ni + 5:]
    outs, (W, sem, s_sem, r_sem) = rest[:no], rest[no:]
    net = Bound(plan, ins, outs, s_sem, r_sem)
    load = pltpu.make_async_copy(W_ref, W, sem)
    load.start()
    net.barrier()
    net.tick(0)
    load.wait()
    cw = heads * HD

    @pl.loop(0, TOK // RT)
    def _(i):
        rows = pl.ds(pl.multiple_of(i * RT, RT), RT)
        t = nn(first[rows, :], W[:, :3 * cw])
        q = (t[:, :cw] + qb[...]).astype(BF)
        k = t[:, cw:2 * cw].astype(BF)
        v = (t[:, 2 * cw:] + vb[...]).astype(BF)
        for h in range(heads):
            qkv[h, rows, :] = q[:, h * HD:(h + 1) * HD]
            qkv[heads + h, rows, :] = k[:, h * HD:(h + 1) * HD]
            qkv[2 * heads + h, rows, :] = v[:, h * HD:(h + 1) * HD]

    tops[...] = jnp.full(tops.shape, -1e30, F32)

    @pl.loop(0, TOK // RT)
    def _(i):
        for t in range(TOK // RT):
            pl.when(i == t)(functools.partial(net.tick, t + 1))
        rows = pl.ds(pl.multiple_of(i * RT, RT), RT)
        rid = lax.broadcasted_iota(jnp.int32, (RT, 1), 0) + i * RT
        cid = lax.broadcasted_iota(jnp.int32, (1, TOK), 1)
        res = []
        for h in range(heads):
            s = nt(qkv[h, rows, :], qkv[heads + h])
            s = jnp.where(cid < length, s, -1e30)
            m = jnp.max(s, axis=1, keepdims=True)
            e = jnp.exp2((s - m) * (SC * LOG2E))
            l = jnp.sum(e, axis=1, keepdims=True)
            o = nn(e.astype(BF), qkv[2 * heads + h]) * (1.0 / l)
            res.append(o.astype(BF))
            lse[rows, h:h + 1] = m * (SC * LOG2E) + jnp.log2(l)
            tops[h:h + 1, :] = jnp.maximum(tops[h:h + 1, :], jnp.max(jnp.where(rid < length, m, -1e30)) * SC)
        a = jnp.concatenate(res, axis=1)
        att[rows, :] = a
        acc[rows, :] = acc_in[rows, :] + nt(a, W[:, 3 * cw:])

    net.tick(4)
    net.tick(5)
    net.tick(6, True)


def attn_fwd(plan, first, W, qb, vb, acc, length):
    D = first.shape[1]
    cw = W.shape[1] // 4
    heads = cw // HD
    in_p, out_p, sems = plan_args(plan)
    got = pl.pallas_call(
        functools.partial(attn_fwd_kernel, length, heads, plan),
        out_shape=(shape((3 * heads, TOK, HD), BF), shape((TOK, cw), BF), shape((TOK, 128), F32), shape((heads, 128), F32), shape((TOK, D), F32), *plan.outs),
        in_specs=[VM] * 4 + [HB] + in_p,
        out_specs=(VM,) * 5 + out_p,
        scratch_shapes=[pltpu.VMEM((D, 4 * cw), BF), pltpu.SemaphoreType.DMA] + sems,
        compiler_params=params(plan, 44),
        cost_estimate=pl.CostEstimate(flops=2 * TOK * (D * cw * 4 + heads * 2 * TOK * HD * 6), bytes_accessed=25 * 2**20, transcendentals=heads * TOK * TOK),
        name="attn_fwd",
    )(first, qb, vb, acc, W, *plan.ins)
    return got[:5], got[5:]


def mlp_kernel(fw, split, plan, second, secondT, gout, goutT, eb, mlp_in, sec_in, W_ref, *rest):
    ni, no = len(plan.ins), len(plan.outs)
    ins, (G, geb, mlp, sec), rest = rest[:ni], rest[ni:ni + 4], rest[ni + 4:]
    outs, (W, E, ST, act_s, gpre_s, out_s, peer_s, sem, c_sem, s_sem, r_sem) = rest[:no], rest[no:]
    net = Bound(plan, ins, outs, s_sem, r_sem)
    load = pltpu.make_async_copy(W_ref, W, sem)
    load.start()
    if split:
        net.barrier([(1, 0)])
    net.tick(0)
    load.wait()
    cut = fw // 128 * 128
    tail = fw - cut
    E[:, :cut] = W[:, :cut]
    ST[:, :cut] = W[:, cut:2 * cut]
    last = W[:, 2 * cut:]
    blank = jnp.zeros((last.shape[0], 128 - tail), BF)
    E[:, cut:] = jnp.concatenate([last[:, :tail], blank], axis=1)
    ST[:, cut:] = jnp.concatenate([last[:, tail:], blank], axis=1)
    geb[...] = jnp.zeros_like(geb)

    @pl.loop(0, TOK // RT)
    def _(i):
        for t in range(1, TOK // RT):
            pl.when(i == t)(functools.partial(net.tick, t))
        rows = pl.ds(pl.multiple_of(i * RT, RT), RT)
        u = nn(second[rows, :], E[...]) + eb[...]
        ga = nn(gout[rows, :], ST[...])
        u2 = u * u
        t = jnp.tanh(u * (tanh_coef + (tanh_coef * cube_coef) * u2))
        hu = 0.5 * (1.0 + t)
        act_s[rows, :] = (u * hu).astype(BF)
        slope = hu + u * (0.5 * tanh_coef) * (1.0 - t * t) * (1.0 + (3.0 * cube_coef) * u2)
        gp = ga * slope
        geb[...] += jnp.sum(gp, axis=0, keepdims=True)
        gpre_s[rows, :] = gp.astype(BF)

    net.tick(3)

    def write_e(dst, peer):
        def write(place, v):
            a, b = v[:, :cut], v[:, cut:fw]
            if peer is not None:
                a = a + peer[place, :cut].astype(F32)
                b = b + peer[place, 2 * cut:2 * cut + tail].astype(F32)
            dst[place, :cut] = a.astype(BF)
            dst[place, 2 * cut:2 * cut + tail] = b.astype(BF)
        return write

    def write_s(dst, peer):
        def write(place, v):
            a, b = v[:, :cut], v[:, cut:fw]
            if peer is not None:
                a = a + peer[place, cut:2 * cut].astype(F32)
                b = b + peer[place, 2 * cut + tail:].astype(F32)
            dst[place, cut:2 * cut] = a.astype(BF)
            dst[place, 2 * cut + tail:] = b.astype(BF)
        return write

    if split:
        block_rows(secondT, gpre_s, 0, write_e(out_s, None))
        block_rows(goutT, act_s, 0, write_s(out_s, None))
        exchange = core_copy(out_s, peer_s, c_sem)
        exchange.start()

    @pl.loop(0, TOK // RT)
    def _(i):
        rows = pl.ds(pl.multiple_of(i * RT, RT), RT)
        mlp[rows, :] = mlp_in[rows, :] + nt(act_s[rows, :], ST[...])
        sec[rows, :] = sec_in[rows, :] + nt(gpre_s[rows, :], E[...])

    net.tick(4)
    if split:
        exchange.wait()
    peer = peer_s if split else None
    block_rows(secondT, gpre_s, 1 if split else None, write_e(G, peer))
    block_rows(goutT, act_s, 1 if split else None, write_s(G, peer))
    net.tick(5)
    net.tick(6, True)


def mlp_call(plan, second, secondT, gout, goutT, W, eb, mlp, sec, split):
    D = second.shape[1]
    fw = W.shape[1] // 2
    wide = fw // 128 * 128 + 128
    eb = jnp.pad(eb, ((0, 0), (0, wide - fw)))
    in_p, out_p, sems = plan_args(plan)
    side = pltpu.VMEM((D // 2, 2 * fw) if split else (16, 128), BF)
    got = pl.pallas_call(
        functools.partial(mlp_kernel, fw, split, plan),
        out_shape=(shape((D // (1 + split), 2 * fw), BF), shape((1, wide), F32), shape((TOK, D), F32), shape((TOK, D), F32), *plan.outs),
        in_specs=[VM] * 7 + [HB] + in_p,
        out_specs=(VM,) * 4 + out_p,
        scratch_shapes=[pltpu.VMEM((D, 2 * fw), BF)] + [pltpu.VMEM((D, wide), BF)] * 2 + [pltpu.VMEM((TOK, wide), BF)] * 2 + [side, side] + [pltpu.SemaphoreType.DMA, pltpu.SemaphoreType.DMA((2,))] + sems,
        compiler_params=params(plan, 56) if plan.copies or not split else pltpu.CompilerParams(vmem_limit_bytes=56 * 2**20, collective_id=plan.number, has_side_effects=True),
        cost_estimate=pl.CostEstimate(flops=2 * 9 * TOK * D * fw, bytes_accessed=35 * 2**20, transcendentals=TOK * fw),
        name="mlp",
    )(second, secondT, gout, goutT, eb, mlp, sec, W, *plan.ins)
    return got[:4], got[4:]


def attn_bwd_kernel(length, heads, split, plan, gmid, gmidT, firstT, qkv, att, lse, acc_in, W_ref, *rest):
    ni, no = len(plan.ins), len(plan.outs)
    ins, (G, gqb, gvb, acc), rest = rest[:ni], rest[ni:ni + 4], rest[ni + 4:]
    outs, (W, ga_s, d_s, dk_s, dv_s, out_s, peer_s, sem, c_sem, s_sem, r_sem) = rest[:no], rest[no:]
    net = Bound(plan, ins, outs, s_sem, r_sem)
    load = pltpu.make_async_copy(W_ref, W, sem)
    load.start()
    if split:
        net.barrier([(1, 0)])
    net.tick(0)
    load.wait()
    cw = heads * HD

    @pl.loop(0, TOK // RT)
    def _(i):
        rows = pl.ds(pl.multiple_of(i * RT, RT), RT)
        g = nn(gmid[rows, :], W[:, 3 * cw:]).astype(BF)
        for h in range(heads):
            ga_s[h, rows, :] = g[:, h * HD:(h + 1) * HD]

    gqb[...] = jnp.zeros_like(gqb)
    dk_s[...] = jnp.zeros_like(dk_s)
    dv_s[...] = jnp.zeros_like(dv_s)

    @pl.loop(0, TOK // RT)
    def _(i):
        rows = pl.ds(pl.multiple_of(i * RT, RT), RT)
        cid = lax.broadcasted_iota(jnp.int32, (1, TOK), 1)
        dqs = []
        for h in range(heads):
            q, k, v, g = qkv[h, rows, :], qkv[heads + h], qkv[2 * heads + h], ga_s[h, rows, :]
            s = nt(q, k)
            p = jnp.exp2(s * (SC * LOG2E) - lse[rows, h:h + 1])
            p = jnp.where(cid < length, p, 0.0)
            dp = nt(g, v)
            dd = jnp.sum(g.astype(F32) * att[rows, h * HD:(h + 1) * HD].astype(F32), axis=1, keepdims=True)
            ds = (p * (dp - dd)).astype(BF)
            dqs.append(nn(ds, k) * SC)
            dk_s[h] += tn(ds, q)
            dv_s[h] += tn(p.astype(BF), g)
        dq = jnp.concatenate(dqs, axis=1)
        gqb[...] += jnp.sum(dq, axis=0, keepdims=True)
        d_s[rows, :cw] = dq.astype(BF)

    dk = jnp.concatenate([dk_s[h] * SC for h in range(heads)], axis=1)
    d_s[:, cw:2 * cw] = dk.astype(BF)
    dv = jnp.concatenate([dv_s[h] for h in range(heads)], axis=1)
    gvb[...] = jnp.sum(dv, axis=0, keepdims=True)
    d_s[:, 2 * cw:] = dv.astype(BF)

    def write(dst, peer, lo, hi):
        def put(place, v):
            if peer is not None:
                v = v + peer[place, lo:hi].astype(F32)
            dst[place, lo:hi] = v.astype(BF)
        return put

    if split:
        block_rows(firstT, d_s, 0, write(out_s, None, 0, 3 * cw))
        block_rows(gmidT, att, 0, write(out_s, None, 3 * cw, 4 * cw))
        exchange = core_copy(out_s, peer_s, c_sem)
        exchange.start()

    @pl.loop(0, TOK // RT)
    def _(i):
        rows = pl.ds(pl.multiple_of(i * RT, RT), RT)
        acc[rows, :] = acc_in[rows, :] + nt(d_s[rows, :], W[:, :3 * cw])

    if split:
        exchange.wait()
    peer = peer_s if split else None
    block_rows(firstT, d_s, 1 if split else None, write(G, peer, 0, 3 * cw))
    block_rows(gmidT, att, 1 if split else None, write(G, peer, 3 * cw, 4 * cw))
    net.tick(6, True)


def attn_bwd(plan, gmid, gmidT, firstT, W, qkv, att, lse, acc, length, split):
    D = gmid.shape[1]
    cw = W.shape[1] // 4
    heads = cw // HD
    in_p, out_p, sems = plan_args(plan)
    side = pltpu.VMEM((D // 2, 4 * cw) if split else (16, 128), BF)
    got = pl.pallas_call(
        functools.partial(attn_bwd_kernel, length, heads, split, plan),
        out_shape=(shape((D // (1 + split), 4 * cw), BF), shape((1, cw), F32), shape((1, cw), F32), shape((TOK, D), F32), *plan.outs),
        in_specs=[VM] * 7 + [HB] + in_p,
        out_specs=(VM,) * 4 + out_p,
        scratch_shapes=[pltpu.VMEM((D, 4 * cw), BF), pltpu.VMEM((heads, TOK, HD), BF), pltpu.VMEM((TOK, 3 * cw), BF), pltpu.VMEM((heads, TOK, HD), F32), pltpu.VMEM((heads, TOK, HD), F32), side, side, pltpu.SemaphoreType.DMA, pltpu.SemaphoreType.DMA((2,))] + sems,
        compiler_params=params(plan, 52) if plan.copies or not split else pltpu.CompilerParams(vmem_limit_bytes=52 * 2**20, collective_id=plan.number, has_side_effects=True),
        cost_estimate=pl.CostEstimate(flops=2 * TOK * (D * cw * 8 + heads * 5 * TOK * HD * 6), bytes_accessed=30 * 2**20, transcendentals=heads * TOK * TOK),
        name="attn_bwd",
    )(gmid, gmidT, firstT, qkv, att, lse, acc, W, *plan.ins)
    return got[:4], got[4:]


def normalize(values):
    centre = jnp.mean(values, axis=-1, keepdims=True)
    centred = values - centre
    spread = jnp.mean(centred * centred, axis=-1, keepdims=True)
    inverse = lax.rsqrt(spread + norm_eps)
    return centred * inverse, inverse


def norm_back(grad_norm, normed, inverse, gain):
    scaled = grad_norm * gain
    first_mean = jnp.mean(scaled, axis=-1, keepdims=True)
    second_mean = jnp.mean(scaled * normed, axis=-1, keepdims=True)
    grad_input = inverse * (scaled - first_mean - normed * second_mean)
    return grad_input, jnp.sum(grad_norm * normed, axis=0), jnp.sum(grad_norm, axis=0)


def slot_table(d, groups):
    z = lax.axis_index("tensor")
    middle = 1 + d % 2
    return jnp.where(z == 0, 0, jnp.where(z == groups - 1, 1, 2)), (z == 0) | (z == groups - 1) | (z == middle)


HOPS = {
    "u1": (1, ((0, None),)), "u2": (3, ((1, None),)), "u3": (1, ((2, None),)),
    "w1": (1, ((3, None),)), "w2": (3, ((2, None),)), "w3": (1, ((1, None),)),
    "v1": (3, ((1, 0), (2, 1))), "v2": (1, ((2, 0), (1, 1))), "v3": (1, ((1, 0), (2, 1))),
}
HOP_FROM = {"u1": "me", "u2": "u1", "u3": "u2", "w1": "me", "w2": "w1", "w3": "w2", "v1": "me", "v2": "v1", "v3": "me"}
NAMES = ("u1", "w1", "v1", "v3"), ("u2", "w2", "v2"), ("u3", "w3")
BEGIN = {"u": 0, "w": 1, "v": 2}


class Wires:
    def __init__(self, s_sem, r_sem):
        self.s, self.r, self.n = s_sem, r_sem, 0
        self.d, self.z = lax.axis_index("dp"), lax.axis_index("tensor")

    def local(self, src, dst, used):
        i = self.n
        self.n += 1
        make = lambda: pltpu.make_async_copy(src, dst, self.s.at[i])
        return (lambda: pl.when(used)(lambda: make().start())), (lambda: pl.when(used)(lambda: make().wait()))

    def swap(self, src, dst, dp=0, z=0, sends=None):
        i = self.n
        self.n += 1
        make = lambda: pltpu.make_async_remote_copy(src_ref=src, dst_ref=dst, send_sem=self.s.at[i], recv_sem=self.r.at[i], device_id=(self.d ^ dp, self.z ^ z), device_id_type=MESH)
        if sends is None:
            return (lambda: make().start()), (lambda: make().wait())

        def any_of(z_here):
            hit = None
            for zz, cc in sends:
                this = z_here == zz
                if cc is not None:
                    this = this & (self.d % 2 == cc)
                hit = this if hit is None else hit | this
            return hit

        def start():
            pl.when(any_of(self.z))(lambda: make().start())

        def wait():
            pl.when(any_of(self.z))(lambda: make().wait_send())
            pl.when(any_of(self.z ^ z))(lambda: make().wait_recv())

        return start, wait


def greet(d, z, masks):
    sem = pltpu.get_barrier_semaphore()
    for dp, t in masks:
        pl.semaphore_signal(sem, inc=1, device_id=(d ^ dp, z ^ t), device_id_type=MESH)
    pl.semaphore_wait(sem, len(masks))


class Summing:
    def __init__(self, wires, H, land, zr, k):
        self.H, self.k = H, k
        self.rows = r = H.shape[0] // 4
        self.one, self.two = one, two = cut_rows(r)
        ax, by = land.at[pl.ds(0, 2 * one), :], land.at[pl.ds(2 * one, 2 * two), :]
        ay, bx = land.at[pl.ds(2 * r, one), :], land.at[pl.ds(2 * r + one, two), :]
        self.land = land
        h = lambda lo, n: H.at[pl.ds(lo, n), :]
        at = lambda ref, lo, n: ref.at[pl.ds(lo, n), :]
        self.c1 = [wires.swap(h(r, one), at(land, 0, one), dp=2), wires.swap(h(3 * r, one), at(land, one, one), dp=2),
                   wires.swap(h(2 * r + one, two), at(land, 2 * one, two), dp=4), wires.swap(h(3 * r + one, two), at(land, 2 * one + two, two), dp=4)]
        self.c2 = [wires.swap(h(2 * r, one), ay, dp=4), wires.swap(h(r + one, two), bx, dp=2)]
        self.c3 = [wires.swap(h(0, r), zr, z=k)] if k else []

    def add(self, lo, n, *froms):
        total = self.H[lo:lo + n, :].astype(F32)
        for f in froms:
            total = total + self.land[f:f + n, :].astype(F32)
        self.H[lo:lo + n, :] = total.astype(BF)

    def step1(self):
        for s, _ in self.c1:
            s()

    def step2(self):
        r, one, two = self.rows, self.one, self.two
        for _, w in self.c1:
            w()
        self.add(2 * r, one, one)
        self.add(r + one, two, 2 * one + two)
        for s, _ in self.c2:
            s()

    def step3(self):
        r, one, two = self.rows, self.one, self.two
        for _, w in self.c2:
            w()
        self.add(0, one, 0, 2 * r)
        self.add(one, two, 2 * one, 2 * r + one)
        for s, _ in self.c3:
            s()

    def step4(self):
        for _, w in self.c3:
            w()


class Sharing:
    def __init__(self, wires, mine, O, chunks):
        self.stages = []
        for lo, n in chunks:
            here = []
            for names in NAMES:
                row = []
                for name in names:
                    mask, sends = HOPS[name]
                    place = O.at[pl.ds(BEGIN[name[0]] * TOK + lo, n), :]
                    row.append(wires.swap(mine.at[pl.ds(lo, n), :] if HOP_FROM[name] == "me" else place, place, z=mask, sends=sends))
                here.append(row)
            self.stages.append(here)

    def start(self, chunk, stage):
        for s, _ in self.stages[chunk][stage]:
            s()

    def wait(self, chunk, stage):
        for _, w in self.stages[chunk][stage]:
            w()

    def on(self, chunk, stage):
        self.wait(chunk, stage - 1)
        self.start(chunk, stage)


OUT_CHUNKS = ((0, 256), (256, 256), (512, 224))
IN_CHUNKS = ((0, 128), (128, 128), (256, 128), (384, 128), (512, 128), (640, 96))
MASKS = [(1, 0), (2, 0), (4, 0), (0, 1), (0, 2), (0, 3)]
COPIES = 180


def back_kernel(length, heads, gain1, gain2, live, geb, tops, gout, midway, sec, firstT, x, mine, whole0, whole1, h2, h3, *rest):
    Ws, qkvs, atts, lses, rest = rest[:4], rest[4:8], rest[8:12], rest[12:16], rest[16:]
    (O_out, O_in, sum_a, sum_m, vec, g_s, gm_s, acc, gT, fT, x_s, W_s, Wo, qkv_s, att_s, lse_s, ga_s, d_s, dk_s, dv_s, out_s,
     Ha, La, Hm, Lm, za, zm, vr, w0_s, w1_s, l_sem, s_sem, r_sem) = rest
    cw = heads * HD
    D = g_s.shape[1]
    wires = Wires(s_sem, r_sem)
    d, z = wires.d, wires.z
    loads = {}
    order = [3, 2, 1, 0]
    names = iter(range(100))

    def load(key, src, dst):
        loads[key] = pltpu.make_async_copy(src, dst, l_sem.at[next(names)])

    load("midway", midway, acc)
    load("sec", sec, gm_s)
    load("gout", gout, g_s)
    load("firstT", firstT, fT)
    load("x", x, x_s)
    load("h2", h2, Hm.at[0])
    load("h3", h3, Hm.at[1])
    load("w0", whole0, w0_s)
    load("w1", whole1, w1_s)
    for i, k in enumerate(order):
        b = i % 2
        load(f"W{i}", Ws[k], W_s.at[b])
        load(f"qkv{i}", qkvs[k], qkv_s.at[b])
        load(f"att{i}", atts[k], att_s.at[b])
        load(f"lse{i}", lses[k], lse_s.at[b])
    for key in ("midway", "sec", "gout", "h2", "h3", "w1", "w0", "firstT", "W0", "qkv0", "att0", "lse0", "x"):
        loads[key].start()
    slot = jnp.where(z == 0, 0, jnp.where(z == 3, 1, 2))
    own_place = pl.ds(pl.multiple_of(slot * TOK, 256), TOK)
    used = (z == 0) | (z == 3) | (z == 1 + d % 2)
    own_out, own_in = wires.local(mine, O_out.at[own_place, :], used), wires.local(g_s, O_in.at[own_place, :], used)
    share_out = Sharing(wires, mine, O_out, OUT_CHUNKS)
    share_in = Sharing(wires, g_s, O_in, IN_CHUNKS)
    sums = {"m2": Summing(wires, Hm.at[0], Lm.at[0], zm.at[1], 2), "m3": Summing(wires, Hm.at[1], Lm.at[1], zm.at[2], 3)}
    for k in range(4):
        sums[f"b{k}"] = Summing(wires, Ha.at[k], La.at[k], za.at[max(k - 1, 0)], k)
    z_m1 = wires.swap(w1_s, zm.at[0], z=1)
    exchange = {k: wires.swap(out_s, Ha.at[k], dp=1) for k in range(4)}
    spread = [wires.swap(vec, vr.at[i], dp=dp, z=t) for i, (dp, t) in enumerate(((1, 0), (2, 0), (4, 0), (0, 1), (0, 2)))]
    greet(d, z, MASKS)

    todo = {
        -3: [lambda: share_out.start(0, 0), own_out[0]],
        -2: [lambda: loads["h2"].wait(), sums["m2"].step1, lambda: loads["w1"].wait(), z_m1[0]],
        0: [lambda: loads["h3"].wait(), lambda: loads["w0"].wait()],
        2: [lambda: share_out.on(0, 1), lambda: share_out.start(1, 0)],
        3: [sums["m2"].step2, sums["m3"].step1],
        5: [sums["m2"].step3],
        8: [sums["b3"].step1, lambda: share_out.on(0, 2), lambda: share_out.on(1, 1), lambda: share_out.start(2, 0)],
        12: [sums["m3"].step2],
        13: [sums["b3"].step2],
        15: [sums["m3"].step3, sums["b3"].step3],
        18: [sums["b2"].step1, lambda: share_out.on(1, 2), lambda: share_out.on(2, 1)],
        23: [sums["b2"].step2],
        25: [sums["b2"].step3],
        28: [sums["b1"].step1, lambda: share_out.on(2, 2)],
        33: [sums["b1"].step2],
        35: [sums["b1"].step3],
        38: [sums["b0"].step1],
    }

    def tick(t):
        for action in todo.get(t, ()):
            action()

    vec[...] = jnp.zeros_like(vec)
    for key in ("midway", "sec", "gout"):
        loads[key].wait()

    def total_of(row, value):
        vec[row:row + 1, :D] += jnp.sum(value, axis=0, keepdims=True)

    def put_row(where, lo, value):
        n = value.shape[1]
        hit = lax.broadcasted_iota(jnp.int32, (8, n), 0) == where
        vec[0:8, lo:lo + n] += jnp.where(hit, jnp.broadcast_to(value, (8, n)), 0.0)

    @pl.loop(0, TOK // RT)
    def _(i):
        for t in range(3):
            pl.when(i == t)(functools.partial(tick, t - 3))
        rows = pl.ds(pl.multiple_of(i * RT, RT), RT)
        normed, inverse = normalize(acc[rows, :])
        e = gm_s[rows, :]
        go = g_s[rows, :].astype(F32)
        scaled = e * gain2[...]
        mean1 = jnp.mean(scaled, axis=-1, keepdims=True)
        mean2 = jnp.mean(scaled * normed, axis=-1, keepdims=True)
        gm = go + inverse * (scaled - mean1 - normed * mean2)
        total_of(4, gm)
        total_of(5, go)
        total_of(8, e * normed)
        total_of(9, e)
        gm_s[rows, :] = gm
        g_s[rows, :] = gm.astype(BF)
        gT[:, rows] = gm.T.astype(BF)

    loads["firstT"].wait()
    acc[...] = jnp.zeros_like(acc)
    for i, k in enumerate(order):
        base, b = 10 * i, i % 2
        W, qkv, att, lse, H = W_s.at[b], qkv_s.at[b], att_s.at[b], lse_s.at[b], Ha.at[k]
        for key in ("W", "qkv", "att", "lse"):
            loads[f"{key}{i}"].wait()
        if i < 3:
            for key in ("W", "qkv", "att", "lse"):
                loads[f"{key}{i + 1}"].start()
        tick(base)
        Wo[...] = W[:, 3 * cw:]

        @pl.loop(0, TOK // RT)
        def _(t):
            rows = pl.ds(pl.multiple_of(t * RT, RT), RT)
            g = nn(g_s[rows, :], Wo[...]).astype(BF)
            for h in range(heads):
                ga_s[h, rows, :] = g[:, h * HD:(h + 1) * HD]

        tick(base + 1)
        dk_s[...] = jnp.zeros_like(dk_s)
        dv_s[...] = jnp.zeros_like(dv_s)
        place = z ^ k

        @pl.loop(0, TOK // RT)
        def _(t):
            for n in range(3):
                pl.when(t == n)(functools.partial(tick, base + 2 + n))
            rows = pl.ds(pl.multiple_of(t * RT, RT), RT)
            cid = lax.broadcasted_iota(jnp.int32, (1, TOK), 1)
            dqs = []
            for h in range(heads):
                q, kk, v, g = qkv[h, rows, :], qkv[heads + h], qkv[2 * heads + h], ga_s[h, rows, :]
                s = nt(q, kk)
                p = jnp.exp2(s * (SC * LOG2E) - lse[rows, h:h + 1])
                p = jnp.where(cid < length, p, 0.0)
                dp = nt(g, v)
                dd = jnp.sum(g.astype(F32) * att[rows, h * HD:(h + 1) * HD].astype(F32), axis=1, keepdims=True)
                ds = (p * (dp - dd)).astype(BF)
                dqs.append(nn(ds, kk) * SC)
                dk_s[h] += tn(ds, q)
                dv_s[h] += tn(p.astype(BF), g)
            dq = jnp.concatenate(dqs, axis=1)
            put_row(place, 0, jnp.sum(dq, axis=0, keepdims=True))
            d_s[rows, :cw] = dq.astype(BF)

        d_s[:, cw:2 * cw] = jnp.concatenate([dk_s[h] * SC for h in range(heads)], axis=1).astype(BF)
        dv = jnp.concatenate([dv_s[h] for h in range(heads)], axis=1)
        put_row(place, 384, jnp.sum(dv, axis=0, keepdims=True))
        d_s[:, 2 * cw:] = dv.astype(BF)
        put_row(place, 768, geb[k])
        put_row(place, 1920, tops[k])
        tick(base + 5)

        def write(dst, lo, hi, add):
            def put(where, val):
                if add:
                    val = val + dst[where, lo:hi].astype(F32)
                dst[where, lo:hi] = val.astype(BF)
            return put

        block_rows(fT, d_s, 0, write(out_s, 0, 3 * cw, False))
        block_rows(gT, att, 0, write(out_s, 3 * cw, 4 * cw, False))
        exchange[k][0]()
        tick(base + 6)

        @pl.loop(0, TOK // RT)
        def _(t):
            rows = pl.ds(pl.multiple_of(t * RT, RT), RT)
            acc[rows, :] += nt(d_s[rows, :], W[:, :3 * cw])

        tick(base + 7)
        exchange[k][1]()
        block_rows(fT, d_s, 1, write(H, 0, 3 * cw, True))
        block_rows(gT, att, 1, write(H, 3 * cw, 4 * cw, True))
        tick(base + 8)

    loads["x"].wait()

    @pl.loop(0, TOK // RT)
    def _(i):
        rows = pl.ds(pl.multiple_of(i * RT, RT), RT)
        normed, inverse = normalize(x_s[rows, :].astype(F32))
        e = acc[rows, :]
        scaled = e * gain1[...]
        mean1 = jnp.mean(scaled, axis=-1, keepdims=True)
        mean2 = jnp.mean(scaled * normed, axis=-1, keepdims=True)
        total_of(6, e * normed)
        total_of(7, e)
        g_s[rows, :] = ((gm_s[rows, :] + inverse * (scaled - mean1 - normed * mean2)) * live[...]).astype(BF)
        for t in range(3):
            @pl.when(i == t)
            def _():
                share_in.start(2 * t, 0)
                share_in.start(2 * t + 1, 0)

    own_in[0]()
    after = {0: [spread[0][0], sums["b0"].step2], 1: [], 2: [sums["b0"].step3]}
    row = lax.broadcasted_iota(jnp.int32, vec.shape, 1)

    def fold(i):
        spread[i][1]()
        a, c = vec[...], vr[i]
        vec[...] = jnp.where(row < 1920, a + c, jnp.maximum(a, c))
        if i < 4:
            spread[i + 1][0]()

    n = len(IN_CHUNKS)
    for t in range(n + 2):
        if t < n:
            share_in.on(t, 1)
        for action in after.get(t, ()):
            action()
        if 1 <= t <= n:
            share_in.on(t - 1, 2)
        if 1 <= t <= 5:
            fold(t - 1)
    for c in range(3):
        share_out.wait(c, 2)
    own_out[1]()
    own_in[1]()
    z_m1[1]()
    for s in ("m2", "m3", "b3", "b2", "b1"):
        sums[s].step4()
    r = sum_a.shape[0]
    sum_a[...] = Ha[0, :r, :].astype(F32) + za[0].astype(F32) + za[1].astype(F32) + za[2].astype(F32)
    sum_m[...] = w0_s[...] + zm[0].astype(F32) + zm[1].astype(F32) + zm[2].astype(F32)
    for c in range(n):
        share_in.wait(c, 2)


def back(number, gain1, gain2, live, geb, tops, gout, midway, sec, firstT, x, mine, whole0, whole1, h2, h3, kept, Ws, length):
    D = gout.shape[1]
    cw = Ws[0].shape[1] // 4
    cm = h2.shape[1]
    heads = cw // HD
    r = D // 8
    qkvs, atts, lses = zip(*kept)
    vm = pltpu.VMEM
    dma = pltpu.SemaphoreType.DMA
    return pl.pallas_call(
        functools.partial(back_kernel, length, heads),
        out_shape=(shape((3 * TOK, D), BF), shape((3 * TOK, D), BF), shape((r, 4 * cw), F32), shape((r, cm), F32), shape((16, 2048), F32)),
        in_specs=[VM] * 5 + [HB] * 26,
        out_specs=(HB, HB, VM, VM, VM),
        scratch_shapes=[vm((TOK, D), BF), vm((TOK, D), F32), vm((TOK, D), F32), vm((D, TOK), BF), vm((D, TOK), BF), vm((TOK, D), BF),
                        vm((2, D, 4 * cw), BF), vm((D, cw), BF), vm((2, 3 * heads, TOK, HD), BF), vm((2, TOK, cw), BF), vm((2, TOK, 128), F32),
                        vm((heads, TOK, HD), BF), vm((TOK, 3 * cw), BF), vm((heads, TOK, HD), F32), vm((heads, TOK, HD), F32), vm((4 * r, 4 * cw), BF),
                        vm((4, 4 * r, 4 * cw), BF), vm((4, 3 * r, 4 * cw), BF), vm((2, 4 * r, cm), BF), vm((2, 3 * r, cm), BF),
                        vm((3, r, 4 * cw), BF), vm((3, r, cm), BF), vm((5, 16, 2048), F32), vm((r, cm), F32), vm((r, cm), BF),
                        dma((32,)), dma((COPIES,)), dma((COPIES,))],
        compiler_params=pltpu.CompilerParams(vmem_limit_bytes=63 * 2**20, collective_id=number, has_side_effects=True),
        cost_estimate=pl.CostEstimate(flops=4 * 2 * TOK * (D * cw * 8 + heads * 5 * TOK * HD * 6), bytes_accessed=60 * 2**20, transcendentals=4 * heads * TOK * TOK),
        name="back",
    )(gain1, gain2, live, geb, tops, gout, midway, sec, firstT, x, mine, whole0, whole1, h2, h3, *Ws, *qkvs, *atts, *lses)


class General:
    split = 0

    def __init__(self, groups, attn_own, mlp_own):
        self.groups = groups
        self.attn, self.mlp = self.spread(attn_own), self.spread(mlp_own)

    def vectors(self, own):
        every = lax.all_gather(own, "tensor")
        return [every[i] for i in range(self.groups)]

    def spread(self, own):
        d, count = lax.axis_index("dp"), lax.axis_size("dp")
        rows = own.shape[0] // count
        piece = lax.dynamic_slice_in_dim(own, d * rows, rows, 0)
        piece = lax.all_gather(piece, "tensor")
        whole = lax.all_gather(piece, "dp", axis=1, tiled=True)
        return [whole[i] for i in range(self.groups)]

    def plan(self, name):
        return Plan(0)

    def done(self, name, got):
        pass

    def reduce(self, parts):
        part = lax.psum_scatter(jnp.stack(parts), "dp", scatter_dimension=1, tiled=True)
        return lax.psum_scatter(part, "tensor", scatter_dimension=0, tiled=True)[0].astype(F32)

    def collect(self, grad_attn, grad_mlp):
        return self.reduce(grad_attn), self.reduce(grad_mlp)

    def by_index(self, items):
        return jnp.stack(items)

    def give(self, mine):
        self.mine = mine

    def gathered(self):
        return self.share(self.mine)

    def share(self, mine):
        every = lax.all_gather(mine, "tensor")
        middle = 1 + lax.axis_index("dp") % 2
        return jnp.stack([every[0], every[self.groups - 1], lax.dynamic_index_in_dim(every, middle, 0, keepdims=False)])


class Line:
    split = 1
    groups = 4
    work = {
        "A0": ("z a1", "z a2", "g a1"),
        "A1": ("g a2", "z a3", "z m1", "zl m2"),
        "A2": ("g a3", "zh m2"),
        "A3": ("g m1", "z m3"),
        "M0": ("g m2",),
        "M1": ("g m3", "r1 m0"),
        "M2": ("r2 m0", "r1 m1"),
        "M3": ("r2 m1",),
    }

    def __init__(self, groups, attn_own, mlp_own):
        d = lax.axis_index("dp")
        self.rows = attn_own.shape[0] // 8
        self.one, self.two = cut_rows(self.rows)
        self.attn, self.mlp = [attn_own, None, None, None], [mlp_own, None, None, None]
        self.piece = {}
        for name, own in (("a", attn_own), ("m", mlp_own)):
            self.piece[name + "0"] = lax.dynamic_slice_in_dim(own, d * self.rows, self.rows, 0)
        self.state, self.hops = {}, {}

    def vectors(self, own):
        return [own] + [lax.ppermute(own, "tensor", [(i, i ^ k) for i in range(4)]) for k in (1, 2, 3)]

    def plan(self, name):
        if name == "end":
            return None
        plan = Plan(list(self.work).index(name))
        self.made = made = []
        rows, one, two = self.rows, self.one, self.two
        fresh = {}
        for job in self.work[name]:
            kind, what, *more = job.split()
            if kind == "z":
                k = int(what[1])
                src = self.piece[what[0] + ("2" if k == 3 else "0")]
                out = plan.give(src.shape)
                plan.copy(0, 2 if "g " + what in self.work[name] else None, plan.take(src), 0, out, 0, rows, z=1 if k == 3 else k)
                fresh[what] = out
                made.append((self.piece, what))
            elif kind in ("zl", "zh"):
                src = self.piece[what[0] + "0"]
                lo, size = (0, two) if kind == "zl" else (two, one)
                out = plan.give((size, src.shape[1]))
                plan.copy(0, None, plan.take(src), lo, out, 0, size, z=2)
                made.append((self.piece, what + kind))
            elif kind == "g":
                t = (2, 3, 4) if what in fresh else (0, 2, 4) if name[0] == "M" else (0, 2, 3)
                src = fresh[what] if what in fresh else plan.take(self.piece[what])
                out = plan.give((rows * 8, self.piece[what[0] + "0"].shape[1]))
                at = lambda mask, off=0: lambda d: (d ^ mask) * rows + off
                plan.copy(t[0], None, src, 0, out, at(0), rows)
                for mask in (2, 4, 1):
                    plan.copy(t[0], t[1], src, 0, out, at(0), rows, dp=mask)
                plan.copy(t[1], t[2], out, at(2), out, at(2), one, dp=4)
                plan.copy(t[1], t[2], out, at(4, one), out, at(4, one), two, dp=2)
                for mask in (2, 4):
                    plan.copy(t[1], None, out, at(mask), out, at(mask), rows, dp=1)
                plan.copy(t[2], None, out, at(6), out, at(6), rows, dp=1)
                made.append((self.attn if what[0] == "a" else self.mlp, int(what[1])))
            elif kind == "r1":
                s = self.state[what]
                columns = s["h"].shape[1]
                h, ax, by = plan.take(s["h"]), plan.give((2 * one, columns)), plan.give((2 * two, columns))
                plan.copy(0, None, h, rows, ax, 0, one, dp=2)
                plan.copy(0, None, h, 3 * rows, ax, one, one, dp=2)
                plan.copy(0, None, h, 2 * rows + one, by, 0, two, dp=4)
                plan.copy(0, None, h, 3 * rows + one, by, two, two, dp=4)
                made += [(s, "ax"), (s, "by")]
            elif kind == "r2":
                s = self.state[what]
                src = self.second(s)
                t, ay, bx = plan.take(src), plan.give((one, src.shape[1])), plan.give((two, src.shape[1]))
                plan.copy(0, None, t, 0, ay, 0, one, dp=4)
                plan.copy(0, None, t, one, bx, 0, two, dp=2)
                made += [(s, "ay"), (s, "bx")]
            elif kind == "r3":
                s, k = self.state[what], int(what[1])
                s["whole"] = self.third(s)
                if k:
                    src = s["whole"].astype(BF)
                    plan.copy(0, None, plan.take(src), 0, plan.give(src.shape), 0, rows, z=k)
                    made.append((s, "z"))
            elif kind == "h":
                half = int(more[0])
                mask, sends = HOPS[what]
                begin = HOP_FROM[what]
                src = self.mine if begin == "me" else self.hops[begin, half]
                size = self.mine.shape[0] // 2
                plan.copy(0, None, plan.take(src), half * size if begin == "me" else 0, plan.give((size, src.shape[1])), 0, size, z=mask, sends=sends)
                made.append((self.hops, (what, half)))
        return plan

    def done(self, name, got):
        for (store, key), value in zip(self.made, got, strict=True):
            store[key] = value
        if name == "A2":
            self.piece["m2"] = jnp.concatenate([self.piece.pop("m2zl"), self.piece.pop("m2zh")])

    def summed(self, name, h):
        self.state[name] = {"h": h}

    def h(self, s, q, lo, hi):
        return s["h"][q * self.rows + lo:q * self.rows + hi].astype(F32)

    def second(self, s):
        one, two = self.one, self.two
        return jnp.concatenate([self.h(s, 2, 0, one) + s["ax"][one:].astype(F32), self.h(s, 1, one, self.rows) + s["by"][two:].astype(F32)]).astype(BF)

    def third(self, s):
        one, two = self.one, self.two
        a = self.h(s, 0, 0, one) + s["ax"][:one].astype(F32) + s["ay"].astype(F32)
        b = self.h(s, 0, one, self.rows) + s["by"][:two].astype(F32) + s["bx"].astype(F32)
        return jnp.concatenate([a, b])

    def dp(self, a, m):
        return lax.ppermute(a, "dp", [(i, i ^ m) for i in range(8)])

    def collect(self, grad_attn, grad_mlp):
        rows, one, two = self.rows, self.one, self.two
        out = []
        for name in ("b", "m"):
            total = None
            for k in range(4):
                s = self.state[name + str(k)]
                if "ax" not in s:
                    s["ax"] = self.dp(jnp.concatenate([s["h"][rows:rows + one], s["h"][3 * rows:3 * rows + one]]), 2)
                    s["by"] = self.dp(jnp.concatenate([s["h"][2 * rows + one:3 * rows], s["h"][3 * rows + one:]]), 4)
                if "ay" not in s:
                    t = self.second(s)
                    s["ay"], s["bx"] = self.dp(t[:one], 4), self.dp(t[one:], 2)
                if "whole" not in s:
                    s["whole"] = self.third(s)
                if k and "z" not in s:
                    s["z"] = lax.ppermute(s["whole"].astype(BF), "tensor", [(i, i ^ k) for i in range(4)])
                part = s["z"].astype(F32) if k else s["whole"]
                total = part if total is None else total + part
            out.append(total)
        return out

    def by_index(self, items):
        return jnp.take(jnp.stack(items), lax.axis_index("tensor") ^ jnp.arange(4), axis=0)

    def give(self, mine):
        self.mine = jnp.pad(mine, ((0, -mine.shape[0] % 32), (0, 0)))

    def select(self, a, g):
        z, c = lax.axis_index("tensor"), lax.axis_index("dp") % 2
        near = jnp.where(c == 0, z, 3 - z)

        def pick(who, options):
            out = options[3]
            for i in (2, 1, 0):
                out = jnp.where(who == i, options[i], out)
            return out

        return jnp.stack([pick(z, [a, g["u1"], g["u2"], g["u3"]]), pick(z, [g["w3"], g["w2"], g["w1"], a]), pick(near, [g["v3"], a, g["v1"], g["v2"]])])

    def gathered(self):
        size = self.mine.shape[0] // 2
        return jnp.concatenate([self.select(self.mine[h * size:(h + 1) * size], {n: self.hops[n, h] for n in HOPS}) for h in (0, 1)], axis=1)

    def share(self, mine):
        rows = -(-mine.shape[0] // 3 // 16) * 16
        result = []
        for start in range(0, mine.shape[0], rows):
            have = {"me": mine[start:start + rows]}
            for name in ("u1", "w1", "v1", "v3", "u2", "w2", "v2", "u3", "w3"):
                mask, sends = HOPS[name]
                pairs = [(i * 4 + s, i * 4 + (s ^ mask)) for i in range(8) for s, c in sends if c is None or c == i % 2]
                have[name] = lax.ppermute(have[HOP_FROM[name]], ("dp", "tensor"), pairs)
            result.append(self.select(have["me"], have))
        return jnp.concatenate(result, axis=1)


def shards(images, counts, cotangent, query_w, query_b, key_w, value_w, value_b, out_w, out_b, norm1_gain, norm1_shift,
           norm2_gain, norm2_shift, expand_w, expand_b, shrink_w, shrink_b):
    slots, length, width = images.shape
    groups = lax.axis_size("tensor")
    d, z = lax.axis_index("dp"), lax.axis_index("tensor")
    cw, fw = query_w.shape[1], expand_w.shape[1]
    heads = cw // HD
    cut = fw // 128 * 128
    slot, used = slot_table(d, groups)
    live = jnp.where(used & (slot < counts[0]), 1.0, 0.0).astype(F32)
    pad = lambda a: jnp.pad(a, ((0, TOK - length), (0, 0)))

    attn_own = jnp.concatenate([query_w, key_w, value_w, out_w.T], axis=1)
    shrink_t = shrink_w.T
    mlp_own = jnp.concatenate([expand_w[:, :cut], shrink_t[:, :cut], expand_w[:, cut:], shrink_t[:, cut:]], axis=1)
    net = (Line if (groups, lax.axis_size("dp")) == (4, 8) else General)(groups, attn_own, mlp_own)
    split = net.split
    biases = net.vectors(jnp.concatenate([query_b, value_b, expand_b]))

    x_low = pad(lax.dynamic_index_in_dim(images, slot, 0, keepdims=False))
    x = x_low.astype(F32)
    gout = pad(lax.dynamic_index_in_dim(cotangent, slot, 0, keepdims=False)) * live.astype(BF)
    gout_t = gout.T
    normed1, inverse1 = normalize(x)
    first = (normed1 * norm1_gain + norm1_shift).astype(BF)
    first_t = first.T
    acc = x + out_b
    kept, tops = [], []
    for k in range(groups):
        b = biases[k]
        plan = net.plan(f"A{k}")
        (qkv, att, lse, top, acc), got = attn_fwd(plan, first, net.attn[k], b[None, :cw], b[None, cw:2 * cw], acc, length)
        net.done(f"A{k}", got)
        kept.append((qkv, att, lse))
        tops.append(top[:, 0])
    midway = acc
    normed2, inverse2 = normalize(midway)
    second = (normed2 * norm2_gain + norm2_shift).astype(BF)
    second_t = second.T
    mlp = midway + shrink_b
    sec = jnp.zeros((TOK, width), F32)
    grad_mlp, geb = [], []
    for k in range(groups):
        plan = net.plan(f"M{k}")
        (grad, g_b, mlp, sec), got = mlp_call(plan, second, second_t, gout, gout_t, net.mlp[k], biases[k][None, 2 * cw:], mlp, sec, split)
        net.done(f"M{k}", got)
        if split:
            net.summed(f"m{k}", grad)
        grad_mlp.append(grad)
        geb.append(g_b[0, :fw] if not split else g_b[0])
    if split:
        net.plan("end")
        mine = (mlp * live).astype(BF)
        state = net.state
        out_all, in_all, sum_attn, sum_mlp, vec = back(
            12, norm1_gain[None], norm2_gain[None], live[None, None], jnp.stack(geb)[:, None], jnp.where(live > 0.0, jnp.stack(tops), -1e30)[:, None],
            gout, midway, sec, first_t, x_low, mine, net.third(state["m0"]), net.third(state["m1"]).astype(BF), state["m2"]["h"], state["m3"]["h"], kept, net.attn, length)
        outputs = out_all.reshape(3, TOK, width)[:, :length]
        input_grads = in_all.reshape(3, TOK, width)[:, :length].astype(F32)
        own = lax.dynamic_index_in_dim(vec, z, 0, keepdims=False)
        grad_query_b, grad_value_b, grad_expand_b, logit_top = own[:cw], own[384:384 + cw], own[768:768 + fw], own[1920:1920 + heads]
        tail = [vec[4 + i, :width] for i in range(6)]
    else:
        back2, gn2g, gn2s = norm_back(sec, normed2, inverse2, norm2_gain)
        gout32 = gout.astype(F32)
        gmid = gout32 + back2
        gmid_low = gmid.astype(BF)
        gmid_t = gmid_low.T
        acc = jnp.zeros((TOK, width), F32)
        grad_attn, gqb, gvb = [None] * groups, [None] * groups, [None] * groups
        for k in reversed(range(groups)):
            (grad, g_q, g_v, acc), _ = attn_bwd(Plan(0), gmid_low, gmid_t, first_t, net.attn[k], *kept[k], acc, length, split)
            grad_attn[k], gqb[k], gvb[k] = grad, g_q[0], g_v[0]
        back1, gn1g, gn1s = norm_back(acc, normed1, inverse1, norm1_gain)
        input_grad = ((gmid + back1) * live)[:length].astype(BF)

        outputs = net.share((mlp[:length] * live).astype(BF))
        input_grads = net.share(input_grad).astype(F32)
        sum_attn, sum_mlp = net.collect(grad_attn, grad_mlp)
        flat = lambda items: net.by_index(items).reshape(-1)
        vector = jnp.concatenate([flat(gqb), flat(gvb), flat(geb), jnp.sum(gmid, axis=0), jnp.sum(gout32, axis=0), gn1g, gn1s, gn2g, gn2s])
        vector = lax.psum(vector, ("dp", "tensor"))
        part = lambda start, size: lax.dynamic_slice_in_dim(vector, start, size, 0)
        whole, hidden = cw * groups, fw * groups
        tail = [vector[2 * whole + hidden + i * width:][:width] for i in range(6)]
        logit_top = lax.pmax(jnp.where(live > 0.0, net.by_index(tops), -1e30), ("dp", "tensor"))
        logit_top = lax.dynamic_index_in_dim(logit_top, z, 0, keepdims=False)
        grad_query_b, grad_value_b, grad_expand_b = part(z * cw, cw), part(whole + z * cw, cw), part(2 * whole + z * fw, fw)
    factor = jnp.sqrt(clip_limit / jnp.maximum(logit_top, clip_limit))
    column_factor = jnp.repeat(factor, HD)
    clipped_query = (query_w.astype(F32) * column_factor).astype(BF)
    clipped_key = (key_w.astype(F32) * column_factor).astype(BF)
    unpack = lambda a, i: jnp.concatenate([a[:, i * cut:(i + 1) * cut], a[:, 2 * cut + i * (fw - cut):][:, :fw - cut]], axis=1)
    return (outputs, input_grads, sum_attn[:, :cw], grad_query_b, sum_attn[:, cw:2 * cw], sum_attn[:, 2 * cw:3 * cw], grad_value_b,
            sum_attn[:, 3 * cw:].T, tail[0], tail[2], tail[3], tail[4], tail[5], unpack(sum_mlp, 0), grad_expand_b, unpack(sum_mlp, 1).T,
            tail[1], clipped_query, clipped_key)


def solution(mesh):
    columns, rows, vector = P(None, "tensor"), P("tensor", None), P("tensor")
    whole = P("dp", None, None)
    return jax.shard_map(
        shards, mesh=mesh,
        in_specs=(whole, P("dp"), whole, columns, vector, columns, columns, vector, rows, P(), P(), P(), P(), P(), columns, vector, rows, P()),
        out_specs=(whole, whole, P("dp", "tensor"), vector, P("dp", "tensor"), P("dp", "tensor"), vector, P("tensor", "dp"), P(), P(), P(), P(), P(),
                   P("dp", "tensor"), vector, P("tensor", "dp"), P(), columns, columns),
        check_vma=False)
```

```python
import functools
import math

import jax
import jax.numpy as jnp
from jax import lax
from jax.experimental import pallas as pl
from jax.experimental.pallas import tpu as pltpu
from jax.sharding import PartitionSpec as P

HD = 72
TOK = 768
RT = 256
SC = 1 / math.sqrt(HD)
LOG2E = 1.4426950408889634
F32 = jnp.float32
BF = jnp.bfloat16
norm_eps = 1e-06
clip_limit = 3.0
tanh_coef = 0.7978845608028654
cube_coef = 0.044715
VM = pl.BlockSpec(memory_space=pltpu.VMEM)
HB = pl.BlockSpec(memory_space=pl.ANY)
MESH = pl.DeviceIdType.MESH


def nn(a, b):
    return jnp.dot(a, b, preferred_element_type=F32)


def nt(a, b):
    return lax.dot_general(a, b, (((1,), (1,)), ((), ())), preferred_element_type=F32)


def tn(a, b):
    return lax.dot_general(a, b, (((0,), (0,)), ((), ())), preferred_element_type=F32)


def shape(dims, dtype):
    return jax.ShapeDtypeStruct(dims, dtype)


def cut_rows(rows):
    first = (rows // 2 + 15) // 16 * 16
    return first, rows - first


def block_rows(lhs, rhs, half, write):
    if half is None:
        @pl.loop(0, lhs.shape[0] // 384)
        def _(t):
            place = pl.ds(pl.multiple_of(t * 384, 128), 384)
            write(place, nn(lhs[place, :], rhs[...]))
    else:
        rows = lhs.shape[0] // 8
        d = lax.axis_index("dp")

        @pl.loop(0, 2)
        def _(t):
            r = 4 * t + 1 - half
            both = [lhs[pl.ds(pl.multiple_of((d ^ q) * rows, 16), rows), :] for q in (r, r + 2)]
            write(pl.ds(pl.multiple_of(t * 2 * rows, 16), 2 * rows), nn(jnp.concatenate(both, axis=0), rhs[...]))


def attn_fwd_kernel(length, heads, first, qb, vb, acc_in, W, qkv, att, lse, tops, acc):
    cw = heads * HD

    @pl.loop(0, TOK // RT)
    def _(i):
        rows = pl.ds(pl.multiple_of(i * RT, RT), RT)
        t = nn(first[rows, :], W[:, :3 * cw])
        q = (t[:, :cw] + qb[...]).astype(BF)
        k = t[:, cw:2 * cw].astype(BF)
        v = (t[:, 2 * cw:] + vb[...]).astype(BF)
        for h in range(heads):
            qkv[h, rows, :] = q[:, h * HD:(h + 1) * HD]
            qkv[heads + h, rows, :] = k[:, h * HD:(h + 1) * HD]
            qkv[2 * heads + h, rows, :] = v[:, h * HD:(h + 1) * HD]

    tops[...] = jnp.full(tops.shape, -1e30, F32)

    @pl.loop(0, TOK // RT)
    def _(i):
        rows = pl.ds(pl.multiple_of(i * RT, RT), RT)
        rid = lax.broadcasted_iota(jnp.int32, (RT, 1), 0) + i * RT
        cid = lax.broadcasted_iota(jnp.int32, (1, TOK), 1)
        res = []
        for h in range(heads):
            s = nt(qkv[h, rows, :], qkv[heads + h])
            s = jnp.where(cid < length, s, -1e30)
            m = jnp.max(s, axis=1, keepdims=True)
            e = jnp.exp2((s - m) * (SC * LOG2E))
            l = jnp.sum(e, axis=1, keepdims=True)
            o = nn(e.astype(BF), qkv[2 * heads + h]) * (1.0 / l)
            res.append(o.astype(BF))
            lse[rows, h:h + 1] = m * (SC * LOG2E) + jnp.log2(l)
            tops[h:h + 1, :] = jnp.maximum(tops[h:h + 1, :], jnp.max(jnp.where(rid < length, m, -1e30)) * SC)
        a = jnp.concatenate(res, axis=1)
        att[rows, :] = a
        acc[rows, :] = acc_in[rows, :] + nt(a, W[:, 3 * cw:])


def attn_fwd(first, W, qb, vb, acc, length):
    D = first.shape[1]
    cw = W.shape[1] // 4
    heads = cw // HD
    return pl.pallas_call(
        functools.partial(attn_fwd_kernel, length, heads),
        out_shape=(shape((3 * heads, TOK, HD), BF), shape((TOK, cw), BF), shape((TOK, 128), F32), shape((heads, 128), F32), shape((TOK, D), F32)),
        in_specs=[VM] * 5,
        out_specs=(VM,) * 5,
        compiler_params=pltpu.CompilerParams(vmem_limit_bytes=44 * 2**20),
        cost_estimate=pl.CostEstimate(flops=2 * TOK * (D * cw * 4 + heads * 2 * TOK * HD * 6), bytes_accessed=25 * 2**20, transcendentals=heads * TOK * TOK),
        name="attn_fwd",
    )(first, qb, vb, acc, W)


def gelu_parts(u):
    u2 = u * u
    t = jnp.tanh(u * (tanh_coef + (tanh_coef * cube_coef) * u2))
    hu = 0.5 * (1.0 + t)
    return u * hu, hu + u * (0.5 * tanh_coef) * (1.0 - t * t) * (1.0 + (3.0 * cube_coef) * u2)


def mlp_kernel(fw, second, secondT, gout, goutT, eb, mlp_in, sec_in, W, G, geb, mlp, sec, E, ST, act_s, gpre_s):
    cut = fw // 128 * 128
    tail = fw - cut
    E[:, :cut] = W[:, :cut]
    ST[:, :cut] = W[:, cut:2 * cut]
    last = W[:, 2 * cut:]
    blank = jnp.zeros((last.shape[0], 128 - tail), BF)
    E[:, cut:] = jnp.concatenate([last[:, :tail], blank], axis=1)
    ST[:, cut:] = jnp.concatenate([last[:, tail:], blank], axis=1)
    geb[...] = jnp.zeros_like(geb)

    @pl.loop(0, TOK // RT)
    def _(i):
        rows = pl.ds(pl.multiple_of(i * RT, RT), RT)
        act, slope = gelu_parts(nn(second[rows, :], E[...]) + eb[...])
        act_s[rows, :] = act.astype(BF)
        gp = nn(gout[rows, :], ST[...]) * slope
        geb[...] += jnp.sum(gp, axis=0, keepdims=True)
        gpre_s[rows, :] = gp.astype(BF)
        mlp[rows, :] = mlp_in[rows, :] + nt(act_s[rows, :], ST[...])
        sec[rows, :] = sec_in[rows, :] + nt(gpre_s[rows, :], E[...])

    def write(lo, last):
        def put(place, v):
            v = v.astype(BF)
            G[place, lo:lo + cut] = v[:, :cut]
            G[place, last:last + tail] = v[:, cut:fw]
        return put

    block_rows(secondT, gpre_s, None, write(0, 2 * cut))
    block_rows(goutT, act_s, None, write(cut, 2 * cut + tail))


def mlp_call(second, secondT, gout, goutT, W, eb, mlp, sec):
    D = second.shape[1]
    fw = W.shape[1] // 2
    wide = fw // 128 * 128 + 128
    eb = jnp.pad(eb, ((0, 0), (0, wide - fw)))
    return pl.pallas_call(
        functools.partial(mlp_kernel, fw),
        out_shape=(shape((D, 2 * fw), BF), shape((1, wide), F32), shape((TOK, D), F32), shape((TOK, D), F32)),
        in_specs=[VM] * 8,
        out_specs=(VM,) * 4,
        scratch_shapes=[pltpu.VMEM((D, wide), BF)] * 2 + [pltpu.VMEM((TOK, wide), BF)] * 2,
        compiler_params=pltpu.CompilerParams(vmem_limit_bytes=56 * 2**20),
        cost_estimate=pl.CostEstimate(flops=2 * 9 * TOK * D * fw, bytes_accessed=35 * 2**20, transcendentals=TOK * fw),
        name="mlp",
    )(second, secondT, gout, goutT, eb, mlp, sec, W)


def attn_bwd_kernel(length, heads, gmid, gmidT, firstT, qkv, att, lse, acc_in, W, G, gqb, gvb, acc, ga_s, d_s, dk_s, dv_s):
    cw = heads * HD

    @pl.loop(0, TOK // RT)
    def _(i):
        rows = pl.ds(pl.multiple_of(i * RT, RT), RT)
        g = nn(gmid[rows, :], W[:, 3 * cw:]).astype(BF)
        for h in range(heads):
            ga_s[h, rows, :] = g[:, h * HD:(h + 1) * HD]

    gqb[...] = jnp.zeros_like(gqb)
    dk_s[...] = jnp.zeros_like(dk_s)
    dv_s[...] = jnp.zeros_like(dv_s)

    @pl.loop(0, TOK // RT)
    def _(i):
        rows = pl.ds(pl.multiple_of(i * RT, RT), RT)
        cid = lax.broadcasted_iota(jnp.int32, (1, TOK), 1)
        dqs = []
        for h in range(heads):
            q, k, v, g = qkv[h, rows, :], qkv[heads + h], qkv[2 * heads + h], ga_s[h, rows, :]
            s = nt(q, k)
            p = jnp.exp2(s * (SC * LOG2E) - lse[rows, h:h + 1])
            p = jnp.where(cid < length, p, 0.0)
            dp = nt(g, v)
            dd = jnp.sum(g.astype(F32) * att[rows, h * HD:(h + 1) * HD].astype(F32), axis=1, keepdims=True)
            ds = (p * (dp - dd)).astype(BF)
            dqs.append(nn(ds, k) * SC)
            dk_s[h] += tn(ds, q)
            dv_s[h] += tn(p.astype(BF), g)
        dq = jnp.concatenate(dqs, axis=1)
        gqb[...] += jnp.sum(dq, axis=0, keepdims=True)
        d_s[rows, :cw] = dq.astype(BF)

    dk = jnp.concatenate([dk_s[h] * SC for h in range(heads)], axis=1)
    d_s[:, cw:2 * cw] = dk.astype(BF)
    dv = jnp.concatenate([dv_s[h] for h in range(heads)], axis=1)
    gvb[...] = jnp.sum(dv, axis=0, keepdims=True)
    d_s[:, 2 * cw:] = dv.astype(BF)

    @pl.loop(0, TOK // RT)
    def _(i):
        rows = pl.ds(pl.multiple_of(i * RT, RT), RT)
        acc[rows, :] = acc_in[rows, :] + nt(d_s[rows, :], W[:, :3 * cw])

    def write(lo, hi):
        def put(place, v):
            G[place, lo:hi] = v.astype(BF)
        return put

    block_rows(firstT, d_s, None, write(0, 3 * cw))
    block_rows(gmidT, att, None, write(3 * cw, 4 * cw))


def attn_bwd(gmid, gmidT, firstT, W, qkv, att, lse, acc, length):
    D = gmid.shape[1]
    cw = W.shape[1] // 4
    heads = cw // HD
    return pl.pallas_call(
        functools.partial(attn_bwd_kernel, length, heads),
        out_shape=(shape((D, 4 * cw), BF), shape((1, cw), F32), shape((1, cw), F32), shape((TOK, D), F32)),
        in_specs=[VM] * 8,
        out_specs=(VM,) * 4,
        scratch_shapes=[pltpu.VMEM((heads, TOK, HD), BF), pltpu.VMEM((TOK, 3 * cw), BF), pltpu.VMEM((heads, TOK, HD), F32), pltpu.VMEM((heads, TOK, HD), F32)],
        compiler_params=pltpu.CompilerParams(vmem_limit_bytes=52 * 2**20),
        cost_estimate=pl.CostEstimate(flops=2 * TOK * (D * cw * 8 + heads * 5 * TOK * HD * 6), bytes_accessed=30 * 2**20, transcendentals=heads * TOK * TOK),
        name="attn_bwd",
    )(gmid, gmidT, firstT, qkv, att, lse, acc, W)


def normalize(values):
    centre = jnp.mean(values, axis=-1, keepdims=True)
    centred = values - centre
    spread = jnp.mean(centred * centred, axis=-1, keepdims=True)
    inverse = lax.rsqrt(spread + norm_eps)
    return centred * inverse, inverse


def norm_back(grad_norm, normed, inverse, gain):
    scaled = grad_norm * gain
    first_mean = jnp.mean(scaled, axis=-1, keepdims=True)
    second_mean = jnp.mean(scaled * normed, axis=-1, keepdims=True)
    grad_input = inverse * (scaled - first_mean - normed * second_mean)
    return grad_input, jnp.sum(grad_norm * normed, axis=0), jnp.sum(grad_norm, axis=0)


def slot_table(d, groups):
    z = lax.axis_index("tensor")
    middle = 1 + d % 2
    return jnp.where(z == 0, 0, jnp.where(z == groups - 1, 1, 2)), (z == 0) | (z == groups - 1) | (z == middle)


HOPS = {
    "u1": (1, ((0, None),)), "u2": (3, ((1, None),)), "u3": (1, ((2, None),)),
    "w1": (1, ((3, None),)), "w2": (3, ((2, None),)), "w3": (1, ((1, None),)),
    "v1": (3, ((1, 0), (2, 1))), "v2": (1, ((2, 0), (1, 1))), "v3": (1, ((1, 0), (2, 1))),
}
HOP_FROM = {"u1": "me", "u2": "u1", "u3": "u2", "w1": "me", "w2": "w1", "w3": "w2", "v1": "me", "v2": "v1", "v3": "me"}
NAMES = ("u1", "w1", "v1", "v3"), ("u2", "w2", "v2"), ("u3", "w3")
BEGIN = {"u": 0, "w": 1, "v": 2}


class Wires:
    def __init__(self, s_sem, r_sem):
        self.s, self.r, self.n = s_sem, r_sem, 0
        self.d, self.z = lax.axis_index("dp"), lax.axis_index("tensor")

    def local(self, src, dst, used):
        i = self.n
        self.n += 1
        make = lambda: pltpu.make_async_copy(src, dst, self.s.at[i])
        return (lambda: pl.when(used)(lambda: make().start())), (lambda: pl.when(used)(lambda: make().wait()))

    def swap(self, src, dst, dp=0, z=0, sends=None):
        i = self.n
        self.n += 1
        make = lambda: pltpu.make_async_remote_copy(src_ref=src, dst_ref=dst, send_sem=self.s.at[i], recv_sem=self.r.at[i], device_id=(self.d ^ dp, self.z ^ z), device_id_type=MESH)
        if sends is None:
            return (lambda: make().start()), (lambda: make().wait())

        def any_of(z_here):
            hit = None
            for zz, cc in sends:
                this = z_here == zz
                if cc is not None:
                    this = this & (self.d % 2 == cc)
                hit = this if hit is None else hit | this
            return hit

        def start():
            pl.when(any_of(self.z))(lambda: make().start())

        def wait():
            pl.when(any_of(self.z))(lambda: make().wait_send())
            pl.when(any_of(self.z ^ z))(lambda: make().wait_recv())

        return start, wait


def greet(d, z, masks):
    sem = pltpu.get_barrier_semaphore()
    for dp, t in masks:
        pl.semaphore_signal(sem, inc=1, device_id=(d ^ dp, z ^ t), device_id_type=MESH)
    pl.semaphore_wait(sem, len(masks))


class Summing:
    def __init__(self, wires, H, land, zr, k):
        self.H, self.k = H, k
        self.rows = r = H.shape[0] // 4
        self.one, self.two = one, two = cut_rows(r)
        ax, by = land.at[pl.ds(0, 2 * one), :], land.at[pl.ds(2 * one, 2 * two), :]
        ay, bx = land.at[pl.ds(2 * r, one), :], land.at[pl.ds(2 * r + one, two), :]
        self.land = land
        h = lambda lo, n: H.at[pl.ds(lo, n), :]
        at = lambda ref, lo, n: ref.at[pl.ds(lo, n), :]
        self.c1 = [wires.swap(h(r, one), at(land, 0, one), dp=2), wires.swap(h(3 * r, one), at(land, one, one), dp=2),
                   wires.swap(h(2 * r + one, two), at(land, 2 * one, two), dp=4), wires.swap(h(3 * r + one, two), at(land, 2 * one + two, two), dp=4)]
        self.c2 = [wires.swap(h(2 * r, one), ay, dp=4), wires.swap(h(r + one, two), bx, dp=2)]
        self.c3 = [wires.swap(h(0, r), zr, z=k)] if k else []

    def add(self, lo, n, *froms):
        total = self.H[lo:lo + n, :].astype(F32)
        for f in froms:
            total = total + self.land[f:f + n, :].astype(F32)
        self.H[lo:lo + n, :] = total.astype(BF)

    def step1(self):
        for s, _ in self.c1:
            s()

    def step2(self):
        r, one, two = self.rows, self.one, self.two
        for _, w in self.c1:
            w()
        self.add(2 * r, one, one)
        self.add(r + one, two, 2 * one + two)
        for s, _ in self.c2:
            s()

    def step3(self):
        r, one, two = self.rows, self.one, self.two
        for _, w in self.c2:
            w()
        self.add(0, one, 0, 2 * r)
        self.add(one, two, 2 * one, 2 * r + one)
        for s, _ in self.c3:
            s()

    def step4(self):
        for _, w in self.c3:
            w()


class Sharing:
    def __init__(self, wires, mine, O, chunks, base=0):
        self.stages = []
        stride = O.shape[0] // 3
        for lo, n in chunks:
            here = []
            for names in NAMES:
                row = []
                for name in names:
                    mask, sends = HOPS[name]
                    place = O.at[pl.ds(BEGIN[name[0]] * stride + lo - base, n), :]
                    row.append(wires.swap(mine.at[pl.ds(lo, n), :] if HOP_FROM[name] == "me" else place, place, z=mask, sends=sends))
                here.append(row)
            self.stages.append(here)

    def start(self, chunk, stage):
        for s, _ in self.stages[chunk][stage]:
            s()

    def wait(self, chunk, stage):
        for _, w in self.stages[chunk][stage]:
            w()

    def on(self, chunk, stage):
        self.wait(chunk, stage - 1)
        self.start(chunk, stage)


OUT_CHUNKS = ((256, 256), (512, 224))
IN_CHUNKS = ((0, 128), (128, 128), (256, 128), (384, 128), (512, 128), (640, 96))
MASKS = [(1, 0), (2, 0), (4, 0), (0, 1), (0, 2), (0, 3)]
COPIES = 180


def back_kernel(length, heads, gain1, gain2, live, geb, tops, gout, midway, sec, firstT, x, mine, whole0, h2, h3, *rest):
    Ws, qkvs, atts, lses, rest = rest[:4], rest[4:8], rest[8:12], rest[12:16], rest[16:]
    (O_out, O_in, sum_a, sum_m, vec, g_s, gm_s, acc, gT, fT, x_s, W_s, Wo, qkv_s, att_s, lse_s, ga_s, d_s, dk_s, dv_s, out_s,
     Ha, La, Hm, Lm, za, zm, vr, w0_s, l_sem, s_sem, r_sem) = rest
    cw = heads * HD
    D = g_s.shape[1]
    wires = Wires(s_sem, r_sem)
    d, z = wires.d, wires.z
    loads = {}
    order = [3, 2, 1, 0]
    names = iter(range(100))

    def load(key, src, dst):
        loads[key] = pltpu.make_async_copy(src, dst, l_sem.at[next(names)])

    load("midway", midway, acc)
    load("sec", sec, gm_s)
    load("gout", gout, g_s)
    load("firstT", firstT, fT)
    load("x", x, x_s)
    load("h2", h2, Hm.at[0])
    load("h3", h3, Hm.at[1])
    load("w0", whole0, w0_s)
    for i, k in enumerate(order):
        b = i % 2
        load(f"W{i}", Ws[k], W_s.at[b])
        load(f"qkv{i}", qkvs[k], qkv_s.at[b])
        load(f"att{i}", atts[k], att_s.at[b])
        load(f"lse{i}", lses[k], lse_s.at[b])
    for key in ("midway", "sec", "gout", "h2", "h3", "w0", "firstT", "W0", "qkv0", "att0", "lse0", "x"):
        loads[key].start()
    slot = jnp.where(z == 0, 0, jnp.where(z == 3, 1, 2))
    own_place = pl.ds(pl.multiple_of(slot * TOK, 256), TOK)
    out_rows = O_out.shape[0] // 3
    out_base = TOK - out_rows
    out_place = pl.ds(pl.multiple_of(slot * out_rows, 256), out_rows)
    used = (z == 0) | (z == 3) | (z == 1 + d % 2)
    own_out, own_in = wires.local(mine.at[pl.ds(out_base, out_rows), :], O_out.at[out_place, :], used), wires.local(g_s, O_in.at[own_place, :], used)
    share_out = Sharing(wires, mine, O_out, OUT_CHUNKS, out_base)
    share_in = Sharing(wires, g_s, O_in, IN_CHUNKS)
    sums = {"m2": Summing(wires, Hm.at[0], Lm.at[0], zm.at[0], 2), "m3": Summing(wires, Hm.at[1], Lm.at[1], zm.at[1], 3)}
    for k in range(4):
        sums[f"b{k}"] = Summing(wires, Ha.at[k], La.at[k], za.at[max(k - 1, 0)], k)
    exchange = {k: wires.swap(out_s, Ha.at[k], dp=1) for k in range(4)}
    spread = [wires.swap(vec, vr.at[i], dp=dp, z=t) for i, (dp, t) in enumerate(((1, 0), (2, 0), (4, 0), (0, 1), (0, 2)))]
    greet(d, z, MASKS)

    todo = {
        -3: [lambda: share_out.start(0, 0), own_out[0]],
        -2: [lambda: loads["h2"].wait(), sums["m2"].step1],
        0: [lambda: loads["h3"].wait(), lambda: loads["w0"].wait()],
        2: [lambda: share_out.on(0, 1), lambda: share_out.start(1, 0)],
        3: [sums["m2"].step2, sums["m3"].step1],
        5: [sums["m2"].step3],
        8: [sums["b3"].step1, lambda: share_out.on(0, 2), lambda: share_out.on(1, 1)],
        12: [sums["m3"].step2],
        13: [sums["b3"].step2],
        15: [sums["m3"].step3, sums["b3"].step3],
        18: [sums["b2"].step1, lambda: share_out.on(1, 2)],
        23: [sums["b2"].step2],
        25: [sums["b2"].step3],
        28: [sums["b1"].step1],
        33: [sums["b1"].step2],
        35: [sums["b1"].step3],
        38: [sums["b0"].step1],
    }

    def tick(t):
        for action in todo.get(t, ()):
            action()

    vec[...] = jnp.zeros_like(vec)
    for key in ("midway", "sec", "gout"):
        loads[key].wait()

    def total_of(row, value):
        vec[row:row + 1, :D] += jnp.sum(value, axis=0, keepdims=True)

    def put_row(where, lo, value):
        n = value.shape[1]
        hit = lax.broadcasted_iota(jnp.int32, (8, n), 0) == where
        vec[0:8, lo:lo + n] += jnp.where(hit, jnp.broadcast_to(value, (8, n)), 0.0)

    @pl.loop(0, TOK // RT)
    def _(i):
        for t in range(3):
            pl.when(i == t)(functools.partial(tick, t - 3))
        rows = pl.ds(pl.multiple_of(i * RT, RT), RT)
        normed, inverse = normalize(acc[rows, :])
        e = gm_s[rows, :]
        go = g_s[rows, :].astype(F32)
        scaled = e * gain2[...]
        mean1 = jnp.mean(scaled, axis=-1, keepdims=True)
        mean2 = jnp.mean(scaled * normed, axis=-1, keepdims=True)
        gm = go + inverse * (scaled - mean1 - normed * mean2)
        total_of(4, gm)
        total_of(5, go)
        total_of(8, e * normed)
        total_of(9, e)
        gm_s[rows, :] = gm
        g_s[rows, :] = gm.astype(BF)
        gT[:, rows] = gm.T.astype(BF)

    loads["firstT"].wait()
    acc[...] = jnp.zeros_like(acc)
    for i, k in enumerate(order):
        base, b = 10 * i, i % 2
        W, qkv, att, lse, H = W_s.at[b], qkv_s.at[b], att_s.at[b], lse_s.at[b], Ha.at[k]
        for key in ("W", "qkv", "att", "lse"):
            loads[f"{key}{i}"].wait()
        if i < 3:
            for key in ("W", "qkv", "att", "lse"):
                loads[f"{key}{i + 1}"].start()
        tick(base)
        Wo[...] = W[:, 3 * cw:]

        @pl.loop(0, TOK // RT)
        def _(t):
            rows = pl.ds(pl.multiple_of(t * RT, RT), RT)
            g = nn(g_s[rows, :], Wo[...]).astype(BF)
            for h in range(heads):
                ga_s[h, rows, :] = g[:, h * HD:(h + 1) * HD]

        tick(base + 1)
        dk_s[...] = jnp.zeros_like(dk_s)
        dv_s[...] = jnp.zeros_like(dv_s)
        place = z ^ k

        @pl.loop(0, TOK // RT)
        def _(t):
            for n in range(3):
                pl.when(t == n)(functools.partial(tick, base + 2 + n))
            rows = pl.ds(pl.multiple_of(t * RT, RT), RT)
            cid = lax.broadcasted_iota(jnp.int32, (1, TOK), 1)
            dqs = []
            for h in range(heads):
                q, kk, v, g = qkv[h, rows, :], qkv[heads + h], qkv[2 * heads + h], ga_s[h, rows, :]
                s = nt(q, kk)
                p = jnp.exp2(s * (SC * LOG2E) - lse[rows, h:h + 1])
                p = jnp.where(cid < length, p, 0.0)
                dp = nt(g, v)
                dd = jnp.sum(g.astype(F32) * att[rows, h * HD:(h + 1) * HD].astype(F32), axis=1, keepdims=True)
                ds = (p * (dp - dd)).astype(BF)
                dqs.append(nn(ds, kk) * SC)
                dk_s[h] += tn(ds, q)
                dv_s[h] += tn(p.astype(BF), g)
            dq = jnp.concatenate(dqs, axis=1)
            put_row(place, 0, jnp.sum(dq, axis=0, keepdims=True))
            d_s[rows, :cw] = dq.astype(BF)

        d_s[:, cw:2 * cw] = jnp.concatenate([dk_s[h] * SC for h in range(heads)], axis=1).astype(BF)
        dv = jnp.concatenate([dv_s[h] for h in range(heads)], axis=1)
        put_row(place, 384, jnp.sum(dv, axis=0, keepdims=True))
        d_s[:, 2 * cw:] = dv.astype(BF)
        put_row(place, 768, geb[k])
        put_row(place, 1920, tops[k])
        tick(base + 5)

        def write(dst, lo, hi, add):
            def put(where, val):
                if add:
                    val = val + dst[where, lo:hi].astype(F32)
                dst[where, lo:hi] = val.astype(BF)
            return put

        block_rows(fT, d_s, 0, write(out_s, 0, 3 * cw, False))
        block_rows(gT, att, 0, write(out_s, 3 * cw, 4 * cw, False))
        exchange[k][0]()
        tick(base + 6)

        @pl.loop(0, TOK // RT)
        def _(t):
            rows = pl.ds(pl.multiple_of(t * RT, RT), RT)
            acc[rows, :] += nt(d_s[rows, :], W[:, :3 * cw])

        tick(base + 7)
        exchange[k][1]()
        block_rows(fT, d_s, 1, write(H, 0, 3 * cw, True))
        block_rows(gT, att, 1, write(H, 3 * cw, 4 * cw, True))
        tick(base + 8)

    loads["x"].wait()

    @pl.loop(0, TOK // RT)
    def _(i):
        rows = pl.ds(pl.multiple_of(i * RT, RT), RT)
        normed, inverse = normalize(x_s[rows, :].astype(F32))
        e = acc[rows, :]
        scaled = e * gain1[...]
        mean1 = jnp.mean(scaled, axis=-1, keepdims=True)
        mean2 = jnp.mean(scaled * normed, axis=-1, keepdims=True)
        total_of(6, e * normed)
        total_of(7, e)
        g_s[rows, :] = ((gm_s[rows, :] + inverse * (scaled - mean1 - normed * mean2)) * live[...]).astype(BF)
        for t in range(3):
            @pl.when(i == t)
            def _():
                share_in.start(2 * t, 0)
                share_in.start(2 * t + 1, 0)

    own_in[0]()
    after = {0: [spread[0][0], sums["b0"].step2], 1: [], 2: [sums["b0"].step3]}
    row = lax.broadcasted_iota(jnp.int32, vec.shape, 1)

    def fold(i):
        spread[i][1]()
        a, c = vec[...], vr[i]
        vec[...] = jnp.where(row < 1920, a + c, jnp.maximum(a, c))
        if i < 4:
            spread[i + 1][0]()

    n = len(IN_CHUNKS)
    for t in range(n + 2):
        if t < n:
            share_in.on(t, 1)
        for action in after.get(t, ()):
            action()
        if 1 <= t <= n:
            share_in.on(t - 1, 2)
        if 1 <= t <= 5:
            fold(t - 1)
    for c in range(len(OUT_CHUNKS)):
        share_out.wait(c, 2)
    own_out[1]()
    own_in[1]()
    for s in ("m2", "m3", "b3", "b2", "b1"):
        sums[s].step4()
    r = sum_a.shape[0]
    sum_a[...] = Ha[0, :r, :].astype(F32) + za[0].astype(F32) + za[1].astype(F32) + za[2].astype(F32)
    sum_m[...] = w0_s[...] + zm[0].astype(F32) + zm[1].astype(F32)
    for c in range(n):
        share_in.wait(c, 2)


def back(number, gain1, gain2, live, geb, tops, gout, midway, sec, firstT, x, mine, whole0, h2, h3, qkvs, atts, lses, Ws, length):
    D = gout.shape[1]
    cw = Ws[0].shape[1] // 4
    cm = h2.shape[1]
    heads = cw // HD
    r = D // 8
    vm = pltpu.VMEM
    dma = pltpu.SemaphoreType.DMA
    return pl.pallas_call(
        functools.partial(back_kernel, length, heads),
        out_shape=(shape((3 * (TOK - OUT_CHUNKS[0][0]), D), BF), shape((3 * TOK, D), BF), shape((r, 4 * cw), F32), shape((r, cm), F32), shape((16, 2048), F32)),
        in_specs=[VM] * 5 + [HB] * 25,
        out_specs=(HB, HB, VM, VM, VM),
        scratch_shapes=[vm((TOK, D), BF), vm((TOK, D), F32), vm((TOK, D), F32), vm((D, TOK), BF), vm((D, TOK), BF), vm((TOK, D), BF),
                        vm((2, D, 4 * cw), BF), vm((D, cw), BF), vm((2, 3 * heads, TOK, HD), BF), vm((2, TOK, cw), BF), vm((2, TOK, 128), F32),
                        vm((heads, TOK, HD), BF), vm((TOK, 3 * cw), BF), vm((heads, TOK, HD), F32), vm((heads, TOK, HD), F32), vm((4 * r, 4 * cw), BF),
                        vm((4, 4 * r, 4 * cw), BF), vm((4, 3 * r, 4 * cw), BF), vm((2, 4 * r, cm), BF), vm((2, 3 * r, cm), BF),
                        vm((3, r, 4 * cw), BF), vm((2, r, cm), BF), vm((5, 16, 2048), F32), vm((r, cm), F32),
                        dma((32,)), dma((COPIES,)), dma((COPIES,))],
        compiler_params=pltpu.CompilerParams(vmem_limit_bytes=63 * 2**20, collective_id=number, has_side_effects=True),
        cost_estimate=pl.CostEstimate(flops=4 * 2 * TOK * (D * cw * 8 + heads * 5 * TOK * HD * 6), bytes_accessed=60 * 2**20, transcendentals=4 * heads * TOK * TOK),
        name="back",
    )(gain1, gain2, live, geb, tops, gout, midway, sec, firstT, x, mine, whole0, h2, h3, *Ws, *qkvs, *atts, *lses)


class Spreading:
    def __init__(self, wires, piece, W):
        rows = W.shape[0] // 8
        one, two = cut_rows(rows)
        d = wires.d
        at = lambda mask, lo=0, n=rows: W.at[pl.ds(pl.multiple_of((d ^ mask) * rows + lo, 16), n), :]
        self.own = wires.local(piece, at(0), d >= 0)
        self.s0 = [wires.swap(piece, at(0), dp=m) for m in (2, 4, 1)]
        self.s1 = [wires.swap(at(2, 0, one), at(2, 0, one), dp=4), wires.swap(at(4, one, two), at(4, one, two), dp=2)]
        self.s1c = [wires.swap(at(m), at(m), dp=1) for m in (2, 4)]
        self.s2 = wires.swap(at(6), at(6), dp=1)

    def step0(self):
        self.own[0]()
        for s, _ in self.s0:
            s()

    def step1(self):
        for _, w in self.s0:
            w()
        for s, _ in self.s1 + self.s1c:
            s()

    def step2(self):
        for _, w in self.s1:
            w()
        self.s2[0]()

    def finish(self):
        for _, w in self.s1c + [self.own, self.s2]:
            w()


class Moves:
    def __init__(self, sem):
        self.sem, self.made = sem, {}

    def add(self, key, src, dst):
        self.made[key] = pltpu.make_async_copy(src, dst, self.sem.at[len(self.made)])

    def start(self, *keys):
        for k in keys:
            self.made[k].start()

    def wait(self, *keys):
        for k in keys:
            self.made[k].wait()


def front_kernel(length, heads, gain1, shift1, gain2, shift2, out_b, bias_own, x, qw, kw, vw, ow, ew, st, te, *rest):
    (qkv0, qkv1, qkv2, qkv3, att0, att1, att2, att3, lse0, lse1, lse2, lse3, firstT, second, secondT, midway, Wa0, Wa1, Wa2, Wa3, Wm0, Wm1, Zm2,
     tops, bias_all, x_s, raw, ow_s, first_s, T_s, second_s, acc, W, Wm, Za, Zm1, qkv_s, att_s, lse_s, bias, l_sem, s_sem, r_sem) = rest
    cw = heads * HD
    D = x_s.shape[1]
    cut = (Wm.shape[1] - 128) // 2
    wires, moves = Wires(s_sem, r_sem), Moves(l_sem)
    d, z = wires.d, wires.z
    rows = D // 8
    own_rows = pl.ds(pl.multiple_of(d * rows, 16), rows)
    for i, ref in enumerate((qw, kw, vw)):
        moves.add(f"w{i}", ref, raw.at[i])
    moves.add("ow", ow, ow_s.at[pl.ds(0, cw), :])
    moves.add("x", x, x_s)
    moves.add("m0", ew.at[:, pl.ds(0, cut)], Wm.at[:, pl.ds(0, cut)])
    moves.add("m1", st.at[:, pl.ds(0, cut)], Wm.at[:, pl.ds(cut, cut)])
    moves.add("m2", te, Wm.at[:, pl.ds(2 * cut, 128)])
    moves.add("oW0", W.at[0], Wa0)
    moves.add("oWm", Wm, Wm0)
    for k, (a, b, c) in enumerate(((qkv0, att0, lse0), (qkv1, att1, lse1), (qkv2, att2, lse2), (qkv3, att3, lse3))):
        moves.add(f"qkv{k}", qkv_s.at[k], a)
        moves.add(f"att{k}", att_s.at[k], b)
        moves.add(f"lse{k}", lse_s.at[k], c)
    for k, ref in enumerate((Wa1, Wa2, Wa3)):
        moves.add(f"oW{k + 1}", W.at[k + 1], ref)
    moves.add("firstT", T_s, firstT)
    moves.add("second", second_s, second)
    moves.add("secondT", T_s, secondT)
    moves.add("midway", acc, midway)
    moves.start("w0", "w1", "w2", "ow", "x", "m0", "m1", "m2")

    zb = [wires.swap(bias.at[0], bias.at[k], z=k) for k in (1, 2, 3)]
    za = [wires.swap(W.at[0, own_rows, :], Za.at[0], z=1), wires.swap(W.at[0, own_rows, :], Za.at[1], z=2), wires.swap(Za.at[1], Za.at[2], z=1)]
    zm = [wires.swap(Wm.at[own_rows, :], Zm1, z=1), wires.swap(Wm.at[own_rows, :], Zm2, z=2)]
    ga = {k: Spreading(wires, Za.at[k - 1], W.at[k]) for k in (1, 2, 3)}
    gm = Spreading(wires, Zm1, Wm1)
    greet(d, z, MASKS)
    bias[0] = bias_own[...]
    for s, _ in zb:
        s()
    moves.wait("w0", "w1", "w2", "ow")

    @pl.loop(0, D // 384)
    def _(i):
        part = pl.ds(pl.multiple_of(i * 384, 128), 384)
        turned = ow_s[:, part].astype(F32).T[:, :cw].astype(BF)
        W[0, part, :] = jnp.concatenate([raw[0, part, :], raw[1, part, :], raw[2, part, :], turned], axis=1)

    za[0][0]()
    za[1][0]()
    moves.start("oW0")
    moves.wait("m0", "m1", "m2")
    moves.start("oWm")
    moves.wait("x")

    @pl.loop(0, TOK // RT)
    def _(i):
        part = pl.ds(pl.multiple_of(i * RT, RT), RT)
        xt = x_s[part, :].astype(F32)
        normed, _ = normalize(xt)
        f = normed * gain1[...] + shift1[...]
        first_s[part, :] = f.astype(BF)
        T_s[:, part] = f.T.astype(BF)
        acc[part, :] = xt + out_b[...]

    moves.start("firstT")
    for _, w in zb:
        w()
    bias_all[...] = bias[...]

    def z_a3():
        za[1][1]()
        za[2][0]()

    todo = {
        0: [za[0][1], ga[1].step0, zm[0][0]],
        2: [],
        3: [ga[1].step1],
        4: [z_a3, ga[2].step0, ga[1].step2],
        10: [],
        11: [ga[2].step1, zm[1][0]],
        12: [za[2][1], ga[3].step0],
        13: [ga[2].step2],
        20: [zm[0][1], gm.step0],
        21: [ga[3].step1],
        23: [ga[3].step2],
        31: [gm.step1],
        34: [gm.step2],
    }

    def tick(t):
        for action in todo.get(t, ()):
            action()

    for k in range(4):
        base = 10 * k
        Wk, qkv, att, lse = W.at[k], qkv_s.at[k], att_s.at[k], lse_s.at[k]
        if k:
            ga[k].finish()
            moves.start(f"oW{k}")
        tick(base)
        qb, vb = bias[k, 0:1, :cw], bias[k, 0:1, 384:384 + cw]

        @pl.loop(0, TOK // RT)
        def _(i):
            part = pl.ds(pl.multiple_of(i * RT, RT), RT)
            t = nn(first_s[part, :], Wk[:, :3 * cw])
            q = (t[:, :cw] + qb).astype(BF)
            kk = t[:, cw:2 * cw].astype(BF)
            v = (t[:, 2 * cw:] + vb).astype(BF)
            for h in range(heads):
                qkv[h, part, :] = q[:, h * HD:(h + 1) * HD]
                qkv[heads + h, part, :] = kk[:, h * HD:(h + 1) * HD]
                qkv[2 * heads + h, part, :] = v[:, h * HD:(h + 1) * HD]

        tick(base + 1)
        moves.start(f"qkv{k}")
        tops[k] = jnp.full(tops.shape[1:], -1e30, F32)

        @pl.loop(0, TOK // RT)
        def _(i):
            for n in range(3):
                pl.when(i == n)(functools.partial(tick, base + 2 + n))
            part = pl.ds(pl.multiple_of(i * RT, RT), RT)
            rid = lax.broadcasted_iota(jnp.int32, (RT, 1), 0) + i * RT
            cid = lax.broadcasted_iota(jnp.int32, (1, TOK), 1)
            res = []
            for h in range(heads):
                s = nt(qkv[h, part, :], qkv[heads + h])
                s = jnp.where(cid < length, s, -1e30)
                m = jnp.max(s, axis=1, keepdims=True)
                e = jnp.exp2((s - m) * (SC * LOG2E))
                l = jnp.sum(e, axis=1, keepdims=True)
                o = nn(e.astype(BF), qkv[2 * heads + h]) * (1.0 / l)
                res.append(o.astype(BF))
                lse[part, h:h + 1] = m * (SC * LOG2E) + jnp.log2(l)
                tops[k, h:h + 1, :] = jnp.maximum(tops[k, h:h + 1, :], jnp.max(jnp.where(rid < length, m, -1e30)) * SC)
            a = jnp.concatenate(res, axis=1)
            att[part, :] = a
            acc[part, :] += nt(a, Wk[:, 3 * cw:])

        moves.start(f"att{k}", f"lse{k}")

    moves.start("midway")
    moves.wait("firstT")

    @pl.loop(0, TOK // RT)
    def _(i):
        part = pl.ds(pl.multiple_of(i * RT, RT), RT)
        normed, _ = normalize(acc[part, :])
        f = normed * gain2[...] + shift2[...]
        second_s[part, :] = f.astype(BF)
        T_s[:, part] = f.T.astype(BF)

    moves.start("second", "secondT")
    gm.finish()
    zm[1][1]()
    for k in range(4):
        moves.wait(f"qkv{k}", f"att{k}", f"lse{k}", f"oW{k}")
    moves.wait("oWm", "second", "secondT", "midway")


def front(number, gain1, shift1, gain2, shift2, out_b, bias_own, x, qw, kw, vw, ow, ew, st, te, length):
    D, cw = qw.shape
    heads = cw // HD
    cut = ew.shape[1] // 128 * 128
    cm = 2 * cut + 128
    r = D // 8
    vm = pltpu.VMEM
    dma = pltpu.SemaphoreType.DMA
    four = lambda s: (s,) * 4
    got = pl.pallas_call(
        functools.partial(front_kernel, length, heads),
        out_shape=(*four(shape((3 * heads, TOK, HD), BF)), *four(shape((TOK, cw), BF)), *four(shape((TOK, 128), F32)),
                   shape((D, TOK), BF), shape((TOK, D), BF), shape((D, TOK), BF), shape((TOK, D), F32), *four(shape((D, 4 * cw), BF)),
                   shape((D, cm), BF), shape((D, cm), BF), shape((r, cm), BF), shape((4, heads, 128), F32), shape((4, 8, 2048), F32)),
        in_specs=[VM] * 6 + [HB] * 8,
        out_specs=(HB,) * 23 + (VM,) * 2,
        scratch_shapes=[vm((TOK, D), BF), vm((3, D, cw), BF), vm((384, D), BF), vm((TOK, D), BF), vm((D, TOK), BF), vm((TOK, D), BF), vm((TOK, D), F32),
                        vm((4, D, 4 * cw), BF), vm((D, cm), BF), vm((3, r, 4 * cw), BF), vm((r, cm), BF), vm((4, 3 * heads, TOK, HD), BF),
                        vm((4, TOK, cw), BF), vm((4, TOK, 128), F32), vm((4, 8, 2048), F32), dma((32,)), dma((64,)), dma((64,))],
        compiler_params=pltpu.CompilerParams(vmem_limit_bytes=62 * 2**20, collective_id=number, has_side_effects=True),
        cost_estimate=pl.CostEstimate(flops=4 * 2 * TOK * (D * cw * 4 + heads * 2 * TOK * HD * 6), bytes_accessed=60 * 2**20, transcendentals=4 * heads * TOK * TOK),
        name="front",
    )(gain1, shift1, gain2, shift2, out_b, bias_own, x, qw, kw, vw, ow, ew, st, te)
    return got[:4], got[4:8], got[8:12], got[12:16], got[16:20], got[20:23], got[23], got[24]


def middle_kernel(fw, live, shrink_b, bias_all, second, secondT, gout, goutT, midway, Wm0, Wm1, Zm2, *rest):
    (mine, sec, O0, H2, H3, geb, part_sum, Wg2, Wg3, Zm3, second_s, secondT_s, gout_s, goutT_s, mlp, sec_s, mine_s, tail_s, E, ST, act_s, slope_s, gpre_s, out_s,
     Hm, Lm, zr, l_sem, s_sem, r_sem) = rest
    D = second_s.shape[1]
    cut = fw // 128 * 128
    tail = fw - cut
    r = D // 8
    wires, moves = Wires(s_sem, r_sem), Moves(l_sem)
    d, z = wires.d, wires.z
    Ws = (Wm0, Wm1, Wg2, Wg3)
    for key, a, b in (("second", second, second_s), ("secondT", secondT, secondT_s), ("gout", gout, gout_s), ("goutT", goutT, goutT_s), ("midway", midway, mlp)):
        moves.add(key, a, b)
    for k in range(4):
        moves.add(f"E{k}", Ws[k].at[:, pl.ds(0, cut)], E.at[k % 2, :, pl.ds(0, cut)])
        moves.add(f"S{k}", Ws[k].at[:, pl.ds(cut, cut)], ST.at[k % 2, :, pl.ds(0, cut)])
        moves.add(f"T{k}", Ws[k].at[:, pl.ds(2 * cut, 128)], tail_s.at[k % 2])
    moves.add("mine", mine_s, mine)
    moves.add("sec", sec_s, sec)
    moves.add("h2", Hm.at[2], H2)
    moves.add("h3", Hm.at[3], H3)
    slot = jnp.where(z == 0, 0, jnp.where(z == 3, 1, 2))
    used = (z == 0) | (z == 3) | (z == 1 + d % 2)
    n0 = O0.shape[0] // 3
    own_out = wires.local(mine_s.at[pl.ds(0, n0), :], O0.at[pl.ds(pl.multiple_of(slot * n0, 256), n0), :], used)
    share = Sharing(wires, mine_s, O0, ((0, n0),))
    z3 = wires.swap(Zm2, Zm3, z=1)
    g2, g3 = Spreading(wires, Zm2, Wg2), Spreading(wires, Zm3, Wg3)
    exchange = [wires.swap(out_s, Hm.at[k], dp=1) for k in range(4)]
    sums = [Summing(wires, Hm.at[k], Lm.at[k], zr, k) for k in (0, 1)]
    moves.start("second", "E0", "S0", "T0", "midway", "gout", "goutT", "secondT")
    greet(d, z, MASKS)
    z3[0]()
    g2.step0()
    sec_s[...] = jnp.zeros_like(sec_s)
    geb[...] = jnp.zeros_like(geb)
    moves.wait("second", "midway")

    def forward(k, tick):
        b = k % 2
        moves.wait(f"E{k}", f"S{k}", f"T{k}")
        lane = lax.broadcasted_iota(jnp.int32, (D, 128), 1)
        last = tail_s[b]
        E[b, :, cut:] = jnp.where(lane < tail, last, jnp.zeros_like(last))
        moved = jnp.concatenate([last[:, tail:2 * tail], jnp.zeros((D, 128 - tail), BF)], axis=1)
        ST[b, :, cut:] = moved
        eb = bias_all[k, 0:1, 768:768 + cut + 128]

        @pl.loop(0, TOK // RT)
        def _(i):
            tick(i)
            rows = pl.ds(pl.multiple_of(i * RT, RT), RT)
            act, slope = gelu_parts(nn(second_s[rows, :], E[b]) + eb)
            act_s[b, rows, :] = act.astype(BF)
            slope_s[b, rows, :] = slope.astype(BF)
            mlp[rows, :] += nt(act_s[b, rows, :], ST[b])

    def grads(k, half):
        b = k % 2
        for t in range(2):
            q = 4 * t + 1 - half
            lhs = lambda ref: jnp.concatenate([ref[pl.ds(pl.multiple_of((d ^ p) * r, 16), r), :] for p in (q, q + 2)], axis=0)
            place = pl.ds(t * 2 * r, 2 * r)
            ve, vs = nn(lhs(secondT_s), gpre_s[...]), nn(lhs(goutT_s), act_s[b])
            last = jnp.concatenate([ve[:, cut:fw], vs[:, cut:fw], jnp.zeros((2 * r, 128 - 2 * tail), F32)], axis=1)
            to = out_s if half == 0 else Hm.at[k]
            for lo, v in ((0, ve[:, :cut]), (cut, vs[:, :cut]), (2 * cut, last)):
                n = v.shape[1]
                if half:
                    v = v + to[place, lo:lo + n].astype(F32)
                to[place, lo:lo + n] = v.astype(BF)

    def backward(k, tick):
        b = k % 2

        @pl.loop(0, TOK // RT)
        def _(i):
            tick(i)
            rows = pl.ds(pl.multiple_of(i * RT, RT), RT)
            gp = nn(gout_s[rows, :], ST[b]) * slope_s[b, rows, :].astype(F32)
            geb[k] += jnp.sum(gp, axis=0, keepdims=True)
            gpre_s[rows, :] = gp.astype(BF)

        grads(k, 0)
        exchange[k][0]()

        @pl.loop(0, TOK // RT)
        def _(i):
            tick(i + 3)
            rows = pl.ds(pl.multiple_of(i * RT, RT), RT)
            sec_s[rows, :] += nt(gpre_s[rows, :], E[b])

        exchange[k][1]()
        grads(k, 1)

    def ticks(table):
        def tick(i):
            for n, actions in table.items():
                def run():
                    for a in actions:
                        a()
                pl.when(i == n)(run)
        return tick

    none = ticks({})
    moves.start("E1", "S1", "T1")
    forward(0, none)
    moves.wait("gout", "goutT", "secondT")
    backward(0, ticks({0: [g2.step1], 2: [z3[1], g3.step0], 3: [g2.step2]}))
    g2.finish()
    moves.start("E2", "S2", "T2")
    sums[0].step1()
    forward(1, ticks({2: [g3.step1]}))
    backward(1, ticks({0: [g3.step2], 2: [sums[0].step2], 4: [sums[0].step3]}))
    g3.finish()
    moves.start("E3", "S3", "T3")
    sums[1].step1()
    forward(2, none)
    forward(3, ticks({1: [sums[1].step2]}))

    @pl.loop(0, TOK // RT)
    def _(i):
        rows = pl.ds(pl.multiple_of(i * RT, RT), RT)
        mine_s[rows, :] = ((mlp[rows, :] + shrink_b[...]) * live[...]).astype(BF)
        pl.when(i == 0)(lambda: share.start(0, 0))

    own_out[0]()
    moves.start("mine")
    backward(2, ticks({0: [sums[1].step3], 4: [lambda: share.on(0, 1)]}))
    moves.start("h2")
    backward(3, ticks({2: [lambda: share.on(0, 2)]}))
    moves.start("h3", "sec")
    sums[1].step4()
    part_sum[...] = Hm[0, :r, :].astype(F32) + zr[...].astype(F32)
    share.wait(0, 2)
    own_out[1]()
    moves.wait("h2", "h3", "sec", "mine")


def middle(number, fw, live, shrink_b, bias_all, second, secondT, gout, goutT, midway, Wm0, Wm1, Zm2):
    D = second.shape[1]
    cut = fw // 128 * 128
    wide = cut + 128
    cm = 2 * cut + 128
    r = D // 8
    n0 = OUT_CHUNKS[0][0]
    vm = pltpu.VMEM
    dma = pltpu.SemaphoreType.DMA
    got = pl.pallas_call(
        functools.partial(middle_kernel, fw),
        out_shape=(shape((TOK, D), BF), shape((TOK, D), F32), shape((3 * n0, D), BF), shape((4 * r, cm), BF), shape((4 * r, cm), BF), shape((4, 1, wide), F32), shape((r, cm), F32),
                   shape((D, cm), BF), shape((D, cm), BF), shape((r, cm), BF)),
        in_specs=[VM] * 3 + [HB] * 8,
        out_specs=(HB,) * 5 + (VM,) * 2 + (HB,) * 3,
        scratch_shapes=[vm((TOK, D), BF), vm((D, TOK), BF), vm((TOK, D), BF), vm((D, TOK), BF), vm((TOK, D), F32), vm((TOK, D), F32), vm((TOK, D), BF), vm((2, D, 128), BF),
                        vm((2, D, wide), BF), vm((2, D, wide), BF), vm((2, TOK, wide), BF), vm((2, TOK, wide), BF), vm((TOK, wide), BF), vm((4 * r, cm), BF),
                        vm((4, 4 * r, cm), BF), vm((2, 3 * r, cm), BF), vm((r, cm), BF), dma((32,)), dma((72,)), dma((72,))],
        compiler_params=pltpu.CompilerParams(vmem_limit_bytes=63 * 2**20, collective_id=number, has_side_effects=True),
        cost_estimate=pl.CostEstimate(flops=4 * 2 * 9 * TOK * D * fw, bytes_accessed=60 * 2**20, transcendentals=4 * TOK * fw),
        name="middle",
    )(live, shrink_b, bias_all, second, secondT, gout, goutT, midway, Wm0, Wm1, Zm2)
    return got[:7]


class General:
    def __init__(self, groups, attn_own, mlp_own):
        self.groups = groups
        self.attn, self.mlp = self.spread(attn_own), self.spread(mlp_own)

    def vectors(self, own):
        every = lax.all_gather(own, "tensor")
        return [every[i] for i in range(self.groups)]

    def spread(self, own):
        d, count = lax.axis_index("dp"), lax.axis_size("dp")
        rows = own.shape[0] // count
        piece = lax.dynamic_slice_in_dim(own, d * rows, rows, 0)
        piece = lax.all_gather(piece, "tensor")
        whole = lax.all_gather(piece, "dp", axis=1, tiled=True)
        return [whole[i] for i in range(self.groups)]

    def reduce(self, parts):
        part = lax.psum_scatter(jnp.stack(parts), "dp", scatter_dimension=1, tiled=True)
        return lax.psum_scatter(part, "tensor", scatter_dimension=0, tiled=True)[0].astype(F32)

    def collect(self, grad_attn, grad_mlp):
        return self.reduce(grad_attn), self.reduce(grad_mlp)

    def by_index(self, items):
        return jnp.stack(items)

    def share(self, mine):
        every = lax.all_gather(mine, "tensor")
        middle = 1 + lax.axis_index("dp") % 2
        return jnp.stack([every[0], every[self.groups - 1], lax.dynamic_index_in_dim(every, middle, 0, keepdims=False)])


def shards(images, counts, cotangent, query_w, query_b, key_w, value_w, value_b, out_w, out_b, norm1_gain, norm1_shift,
           norm2_gain, norm2_shift, expand_w, expand_b, shrink_w, shrink_b):
    slots, length, width = images.shape
    groups = lax.axis_size("tensor")
    d, z = lax.axis_index("dp"), lax.axis_index("tensor")
    cw, fw = query_w.shape[1], expand_w.shape[1]
    heads = cw // HD
    cut = fw // 128 * 128
    slot, used = slot_table(d, groups)
    live = jnp.where(used & (slot < counts[0]), 1.0, 0.0).astype(F32)
    pad = lambda a: jnp.pad(a, ((0, TOK - length), (0, 0)))

    x_low = pad(lax.dynamic_index_in_dim(images, slot, 0, keepdims=False))
    gout = pad(lax.dynamic_index_in_dim(cotangent, slot, 0, keepdims=False)) * live.astype(BF)
    gout_t = gout.T
    shrink_t = shrink_w.T
    if (groups, lax.axis_size("dp")) == (4, 8):
        one = lambda a: a[None]
        blank = lambda n: jnp.zeros((n,), F32)
        bias_own = jnp.concatenate([query_b, blank(384 - cw), value_b, blank(384 - cw), expand_b, blank(1280 - fw)])
        tail_own = jnp.concatenate([expand_w[:, cut:], shrink_t[:, cut:], jnp.zeros((width, 128 - 2 * (fw - cut)), BF)], axis=1)
        qkvs, atts, lses, (first_t, second, second_t, midway), attn_ws, mlp_ws, tops, bias_all = front(
            0, one(norm1_gain), one(norm1_shift), one(norm2_gain), one(norm2_shift), one(out_b), jnp.broadcast_to(bias_own, (8, 2048)),
            x_low, query_w, key_w, value_w, out_w, expand_w, shrink_t, tail_own, length)
        mine, sec, out_low, h2, h3, geb, part_sum = middle(1, fw, live[None, None], one(shrink_b), bias_all, second, second_t, gout, gout_t, midway, *mlp_ws)
        out_high, in_all, sum_attn, sum_mlp, vec = back(
            2, one(norm1_gain), one(norm2_gain), live[None, None], geb, jnp.where(live > 0.0, tops[:, :, 0], -1e30)[:, None],
            gout, midway, sec, first_t, x_low, mine, part_sum, h2, h3, qkvs, atts, lses, attn_ws, length)
        outputs = jnp.concatenate([out_low.reshape(3, -1, width), out_high.reshape(3, -1, width)], axis=1)[:, :length]
        input_grads = in_all.reshape(3, TOK, width)[:, :length].astype(F32)
        own = lax.dynamic_index_in_dim(vec, z, 0, keepdims=False)
        grad_query_b, grad_value_b, grad_expand_b, logit_top = own[:cw], own[384:384 + cw], own[768:768 + fw], own[1920:1920 + heads]
        tail = [vec[4 + i, :width] for i in range(6)]
    else:
        attn_own = jnp.concatenate([query_w, key_w, value_w, out_w.T], axis=1)
        mlp_own = jnp.concatenate([expand_w[:, :cut], shrink_t[:, :cut], expand_w[:, cut:], shrink_t[:, cut:]], axis=1)
        net = General(groups, attn_own, mlp_own)
        biases = net.vectors(jnp.concatenate([query_b, value_b, expand_b]))

        x = x_low.astype(F32)
        normed1, inverse1 = normalize(x)
        first = (normed1 * norm1_gain + norm1_shift).astype(BF)
        first_t = first.T
        acc = x + out_b
        kept, tops = [], []
        for k in range(groups):
            b = biases[k]
            qkv, att, lse, top, acc = attn_fwd(first, net.attn[k], b[None, :cw], b[None, cw:2 * cw], acc, length)
            kept.append((qkv, att, lse))
            tops.append(top[:, 0])
        midway = acc
        normed2, inverse2 = normalize(midway)
        second = (normed2 * norm2_gain + norm2_shift).astype(BF)
        second_t = second.T
        mlp = midway + shrink_b
        sec = jnp.zeros((TOK, width), F32)
        grad_mlp, geb = [], []
        for k in range(groups):
            grad, g_b, mlp, sec = mlp_call(second, second_t, gout, gout_t, net.mlp[k], biases[k][None, 2 * cw:], mlp, sec)
            grad_mlp.append(grad)
            geb.append(g_b[0, :fw])
        back2, gn2g, gn2s = norm_back(sec, normed2, inverse2, norm2_gain)
        gout32 = gout.astype(F32)
        gmid = gout32 + back2
        gmid_low = gmid.astype(BF)
        gmid_t = gmid_low.T
        acc = jnp.zeros((TOK, width), F32)
        grad_attn, gqb, gvb = [None] * groups, [None] * groups, [None] * groups
        for k in reversed(range(groups)):
            grad, g_q, g_v, acc = attn_bwd(gmid_low, gmid_t, first_t, net.attn[k], *kept[k], acc, length)
            grad_attn[k], gqb[k], gvb[k] = grad, g_q[0], g_v[0]
        back1, gn1g, gn1s = norm_back(acc, normed1, inverse1, norm1_gain)
        input_grad = ((gmid + back1) * live)[:length].astype(BF)

        outputs = net.share((mlp[:length] * live).astype(BF))
        input_grads = net.share(input_grad).astype(F32)
        sum_attn, sum_mlp = net.collect(grad_attn, grad_mlp)
        flat = lambda items: net.by_index(items).reshape(-1)
        vector = jnp.concatenate([flat(gqb), flat(gvb), flat(geb), jnp.sum(gmid, axis=0), jnp.sum(gout32, axis=0), gn1g, gn1s, gn2g, gn2s])
        vector = lax.psum(vector, ("dp", "tensor"))
        part = lambda start, size: lax.dynamic_slice_in_dim(vector, start, size, 0)
        whole, hidden = cw * groups, fw * groups
        tail = [vector[2 * whole + hidden + i * width:][:width] for i in range(6)]
        logit_top = lax.pmax(jnp.where(live > 0.0, net.by_index(tops), -1e30), ("dp", "tensor"))
        logit_top = lax.dynamic_index_in_dim(logit_top, z, 0, keepdims=False)
        grad_query_b, grad_value_b, grad_expand_b = part(z * cw, cw), part(whole + z * cw, cw), part(2 * whole + z * fw, fw)
    factor = jnp.sqrt(clip_limit / jnp.maximum(logit_top, clip_limit))
    column_factor = jnp.repeat(factor, HD)
    clipped_query = (query_w.astype(F32) * column_factor).astype(BF)
    clipped_key = (key_w.astype(F32) * column_factor).astype(BF)
    unpack = lambda a, i: jnp.concatenate([a[:, i * cut:(i + 1) * cut], a[:, 2 * cut + i * (fw - cut):][:, :fw - cut]], axis=1)
    return (outputs, input_grads, sum_attn[:, :cw], grad_query_b, sum_attn[:, cw:2 * cw], sum_attn[:, 2 * cw:3 * cw], grad_value_b,
            sum_attn[:, 3 * cw:].T, tail[0], tail[2], tail[3], tail[4], tail[5], unpack(sum_mlp, 0), grad_expand_b, unpack(sum_mlp, 1).T,
            tail[1], clipped_query, clipped_key)


def solution(mesh):
    columns, rows, vector = P(None, "tensor"), P("tensor", None), P("tensor")
    whole = P("dp", None, None)
    return jax.shard_map(
        shards, mesh=mesh,
        in_specs=(whole, P("dp"), whole, columns, vector, columns, columns, vector, rows, P(), P(), P(), P(), P(), columns, vector, rows, P()),
        out_specs=(whole, whole, P("dp", "tensor"), vector, P("dp", "tensor"), P("dp", "tensor"), vector, P("tensor", "dp"), P(), P(), P(), P(), P(),
                   P("dp", "tensor"), vector, P("tensor", "dp"), P(), columns, columns),
        check_vma=False)
```

```python
import functools
import math

import jax
import jax.numpy as jnp
from jax import lax
from jax.experimental import pallas as pl
from jax.experimental.pallas import tpu as pltpu
from jax.sharding import PartitionSpec as P

HD = 72
TOK = 768
RT = 256
SC = 1 / math.sqrt(HD)
LOG2E = 1.4426950408889634
F32 = jnp.float32
BF = jnp.bfloat16
norm_eps = 1e-06
clip_limit = 3.0
tanh_coef = 0.7978845608028654
cube_coef = 0.044715
VM = pl.BlockSpec(memory_space=pltpu.VMEM)
HB = pl.BlockSpec(memory_space=pl.ANY)
MESH = pl.DeviceIdType.MESH


def nn(a, b):
    return jnp.dot(a, b, preferred_element_type=F32)


def nt(a, b):
    return lax.dot_general(a, b, (((1,), (1,)), ((), ())), preferred_element_type=F32)


def tn(a, b):
    return lax.dot_general(a, b, (((0,), (0,)), ((), ())), preferred_element_type=F32)


def shape(dims, dtype):
    return jax.ShapeDtypeStruct(dims, dtype)


def cut_rows(rows):
    first = (rows // 2 + 15) // 16 * 16
    return first, rows - first


def block_rows(lhs, rhs, half, write):
    if half is None:
        @pl.loop(0, lhs.shape[0] // 384)
        def _(t):
            place = pl.ds(pl.multiple_of(t * 384, 128), 384)
            write(place, nn(lhs[place, :], rhs[...]))
    else:
        rows = lhs.shape[0] // 8
        d = lax.axis_index("dp")

        @pl.loop(0, 2)
        def _(t):
            r = 4 * t + 1 - half
            both = [lhs[pl.ds(pl.multiple_of((d ^ q) * rows, 16), rows), :] for q in (r, r + 2)]
            write(pl.ds(pl.multiple_of(t * 2 * rows, 16), 2 * rows), nn(jnp.concatenate(both, axis=0), rhs[...]))


def attn_fwd_kernel(length, heads, first, qb, vb, acc_in, W, qkv, att, lse, tops, acc):
    cw = heads * HD

    @pl.loop(0, TOK // RT)
    def _(i):
        rows = pl.ds(pl.multiple_of(i * RT, RT), RT)
        t = nn(first[rows, :], W[:, :3 * cw])
        q = (t[:, :cw] + qb[...]).astype(BF)
        k = t[:, cw:2 * cw].astype(BF)
        v = (t[:, 2 * cw:] + vb[...]).astype(BF)
        for h in range(heads):
            qkv[h, rows, :] = q[:, h * HD:(h + 1) * HD]
            qkv[heads + h, rows, :] = k[:, h * HD:(h + 1) * HD]
            qkv[2 * heads + h, rows, :] = v[:, h * HD:(h + 1) * HD]

    tops[...] = jnp.full(tops.shape, -1e30, F32)

    @pl.loop(0, TOK // RT)
    def _(i):
        rows = pl.ds(pl.multiple_of(i * RT, RT), RT)
        rid = lax.broadcasted_iota(jnp.int32, (RT, 1), 0) + i * RT
        cid = lax.broadcasted_iota(jnp.int32, (1, TOK), 1)
        res = []
        for h in range(heads):
            s = nt(qkv[h, rows, :], qkv[heads + h])
            s = jnp.where(cid < length, s, -1e30)
            m = jnp.max(s, axis=1, keepdims=True)
            e = jnp.exp2((s - m) * (SC * LOG2E))
            l = jnp.sum(e, axis=1, keepdims=True)
            o = nn(e.astype(BF), qkv[2 * heads + h]) * (1.0 / l)
            res.append(o.astype(BF))
            lse[rows, h:h + 1] = m * (SC * LOG2E) + jnp.log2(l)
            tops[h:h + 1, :] = jnp.maximum(tops[h:h + 1, :], jnp.max(jnp.where(rid < length, m, -1e30)) * SC)
        a = jnp.concatenate(res, axis=1)
        att[rows, :] = a
        acc[rows, :] = acc_in[rows, :] + nt(a, W[:, 3 * cw:])


def attn_fwd(first, W, qb, vb, acc, length):
    D = first.shape[1]
    cw = W.shape[1] // 4
    heads = cw // HD
    return pl.pallas_call(
        functools.partial(attn_fwd_kernel, length, heads),
        out_shape=(shape((3 * heads, TOK, HD), BF), shape((TOK, cw), BF), shape((TOK, 128), F32), shape((heads, 128), F32), shape((TOK, D), F32)),
        in_specs=[VM] * 5,
        out_specs=(VM,) * 5,
        compiler_params=pltpu.CompilerParams(vmem_limit_bytes=44 * 2**20),
        cost_estimate=pl.CostEstimate(flops=2 * TOK * (D * cw * 4 + heads * 2 * TOK * HD * 6), bytes_accessed=25 * 2**20, transcendentals=heads * TOK * TOK),
        name="attn_fwd",
    )(first, qb, vb, acc, W)


def gelu_parts(u):
    u2 = u * u
    t = jnp.tanh(u * (tanh_coef + (tanh_coef * cube_coef) * u2))
    hu = 0.5 * (1.0 + t)
    return u * hu, hu + u * (0.5 * tanh_coef) * (1.0 - t * t) * (1.0 + (3.0 * cube_coef) * u2)


def mlp_kernel(fw, second, secondT, gout, goutT, eb, mlp_in, sec_in, W, G, geb, mlp, sec, E, ST, act_s, gpre_s):
    cut = fw // 128 * 128
    tail = fw - cut
    E[:, :cut] = W[:, :cut]
    ST[:, :cut] = W[:, cut:2 * cut]
    last = W[:, 2 * cut:]
    blank = jnp.zeros((last.shape[0], 128 - tail), BF)
    E[:, cut:] = jnp.concatenate([last[:, :tail], blank], axis=1)
    ST[:, cut:] = jnp.concatenate([last[:, tail:], blank], axis=1)
    geb[...] = jnp.zeros_like(geb)

    @pl.loop(0, TOK // RT)
    def _(i):
        rows = pl.ds(pl.multiple_of(i * RT, RT), RT)
        act, slope = gelu_parts(nn(second[rows, :], E[...]) + eb[...])
        act_s[rows, :] = act.astype(BF)
        gp = nn(gout[rows, :], ST[...]) * slope
        geb[...] += jnp.sum(gp, axis=0, keepdims=True)
        gpre_s[rows, :] = gp.astype(BF)
        mlp[rows, :] = mlp_in[rows, :] + nt(act_s[rows, :], ST[...])
        sec[rows, :] = sec_in[rows, :] + nt(gpre_s[rows, :], E[...])

    def write(lo, last):
        def put(place, v):
            v = v.astype(BF)
            G[place, lo:lo + cut] = v[:, :cut]
            G[place, last:last + tail] = v[:, cut:fw]
        return put

    block_rows(secondT, gpre_s, None, write(0, 2 * cut))
    block_rows(goutT, act_s, None, write(cut, 2 * cut + tail))


def mlp_call(second, secondT, gout, goutT, W, eb, mlp, sec):
    D = second.shape[1]
    fw = W.shape[1] // 2
    wide = fw // 128 * 128 + 128
    eb = jnp.pad(eb, ((0, 0), (0, wide - fw)))
    return pl.pallas_call(
        functools.partial(mlp_kernel, fw),
        out_shape=(shape((D, 2 * fw), BF), shape((1, wide), F32), shape((TOK, D), F32), shape((TOK, D), F32)),
        in_specs=[VM] * 8,
        out_specs=(VM,) * 4,
        scratch_shapes=[pltpu.VMEM((D, wide), BF)] * 2 + [pltpu.VMEM((TOK, wide), BF)] * 2,
        compiler_params=pltpu.CompilerParams(vmem_limit_bytes=56 * 2**20),
        cost_estimate=pl.CostEstimate(flops=2 * 9 * TOK * D * fw, bytes_accessed=35 * 2**20, transcendentals=TOK * fw),
        name="mlp",
    )(second, secondT, gout, goutT, eb, mlp, sec, W)


def attn_bwd_kernel(length, heads, gmid, gmidT, firstT, qkv, att, lse, acc_in, W, G, gqb, gvb, acc, ga_s, d_s, dk_s, dv_s):
    cw = heads * HD

    @pl.loop(0, TOK // RT)
    def _(i):
        rows = pl.ds(pl.multiple_of(i * RT, RT), RT)
        g = nn(gmid[rows, :], W[:, 3 * cw:]).astype(BF)
        for h in range(heads):
            ga_s[h, rows, :] = g[:, h * HD:(h + 1) * HD]

    gqb[...] = jnp.zeros_like(gqb)
    dk_s[...] = jnp.zeros_like(dk_s)
    dv_s[...] = jnp.zeros_like(dv_s)

    @pl.loop(0, TOK // RT)
    def _(i):
        rows = pl.ds(pl.multiple_of(i * RT, RT), RT)
        cid = lax.broadcasted_iota(jnp.int32, (1, TOK), 1)
        dqs = []
        for h in range(heads):
            q, k, v, g = qkv[h, rows, :], qkv[heads + h], qkv[2 * heads + h], ga_s[h, rows, :]
            s = nt(q, k)
            p = jnp.exp2(s * (SC * LOG2E) - lse[rows, h:h + 1])
            p = jnp.where(cid < length, p, 0.0)
            dp = nt(g, v)
            dd = jnp.sum(g.astype(F32) * att[rows, h * HD:(h + 1) * HD].astype(F32), axis=1, keepdims=True)
            ds = (p * (dp - dd)).astype(BF)
            dqs.append(nn(ds, k) * SC)
            dk_s[h] += tn(ds, q)
            dv_s[h] += tn(p.astype(BF), g)
        dq = jnp.concatenate(dqs, axis=1)
        gqb[...] += jnp.sum(dq, axis=0, keepdims=True)
        d_s[rows, :cw] = dq.astype(BF)

    dk = jnp.concatenate([dk_s[h] * SC for h in range(heads)], axis=1)
    d_s[:, cw:2 * cw] = dk.astype(BF)
    dv = jnp.concatenate([dv_s[h] for h in range(heads)], axis=1)
    gvb[...] = jnp.sum(dv, axis=0, keepdims=True)
    d_s[:, 2 * cw:] = dv.astype(BF)

    @pl.loop(0, TOK // RT)
    def _(i):
        rows = pl.ds(pl.multiple_of(i * RT, RT), RT)
        acc[rows, :] = acc_in[rows, :] + nt(d_s[rows, :], W[:, :3 * cw])

    def write(lo, hi):
        def put(place, v):
            G[place, lo:hi] = v.astype(BF)
        return put

    block_rows(firstT, d_s, None, write(0, 3 * cw))
    block_rows(gmidT, att, None, write(3 * cw, 4 * cw))


def attn_bwd(gmid, gmidT, firstT, W, qkv, att, lse, acc, length):
    D = gmid.shape[1]
    cw = W.shape[1] // 4
    heads = cw // HD
    return pl.pallas_call(
        functools.partial(attn_bwd_kernel, length, heads),
        out_shape=(shape((D, 4 * cw), BF), shape((1, cw), F32), shape((1, cw), F32), shape((TOK, D), F32)),
        in_specs=[VM] * 8,
        out_specs=(VM,) * 4,
        scratch_shapes=[pltpu.VMEM((heads, TOK, HD), BF), pltpu.VMEM((TOK, 3 * cw), BF), pltpu.VMEM((heads, TOK, HD), F32), pltpu.VMEM((heads, TOK, HD), F32)],
        compiler_params=pltpu.CompilerParams(vmem_limit_bytes=52 * 2**20),
        cost_estimate=pl.CostEstimate(flops=2 * TOK * (D * cw * 8 + heads * 5 * TOK * HD * 6), bytes_accessed=30 * 2**20, transcendentals=heads * TOK * TOK),
        name="attn_bwd",
    )(gmid, gmidT, firstT, qkv, att, lse, acc, W)


def normalize(values):
    centre = jnp.mean(values, axis=-1, keepdims=True)
    centred = values - centre
    spread = jnp.mean(centred * centred, axis=-1, keepdims=True)
    inverse = lax.rsqrt(spread + norm_eps)
    return centred * inverse, inverse


def norm_back(grad_norm, normed, inverse, gain):
    scaled = grad_norm * gain
    first_mean = jnp.mean(scaled, axis=-1, keepdims=True)
    second_mean = jnp.mean(scaled * normed, axis=-1, keepdims=True)
    grad_input = inverse * (scaled - first_mean - normed * second_mean)
    return grad_input, jnp.sum(grad_norm * normed, axis=0), jnp.sum(grad_norm, axis=0)


def slot_table(d, groups):
    z = lax.axis_index("tensor")
    middle = 1 + d % 2
    return jnp.where(z == 0, 0, jnp.where(z == groups - 1, 1, 2)), (z == 0) | (z == groups - 1) | (z == middle)


HOPS = {
    "u1": (1, ((0, None),)), "u2": (3, ((1, None),)), "u3": (1, ((2, None),)),
    "w1": (1, ((3, None),)), "w2": (3, ((2, None),)), "w3": (1, ((1, None),)),
    "v1": (3, ((1, 0), (2, 1))), "v2": (1, ((2, 0), (1, 1))), "v3": (1, ((1, 0), (2, 1))),
}
HOP_FROM = {"u1": "me", "u2": "u1", "u3": "u2", "w1": "me", "w2": "w1", "w3": "w2", "v1": "me", "v2": "v1", "v3": "me"}
NAMES = ("u1", "w1", "v1", "v3"), ("u2", "w2", "v2"), ("u3", "w3")
BEGIN = {"u": 0, "w": 1, "v": 2}


class Wires:
    def __init__(self, s_sem, r_sem):
        self.s, self.r, self.n = s_sem, r_sem, 0
        self.d, self.z = lax.axis_index("dp"), lax.axis_index("tensor")

    def local(self, src, dst, used):
        i = self.n
        self.n += 1
        make = lambda: pltpu.make_async_copy(src, dst, self.s.at[i])
        return (lambda: pl.when(used)(lambda: make().start())), (lambda: pl.when(used)(lambda: make().wait()))

    def swap(self, src, dst, dp=0, z=0, sends=None):
        i = self.n
        self.n += 1
        make = lambda: pltpu.make_async_remote_copy(src_ref=src, dst_ref=dst, send_sem=self.s.at[i], recv_sem=self.r.at[i], device_id=(self.d ^ dp, self.z ^ z), device_id_type=MESH)
        if sends is None:
            return (lambda: make().start()), (lambda: make().wait())

        def any_of(z_here):
            hit = None
            for zz, cc in sends:
                this = z_here == zz
                if cc is not None:
                    this = this & (self.d % 2 == cc)
                hit = this if hit is None else hit | this
            return hit

        def start():
            pl.when(any_of(self.z))(lambda: make().start())

        def wait():
            pl.when(any_of(self.z))(lambda: make().wait_send())
            pl.when(any_of(self.z ^ z))(lambda: make().wait_recv())

        return start, wait


def greet(d, z, masks):
    sem = pltpu.get_barrier_semaphore()
    for dp, t in masks:
        pl.semaphore_signal(sem, inc=1, device_id=(d ^ dp, z ^ t), device_id_type=MESH)
    pl.semaphore_wait(sem, len(masks))


class Summing:
    def __init__(self, wires, H, land):
        self.H = H
        self.rows = r = H.shape[0] // 4
        self.one, self.two = one, two = cut_rows(r)
        ax, by = land.at[pl.ds(0, 2 * one), :], land.at[pl.ds(2 * one, 2 * two), :]
        ay, bx = land.at[pl.ds(2 * r, one), :], land.at[pl.ds(2 * r + one, two), :]
        self.land = land
        h = lambda lo, n: H.at[pl.ds(lo, n), :]
        at = lambda ref, lo, n: ref.at[pl.ds(lo, n), :]
        self.c1 = [wires.swap(h(r, one), at(land, 0, one), dp=2), wires.swap(h(3 * r, one), at(land, one, one), dp=2),
                   wires.swap(h(2 * r + one, two), at(land, 2 * one, two), dp=4), wires.swap(h(3 * r + one, two), at(land, 2 * one + two, two), dp=4)]
        self.c2 = [wires.swap(h(2 * r, one), ay, dp=4), wires.swap(h(r + one, two), bx, dp=2)]

    def add(self, lo, n, *froms):
        total = self.H[lo:lo + n, :].astype(F32)
        for f in froms:
            total = total + self.land[f:f + n, :].astype(F32)
        self.H[lo:lo + n, :] = total.astype(BF)

    def step1(self):
        for s, _ in self.c1:
            s()

    def step2(self):
        r, one, two = self.rows, self.one, self.two
        for _, w in self.c1:
            w()
        self.add(2 * r, one, one)
        self.add(r + one, two, 2 * one + two)
        for s, _ in self.c2:
            s()

    def step3(self):
        r, one, two = self.rows, self.one, self.two
        for _, w in self.c2:
            w()
        self.add(0, one, 0, 2 * r)
        self.add(one, two, 2 * one, 2 * r + one)


ENDS = ((0, None), (3, None))
INNER = ((1, None), (2, None))


class LineSum:
    def __init__(self, wires, parts, land):
        self.parts, self.land = parts, land
        self.inner = (wires.z == 1) | (wires.z == 2)
        self.a = {k: wires.swap(parts[k], land.at[k - 1], z=1, sends=ENDS) for k in (1, 2, 3)}
        self.b = [wires.swap(parts[3], land.at[3], z=3, sends=INNER), wires.swap(parts[2], land.at[4], z=3, sends=INNER)]
        self.g = wires.swap(parts[1], land.at[0], z=1, sends=INNER)

    def alpha(self, k):
        self.a[k][0]()

    def add(self, k, i):
        @pl.when(self.inner)
        def _():
            self.parts[k][...] = (self.parts[k][...].astype(F32) + self.land[i].astype(F32)).astype(BF)

    def beta(self):
        self.a[2][1]()
        self.a[3][1]()
        self.add(3, 1)
        self.add(2, 2)
        for s, _ in self.b:
            s()

    def gamma(self):
        for _, w in self.b:
            w()
        self.a[1][1]()
        self.add(1, 4)
        self.g[0]()

    def total(self, own):
        self.g[1]()
        other = jnp.where(self.inner, self.land[3].astype(F32), 0.0)
        return own + self.land[0].astype(F32) + other


class Sharing:
    def __init__(self, wires, mine, O, chunks, base=0):
        self.stages = []
        stride = O.shape[0] // 3
        for lo, n in chunks:
            here = []
            for names in NAMES:
                row = []
                for name in names:
                    mask, sends = HOPS[name]
                    place = O.at[pl.ds(BEGIN[name[0]] * stride + lo - base, n), :]
                    row.append(wires.swap(mine.at[pl.ds(lo, n), :] if HOP_FROM[name] == "me" else place, place, z=mask, sends=sends))
                here.append(row)
            self.stages.append(here)

    def start(self, chunk, stage):
        for s, _ in self.stages[chunk][stage]:
            s()

    def wait(self, chunk, stage):
        for _, w in self.stages[chunk][stage]:
            w()

    def on(self, chunk, stage):
        self.wait(chunk, stage - 1)
        self.start(chunk, stage)


OUT_CHUNKS = ((256, 256), (512, 224))
IN_CHUNKS = ((0, 128), (128, 128), (256, 128), (384, 128), (512, 128), (640, 96))
MASKS = [(1, 0), (2, 0), (4, 0), (0, 1), (0, 2), (0, 3)]
COPIES = 180


def back_kernel(length, heads, gain1, gain2, live, geb, tops, gout, midway, sec, firstT, x, mine, whole0, h1, h2, h3, *rest):
    Ws, qkvs, atts, lses, rest = rest[:4], rest[4:8], rest[8:12], rest[12:16], rest[16:]
    (O_out, O_in, sum_a, sum_m, vec, g_s, gm_s, acc, gT, fT, x_s, W_s, qkv_s, att_s, lse_s, ga_s, d_s, dk_s, dv_s, out_s,
     Ha, La, Hm, Lm, za, zm, vr, w0_s, w1_s, l_sem, s_sem, r_sem) = rest
    cw = heads * HD
    D = g_s.shape[1]
    wires = Wires(s_sem, r_sem)
    d, z = wires.d, wires.z
    loads = {}
    order = [3, 2, 1, 0]
    names = iter(range(100))

    def load(key, src, dst):
        loads[key] = pltpu.make_async_copy(src, dst, l_sem.at[next(names)])

    load("midway", midway, acc)
    load("sec", sec, gm_s)
    load("gout", gout, g_s)
    load("firstT", firstT, fT)
    load("x", x, x_s)
    load("h2", h2, Hm.at[0])
    load("h3", h3, Hm.at[1])
    load("w0", whole0, w0_s)
    load("w1", h1, w1_s)
    for i, k in enumerate(order):
        b = i % 2
        load(f"W{i}", Ws[k], W_s.at[b])
        load(f"qkv{i}", qkvs[k], qkv_s.at[b])
        load(f"att{i}", atts[k], att_s.at[b])
        load(f"lse{i}", lses[k], lse_s.at[b])
    for key in ("midway", "sec", "gout", "h2", "h3", "w1", "w0", "firstT", "W0", "qkv0", "att0", "lse0", "x"):
        loads[key].start()
    slot = jnp.where(z == 0, 0, jnp.where(z == 3, 1, 2))
    own_place = pl.ds(pl.multiple_of(slot * TOK, 256), TOK)
    out_rows = O_out.shape[0] // 3
    out_base = TOK - out_rows
    out_place = pl.ds(pl.multiple_of(slot * out_rows, 256), out_rows)
    used = (z == 0) | (z == 3) | (z == 1 + d % 2)
    own_out, own_in = wires.local(mine.at[pl.ds(out_base, out_rows), :], O_out.at[out_place, :], used), wires.local(g_s, O_in.at[own_place, :], used)
    share_out = Sharing(wires, mine, O_out, OUT_CHUNKS, out_base)
    share_in = Sharing(wires, g_s, O_in, IN_CHUNKS)
    sums = {"m2": Summing(wires, Hm.at[0], Lm.at[0]), "m3": Summing(wires, Hm.at[1], Lm.at[1])}
    for k in range(4):
        sums[f"b{k}"] = Summing(wires, Ha.at[k], La.at[k])
    r = sum_a.shape[0]
    top = pl.ds(0, r)
    line_m = LineSum(wires, [None, w1_s, Hm.at[0, top, :], Hm.at[1, top, :]], zm)
    line_b = LineSum(wires, [Ha.at[k, top, :] for k in range(4)], za)
    exchange = {k: wires.swap(out_s, Ha.at[k], dp=1) for k in range(4)}
    spread = [wires.swap(vec, vr.at[i], dp=dp, z=t) for i, (dp, t) in enumerate(((1, 0), (2, 0), (4, 0), (0, 1), (0, 2)))]
    greet(d, z, MASKS)

    todo = {
        -3: [lambda: share_out.start(0, 0), own_out[0]],
        -2: [lambda: loads["h2"].wait(), sums["m2"].step1, lambda: loads["w1"].wait(), lambda: line_m.alpha(1)],
        0: [lambda: loads["h3"].wait(), lambda: loads["w0"].wait()],
        5: [sums["m2"].step2, sums["m3"].step1],
        8: [lambda: share_out.on(0, 1), lambda: share_out.start(1, 0)],
        10: [sums["m2"].step3, lambda: line_m.alpha(2)],
        15: [sums["m3"].step2],
        18: [lambda: share_out.on(0, 2), lambda: share_out.on(1, 1), sums["b3"].step2],
        20: [sums["m3"].step3, lambda: line_m.alpha(3)],
        22: [sums["b3"].step3, lambda: line_b.alpha(3)],
        25: [line_m.beta],
        28: [lambda: share_out.on(1, 2), sums["b2"].step2],
        33: [sums["b2"].step3, lambda: line_b.alpha(2)],
        35: [sums["b1"].step2],
        38: [sums["b1"].step3, lambda: line_b.alpha(1), line_m.gamma],
    }

    def tick(t):
        for action in todo.get(t, ()):
            action()

    vec[...] = jnp.zeros_like(vec)
    for key in ("midway", "sec", "gout"):
        loads[key].wait()

    def total_of(row, value):
        vec[row:row + 1, :D] += jnp.sum(value, axis=0, keepdims=True)

    def put_row(where, lo, value):
        n = value.shape[1]
        hit = lax.broadcasted_iota(jnp.int32, (8, n), 0) == where
        vec[0:8, lo:lo + n] += jnp.where(hit, jnp.broadcast_to(value, (8, n)), 0.0)

    @pl.loop(0, TOK // RT)
    def _(i):
        for t in range(3):
            pl.when(i == t)(functools.partial(tick, t - 3))
        rows = pl.ds(pl.multiple_of(i * RT, RT), RT)
        normed, inverse = normalize(acc[rows, :])
        e = gm_s[rows, :]
        go = g_s[rows, :].astype(F32)
        scaled = e * gain2[...]
        mean1 = jnp.mean(scaled, axis=-1, keepdims=True)
        mean2 = jnp.mean(scaled * normed, axis=-1, keepdims=True)
        gm = go + inverse * (scaled - mean1 - normed * mean2)
        total_of(4, gm)
        total_of(5, go)
        total_of(8, e * normed)
        total_of(9, e)
        gm_s[rows, :] = gm
        g_s[rows, :] = gm.astype(BF)
        gT[:, rows] = gm.T.astype(BF)

    def write(dst, lo, hi, add):
        def put(where, val):
            if add:
                val = val + dst[where, lo:hi].astype(F32)
            dst[where, lo:hi] = val.astype(BF)
        return put

    def keep(i):
        k, b = order[i], i % 2
        exchange[k][1]()
        block_rows(fT, d_s.at[b], 1, write(Ha.at[k], 0, 3 * cw, True))
        block_rows(gT, att_s.at[b], 1, write(Ha.at[k], 3 * cw, 4 * cw, True))

    loads["firstT"].wait()
    acc[...] = jnp.zeros_like(acc)
    for i, k in enumerate(order):
        base, b = 10 * i, i % 2
        W, qkv, att, lse, dd_s = W_s.at[b], qkv_s.at[b], att_s.at[b], lse_s.at[b], d_s.at[b]
        for key in ("W", "qkv", "att", "lse"):
            loads[f"{key}{i}"].wait()
        if i < 3:
            for key in ("W", "qkv", "lse"):
                loads[f"{key}{i + 1}"].start()
        tick(base)

        @pl.loop(0, TOK // RT)
        def _(t):
            rows = pl.ds(pl.multiple_of(t * RT, RT), RT)
            g = nt(g_s[rows, :], W[3 * cw:, :]).astype(BF)
            for h in range(heads):
                ga_s[h, rows, :] = g[:, h * HD:(h + 1) * HD]

        if i:
            keep(i - 1)
            sums[f"b{order[i - 1]}"].step1()
        if i < 3:
            loads[f"att{i + 1}"].start()
        tick(base + 1)
        dk_s[...] = jnp.zeros_like(dk_s)
        dv_s[...] = jnp.zeros_like(dv_s)
        place = z ^ k

        @pl.loop(0, TOK // RT)
        def _(t):
            for n in range(3):
                pl.when(t == n)(functools.partial(tick, base + 2 + n))
            rows = pl.ds(pl.multiple_of(t * RT, RT), RT)
            cid = lax.broadcasted_iota(jnp.int32, (1, TOK), 1)
            dqs = []
            for h in range(heads):
                q, kk, v, g = qkv[h, rows, :], qkv[heads + h], qkv[2 * heads + h], ga_s[h, rows, :]
                s = nt(q, kk)
                p = jnp.exp2(s * (SC * LOG2E) - lse[rows, h:h + 1])
                p = jnp.where(cid < length, p, 0.0)
                dp = nt(g, v)
                dd = jnp.sum(g.astype(F32) * att[rows, h * HD:(h + 1) * HD].astype(F32), axis=1, keepdims=True)
                ds = (p * (dp - dd)).astype(BF)
                dqs.append(nn(ds, kk) * SC)
                dk_s[h] += tn(ds, q)
                dv_s[h] += tn(p.astype(BF), g)
            dq = jnp.concatenate(dqs, axis=1)
            put_row(place, 0, jnp.sum(dq, axis=0, keepdims=True))
            dd_s[rows, :cw] = dq.astype(BF)

        dd_s[:, cw:2 * cw] = jnp.concatenate([dk_s[h] * SC for h in range(heads)], axis=1).astype(BF)
        dv = jnp.concatenate([dv_s[h] for h in range(heads)], axis=1)
        put_row(place, 384, jnp.sum(dv, axis=0, keepdims=True))
        dd_s[:, 2 * cw:] = dv.astype(BF)
        put_row(place, 768, geb[k])
        put_row(place, 1920, tops[k])
        tick(base + 5)

        block_rows(fT, dd_s, 0, write(out_s, 0, 3 * cw, False))
        block_rows(gT, att, 0, write(out_s, 3 * cw, 4 * cw, False))
        exchange[k][0]()
        tick(base + 6)

        @pl.loop(0, TOK // RT)
        def _(t):
            rows = pl.ds(pl.multiple_of(t * RT, RT), RT)
            acc[rows, :] += nn(dd_s[rows, :], W[:3 * cw, :])

        tick(base + 7)
        tick(base + 8)

    loads["x"].wait()

    @pl.loop(0, TOK // RT)
    def _(i):
        rows = pl.ds(pl.multiple_of(i * RT, RT), RT)
        normed, inverse = normalize(x_s[rows, :].astype(F32))
        e = acc[rows, :]
        scaled = e * gain1[...]
        mean1 = jnp.mean(scaled, axis=-1, keepdims=True)
        mean2 = jnp.mean(scaled * normed, axis=-1, keepdims=True)
        total_of(6, e * normed)
        total_of(7, e)
        g_s[rows, :] = ((gm_s[rows, :] + inverse * (scaled - mean1 - normed * mean2)) * live[...]).astype(BF)
        for t in range(3):
            @pl.when(i == t)
            def _():
                share_in.start(2 * t, 0)
                share_in.start(2 * t + 1, 0)

    own_in[0]()
    spread[0][0]()
    keep(3)
    sums["b0"].step1()
    after = {0: [line_b.beta], 1: [sums["b0"].step2], 2: [sums["b0"].step3], 3: [line_b.gamma]}
    row = lax.broadcasted_iota(jnp.int32, vec.shape, 1)

    def fold(i):
        spread[i][1]()
        a, c = vec[...], vr[i]
        vec[...] = jnp.where(row < 1920, a + c, jnp.maximum(a, c))
        if i < 4:
            spread[i + 1][0]()

    n = len(IN_CHUNKS)
    for t in range(n + 2):
        if t < n:
            share_in.on(t, 1)
        for action in after.get(t, ()):
            action()
        if 1 <= t <= n:
            share_in.on(t - 1, 2)
        if 1 <= t <= 5:
            fold(t - 1)
    for c in range(len(OUT_CHUNKS)):
        share_out.wait(c, 2)
    own_out[1]()
    own_in[1]()
    sum_m[...] = line_m.total(w0_s[...].astype(F32))
    sum_a[...] = line_b.total(Ha[0, :r, :].astype(F32))
    for c in range(n):
        share_in.wait(c, 2)


def back(number, gain1, gain2, live, geb, tops, gout, midway, sec, firstT, x, mine, whole0, h1, h2, h3, qkvs, atts, lses, Ws, length):
    D = gout.shape[1]
    cw = Ws[0].shape[0] // 4
    cm = h2.shape[1]
    heads = cw // HD
    r = D // 8
    vm = pltpu.VMEM
    dma = pltpu.SemaphoreType.DMA
    return pl.pallas_call(
        functools.partial(back_kernel, length, heads),
        out_shape=(shape((3 * (TOK - OUT_CHUNKS[0][0]), D), BF), shape((3 * TOK, D), BF), shape((r, 4 * cw), F32), shape((r, cm), F32), shape((16, 2048), F32)),
        in_specs=[VM] * 5 + [HB] * 26,
        out_specs=(HB, HB, VM, VM, VM),
        scratch_shapes=[vm((TOK, D), BF), vm((TOK, D), F32), vm((TOK, D), F32), vm((D, TOK), BF), vm((D, TOK), BF), vm((TOK, D), BF),
                        vm((2, 4 * cw, D), BF), vm((2, 3 * heads, TOK, HD), BF), vm((2, TOK, cw), BF), vm((2, TOK, 128), F32),
                        vm((heads, TOK, HD), BF), vm((2, TOK, 3 * cw), BF), vm((heads, TOK, HD), F32), vm((heads, TOK, HD), F32), vm((4 * r, 4 * cw), BF),
                        vm((4, 4 * r, 4 * cw), BF), vm((4, 3 * r, 4 * cw), BF), vm((2, 4 * r, cm), BF), vm((2, 3 * r, cm), BF),
                        vm((5, r, 4 * cw), BF), vm((5, r, cm), BF), vm((5, 16, 2048), F32), vm((r, cm), BF), vm((r, cm), BF),
                        dma((32,)), dma((COPIES,)), dma((COPIES,))],
        compiler_params=pltpu.CompilerParams(vmem_limit_bytes=63 * 2**20, collective_id=number, has_side_effects=True),
        cost_estimate=pl.CostEstimate(flops=4 * 2 * TOK * (D * cw * 8 + heads * 5 * TOK * HD * 6), bytes_accessed=60 * 2**20, transcendentals=4 * heads * TOK * TOK),
        name="back",
    )(gain1, gain2, live, geb, tops, gout, midway, sec, firstT, x, mine, whole0, h1, h2, h3, *Ws, *qkvs, *atts, *lses)


class Spreading:
    def __init__(self, wires, piece, W):
        rows = W.shape[0] // 8
        one, two = cut_rows(rows)
        d = wires.d
        at = lambda mask, lo=0, n=rows: W.at[pl.ds(pl.multiple_of((d ^ mask) * rows + lo, 16), n), :]
        self.own = wires.local(piece, at(0), d >= 0)
        self.s0 = [wires.swap(piece, at(0), dp=m) for m in (2, 4, 1)]
        self.s1 = [wires.swap(at(2, 0, one), at(2, 0, one), dp=4), wires.swap(at(4, one, two), at(4, one, two), dp=2)]
        self.s1c = [wires.swap(at(m), at(m), dp=1) for m in (2, 4)]
        self.s2 = wires.swap(at(6), at(6), dp=1)

    def step0(self):
        self.own[0]()
        for s, _ in self.s0:
            s()

    def landed(self):
        for _, w in self.s0 + [self.own]:
            w()

    def go_on(self):
        for s, _ in self.s1 + self.s1c:
            s()

    def step1(self):
        for _, w in self.s0:
            w()
        self.go_on()

    def step2(self):
        for _, w in self.s1:
            w()
        self.s2[0]()

    def finish(self, own=True):
        for _, w in self.s1c + [self.s2] + [self.own] * own:
            w()


class Moves:
    def __init__(self, sem):
        self.sem, self.made = sem, {}

    def add(self, key, src, dst):
        self.made[key] = pltpu.make_async_copy(src, dst, self.sem.at[len(self.made)])

    def start(self, *keys):
        for k in keys:
            self.made[k].start()

    def wait(self, *keys):
        for k in keys:
            self.made[k].wait()


def front_kernel(length, heads, gain1, shift1, gain2, shift2, out_b, bias_own, x, qw, kw, vw, ow, mw, *rest):
    (qkv0, qkv1, qkv2, qkv3, att0, att1, att2, att3, lse0, lse1, lse2, lse3, firstT, second, secondT, midway, Wa0, Wa1, Wa2, Wa3, Wm1, Zm2,
     tops, bias_all, x_s, first_s, T_s, second_s, acc, W, Za, Zm1, qkv_s, att_s, lse_s, bias, l_sem, s_sem, r_sem) = rest
    cw = heads * HD
    D = x_s.shape[1]
    wires, moves = Wires(s_sem, r_sem), Moves(l_sem)
    d, z = wires.d, wires.z

    def own_rows(ref):
        n = ref.shape[0] // 8
        return pl.ds(pl.multiple_of(d * n, 16), n)

    for i, ref in enumerate((qw, kw, vw, ow)):
        moves.add(f"w{i}", ref, W.at[0, pl.ds(i * cw, cw), :])
    moves.add("x", x, x_s)
    moves.add("oW0", W.at[0], Wa0)
    for k, (a, b, c) in enumerate(((qkv0, att0, lse0), (qkv1, att1, lse1), (qkv2, att2, lse2), (qkv3, att3, lse3))):
        moves.add(f"qkv{k}", qkv_s.at[k], a)
        moves.add(f"att{k}", att_s.at[k], b)
        moves.add(f"lse{k}", lse_s.at[k], c)
    for k, ref in enumerate((Wa1, Wa2, Wa3)):
        moves.add(f"oW{k + 1}", W.at[k + 1], ref)
    moves.add("firstT", T_s, firstT)
    moves.add("second", second_s, second)
    moves.add("secondT", T_s, secondT)
    moves.add("midway", acc, midway)
    moves.start("w0", "w1", "w2", "w3", "x")

    zb = [wires.swap(bias.at[0], bias.at[k], z=k) for k in (1, 2, 3)]
    a_piece, m_piece = W.at[0, own_rows(W.at[0]), :], mw.at[own_rows(mw), :]
    za = [wires.swap(a_piece, Za.at[0], z=1), wires.swap(a_piece, Za.at[1], z=2), wires.swap(Za.at[1], Za.at[2], z=1)]
    zm = [wires.swap(m_piece, Zm1, z=1), wires.swap(m_piece, Zm2, z=2)]
    ga = {k: Spreading(wires, Za.at[k - 1], W.at[k]) for k in (1, 2, 3)}
    gm = Spreading(wires, Zm1, Wm1)
    greet(d, z, MASKS)
    bias[0] = bias_own[...]
    for s, _ in zb:
        s()
    moves.wait("w0", "w1", "w2", "w3")
    za[0][0]()
    za[1][0]()
    moves.start("oW0")
    moves.wait("x")

    @pl.loop(0, TOK // RT)
    def _(i):
        part = pl.ds(pl.multiple_of(i * RT, RT), RT)
        xt = x_s[part, :].astype(F32)
        normed, _ = normalize(xt)
        f = normed * gain1[...] + shift1[...]
        first_s[part, :] = f.astype(BF)
        T_s[:, part] = f.T.astype(BF)
        acc[part, :] = xt + out_b[...]

    moves.start("firstT")
    for _, w in zb:
        w()
    bias_all[...] = bias[...]

    def z_a3():
        za[1][1]()
        za[2][0]()

    todo = {
        0: [zm[0][0]],
        1: [za[0][1], ga[1].step0],
        5: [z_a3, ga[2].step0, ga[1].step1, ga[1].step2],
        10: [za[2][1], ga[3].step0],
        11: [zm[1][0]],
        13: [ga[2].step1],
        15: [ga[2].step2],
        20: [ga[3].step1, zm[0][1], gm.step0],
        23: [ga[3].step2],
    }

    def tick(t):
        for action in todo.get(t, ()):
            action()

    for k in range(4):
        base = 10 * k
        Wk, qkv, att, lse = W.at[k], qkv_s.at[k], att_s.at[k], lse_s.at[k]
        if k:
            ga[k].finish()
            moves.start(f"oW{k}")
        tick(base)
        qb, vb = bias[k, 0:1, :cw], bias[k, 0:1, 384:384 + cw]

        @pl.loop(0, TOK // RT)
        def _(i):
            part = pl.ds(pl.multiple_of(i * RT, RT), RT)
            t = nt(first_s[part, :], Wk[:3 * cw, :])
            q = (t[:, :cw] + qb).astype(BF)
            kk = t[:, cw:2 * cw].astype(BF)
            v = (t[:, 2 * cw:] + vb).astype(BF)
            for h in range(heads):
                qkv[h, part, :] = q[:, h * HD:(h + 1) * HD]
                qkv[heads + h, part, :] = kk[:, h * HD:(h + 1) * HD]
                qkv[2 * heads + h, part, :] = v[:, h * HD:(h + 1) * HD]

        tick(base + 1)
        moves.start(f"qkv{k}")
        tops[k] = jnp.full(tops.shape[1:], -1e30, F32)

        @pl.loop(0, TOK // RT)
        def _(i):
            for n in range(3):
                pl.when(i == n)(functools.partial(tick, base + 2 + n))
            part = pl.ds(pl.multiple_of(i * RT, RT), RT)
            rid = lax.broadcasted_iota(jnp.int32, (RT, 1), 0) + i * RT
            cid = lax.broadcasted_iota(jnp.int32, (1, TOK), 1)
            res = []
            for h in range(heads):
                s = nt(qkv[h, part, :], qkv[heads + h])
                s = jnp.where(cid < length, s, -1e30)
                m = jnp.max(s, axis=1, keepdims=True)
                e = jnp.exp2((s - m) * (SC * LOG2E))
                l = jnp.sum(e, axis=1, keepdims=True)
                o = nn(e.astype(BF), qkv[2 * heads + h]) * (1.0 / l)
                res.append(o.astype(BF))
                lse[part, h:h + 1] = m * (SC * LOG2E) + jnp.log2(l)
                tops[k, h:h + 1, :] = jnp.maximum(tops[k, h:h + 1, :], jnp.max(jnp.where(rid < length, m, -1e30)) * SC)
            a = jnp.concatenate(res, axis=1)
            att[part, :] = a
            acc[part, :] += nn(a, Wk[3 * cw:, :])

        moves.start(f"att{k}", f"lse{k}")
        tick(base + 5)

    moves.start("midway")
    moves.wait("firstT")

    @pl.loop(0, TOK // RT)
    def _(i):
        part = pl.ds(pl.multiple_of(i * RT, RT), RT)
        normed, _ = normalize(acc[part, :])
        f = normed * gain2[...] + shift2[...]
        second_s[part, :] = f.astype(BF)
        T_s[:, part] = f.T.astype(BF)

    moves.start("second", "secondT")
    gm.landed()
    zm[1][1]()
    for k in range(4):
        moves.wait(f"qkv{k}", f"att{k}", f"lse{k}", f"oW{k}")
    moves.wait("second", "secondT", "midway")


def front(number, gain1, shift1, gain2, shift2, out_b, bias_own, x, qw, kw, vw, ow, mw, length):
    cw, D = qw.shape
    heads = cw // HD
    cm = mw.shape[0]
    vm = pltpu.VMEM
    dma = pltpu.SemaphoreType.DMA
    four = lambda s: (s,) * 4
    got = pl.pallas_call(
        functools.partial(front_kernel, length, heads),
        out_shape=(*four(shape((3 * heads, TOK, HD), BF)), *four(shape((TOK, cw), BF)), *four(shape((TOK, 128), F32)),
                   shape((D, TOK), BF), shape((TOK, D), BF), shape((D, TOK), BF), shape((TOK, D), F32), *four(shape((4 * cw, D), BF)),
                   shape((cm, D), BF), shape((cm // 8, D), BF), shape((4, heads, 128), F32), shape((4, 8, 2048), F32)),
        in_specs=[VM] * 6 + [HB] * 6,
        out_specs=(HB,) * 22 + (VM,) * 2,
        scratch_shapes=[vm((TOK, D), BF), vm((TOK, D), BF), vm((D, TOK), BF), vm((TOK, D), BF), vm((TOK, D), F32),
                        vm((4, 4 * cw, D), BF), vm((3, cw // 2, D), BF), vm((cm // 8, D), BF), vm((4, 3 * heads, TOK, HD), BF),
                        vm((4, TOK, cw), BF), vm((4, TOK, 128), F32), vm((4, 8, 2048), F32), dma((32,)), dma((64,)), dma((64,))],
        compiler_params=pltpu.CompilerParams(vmem_limit_bytes=62 * 2**20, collective_id=number, has_side_effects=True),
        cost_estimate=pl.CostEstimate(flops=4 * 2 * TOK * (D * cw * 4 + heads * 2 * TOK * HD * 6), bytes_accessed=60 * 2**20, transcendentals=4 * heads * TOK * TOK),
        name="front",
    )(gain1, shift1, gain2, shift2, out_b, bias_own, x, qw, kw, vw, ow, mw)
    return got[:4], got[4:8], got[8:12], got[12:16], got[16:20], got[20:22], got[22], got[23]


def middle_kernel(fw, live, shrink_b, bias_all, second, secondT, gout, goutT, midway, Wm0, Wm1, Zm2, *rest):
    (mine, sec, O0, H1, H2, H3, geb, part_sum, Wg2, Wg3, Zm3, Wg1, second_s, secondT_s, gout_s, goutT_s, mlp, sec_s, mine_s, W, act_s, slope_s, gpre_s, out_s,
     Hm, Lm, l_sem, s_sem, r_sem) = rest
    D = second_s.shape[1]
    hid = W.shape[1] // 2
    cut = fw // 128 * 128
    tail = fw - cut
    r = D // 8
    wires, moves = Wires(s_sem, r_sem), Moves(l_sem)
    d, z = wires.d, wires.z
    Ws = (Wm0, Wg1, Wg2, Wg3)
    for key, a, b in (("second", second, second_s), ("secondT", secondT, secondT_s), ("gout", gout, gout_s), ("goutT", goutT, goutT_s), ("midway", midway, mlp)):
        moves.add(key, a, b)
    for k in range(4):
        moves.add(f"W{k}", Ws[k], W.at[k % 2])
    moves.add("mine", mine_s, mine)
    moves.add("sec", sec_s, sec)
    moves.add("h1", Hm.at[1, pl.ds(0, r), :], H1)
    moves.add("h2", Hm.at[2], H2)
    moves.add("h3", Hm.at[3], H3)
    slot = jnp.where(z == 0, 0, jnp.where(z == 3, 1, 2))
    used = (z == 0) | (z == 3) | (z == 1 + d % 2)
    n0 = O0.shape[0] // 3
    own_out = wires.local(mine_s.at[pl.ds(0, n0), :], O0.at[pl.ds(pl.multiple_of(slot * n0, 256), n0), :], used)
    share = Sharing(wires, mine_s, O0, ((0, n0),))
    z3 = wires.swap(Zm2, Zm3, z=1)
    g1, g2, g3 = Spreading(wires, Zm2, Wg1), Spreading(wires, Zm2, Wg2), Spreading(wires, Zm3, Wg3)
    exchange = [wires.swap(out_s.at[k % 2], Hm.at[k], dp=1) for k in range(4)]
    sums = [Summing(wires, Hm.at[k], Lm.at[k]) for k in (0, 1)]
    moves.start("second", "W0", "midway", "gout", "goutT", "secondT")
    greet(d, z, MASKS)
    g1.go_on()
    z3[0]()
    sec_s[...] = jnp.zeros_like(sec_s)
    geb[...] = jnp.zeros_like(geb)
    moves.wait("second", "midway")

    def forward(k, tick):
        b = k % 2
        moves.wait(f"W{k}")
        eb = bias_all[k, 0:1, 768:768 + hid]

        @pl.loop(0, TOK // RT)
        def _(i):
            tick(i)
            rows = pl.ds(pl.multiple_of(i * RT, RT), RT)
            act, slope = gelu_parts(nt(second_s[rows, :], W[b, :hid, :]) + eb)
            act_s[b, rows, :] = act.astype(BF)
            slope_s[b, rows, :] = slope.astype(BF)
            mlp[rows, :] += nn(act_s[b, rows, :], W[b, hid:, :])

    def grads(k, half):
        b = k % 2
        for t in range(2):
            q = 4 * t + 1 - half
            lhs = lambda ref: jnp.concatenate([ref[pl.ds(pl.multiple_of((d ^ p) * r, 16), r), :] for p in (q, q + 2)], axis=0)
            place = pl.ds(t * 2 * r, 2 * r)
            ve, vs = nn(lhs(secondT_s), gpre_s[b]), nn(lhs(goutT_s), act_s[b])
            last = jnp.concatenate([ve[:, cut:fw], vs[:, cut:fw], jnp.zeros((2 * r, 128 - 2 * tail), F32)], axis=1)
            to = out_s.at[b] if half == 0 else Hm.at[k]
            for lo, v in ((0, ve[:, :cut]), (cut, vs[:, :cut]), (2 * cut, last)):
                n = v.shape[1]
                if half:
                    v = v + to[place, lo:lo + n].astype(F32)
                to[place, lo:lo + n] = v.astype(BF)

    def back_a(k, tick):
        b = k % 2

        @pl.loop(0, TOK // RT)
        def _(i):
            tick(i)
            rows = pl.ds(pl.multiple_of(i * RT, RT), RT)
            gp = nt(gout_s[rows, :], W[b, hid:, :]) * slope_s[b, rows, :].astype(F32)
            geb[k] += jnp.sum(gp, axis=0, keepdims=True)
            gpre_s[b, rows, :] = gp.astype(BF)

        grads(k, 0)
        exchange[k][0]()

        @pl.loop(0, TOK // RT)
        def _(i):
            tick(i + 3)
            rows = pl.ds(pl.multiple_of(i * RT, RT), RT)
            sec_s[rows, :] += nn(gpre_s[b, rows, :], W[b, :hid, :])

    def back_b(k):
        exchange[k][1]()
        grads(k, 1)

    def ticks(table):
        def tick(i):
            for n, actions in table.items():
                def run():
                    for a in actions:
                        a()
                pl.when(i == n)(run)
        return tick

    none = ticks({})
    forward(0, ticks({2: [g2.step0]}))
    moves.wait("gout", "goutT", "secondT")
    back_a(0, ticks({2: [g1.step2]}))
    g1.finish(False)
    moves.start("W1")
    forward(1, ticks({1: [g2.step1], 2: [z3[1], g3.step0]}))
    back_b(0)
    back_a(1, ticks({1: [g2.step2], 4: [g3.step1]}))
    g2.finish()
    moves.start("W2")
    forward(2, ticks({2: [g3.step2]}))
    back_b(1)
    g3.finish()
    moves.start("W3")
    sums[0].step1()
    forward(3, none)

    @pl.loop(0, TOK // RT)
    def _(i):
        rows = pl.ds(pl.multiple_of(i * RT, RT), RT)
        mine_s[rows, :] = ((mlp[rows, :] + shrink_b[...]) * live[...]).astype(BF)
        pl.when(i == 0)(lambda: share.start(0, 0))

    own_out[0]()
    moves.start("mine")
    sums[1].step1()
    back_a(2, ticks({4: [lambda: share.on(0, 1), sums[0].step2]}))
    back_a(3, ticks({4: [sums[0].step3, lambda: share.on(0, 2)]}))
    sums[1].step2()
    moves.start("sec")
    back_b(2)
    moves.start("h2")
    back_b(3)
    moves.start("h3")
    sums[1].step3()
    moves.start("h1")
    part_sum[...] = Hm[0, :r, :]
    share.wait(0, 2)
    own_out[1]()
    moves.wait("h1", "h2", "h3", "sec", "mine")


def middle(number, fw, live, shrink_b, bias_all, second, secondT, gout, goutT, midway, Wm0, Wm1, Zm2):
    D = second.shape[1]
    cm, hid = Wm0.shape[0], Wm0.shape[0] // 2
    cg = fw // 128 * 256 + 128
    r = D // 8
    n0 = OUT_CHUNKS[0][0]
    vm = pltpu.VMEM
    dma = pltpu.SemaphoreType.DMA
    got = pl.pallas_call(
        functools.partial(middle_kernel, fw),
        out_shape=(shape((TOK, D), BF), shape((TOK, D), F32), shape((3 * n0, D), BF), shape((r, cg), BF), shape((4 * r, cg), BF), shape((4 * r, cg), BF), shape((4, 1, hid), F32), shape((r, cg), BF),
                   shape((cm, D), BF), shape((cm, D), BF), shape((cm // 8, D), BF), shape((cm, D), BF)),
        in_specs=[VM] * 3 + [HB] * 8,
        out_specs=(HB,) * 6 + (VM,) * 2 + (HB,) * 4,
        input_output_aliases={9: 11},
        scratch_shapes=[vm((TOK, D), BF), vm((D, TOK), BF), vm((TOK, D), BF), vm((D, TOK), BF), vm((TOK, D), F32), vm((TOK, D), F32), vm((TOK, D), BF), vm((2, cm, D), BF),
                        vm((2, TOK, hid), BF), vm((2, TOK, hid), BF), vm((2, TOK, hid), BF), vm((2, 4 * r, cg), BF),
                        vm((4, 4 * r, cg), BF), vm((2, 3 * r, cg), BF), dma((32,)), dma((72,)), dma((72,))],
        compiler_params=pltpu.CompilerParams(vmem_limit_bytes=63 * 2**20, collective_id=number, has_side_effects=True),
        cost_estimate=pl.CostEstimate(flops=4 * 2 * 9 * TOK * D * fw, bytes_accessed=60 * 2**20, transcendentals=4 * TOK * fw),
        name="middle",
    )(live, shrink_b, bias_all, second, secondT, gout, goutT, midway, Wm0, Wm1, Zm2)
    return got[:8]


class General:
    def __init__(self, groups, attn_own, mlp_own):
        self.groups = groups
        self.attn, self.mlp = self.spread(attn_own), self.spread(mlp_own)

    def vectors(self, own):
        every = lax.all_gather(own, "tensor")
        return [every[i] for i in range(self.groups)]

    def spread(self, own):
        d, count = lax.axis_index("dp"), lax.axis_size("dp")
        rows = own.shape[0] // count
        piece = lax.dynamic_slice_in_dim(own, d * rows, rows, 0)
        piece = lax.all_gather(piece, "tensor")
        whole = lax.all_gather(piece, "dp", axis=1, tiled=True)
        return [whole[i] for i in range(self.groups)]

    def reduce(self, parts):
        part = lax.psum_scatter(jnp.stack(parts), "dp", scatter_dimension=1, tiled=True)
        return lax.psum_scatter(part, "tensor", scatter_dimension=0, tiled=True)[0].astype(F32)

    def collect(self, grad_attn, grad_mlp):
        return self.reduce(grad_attn), self.reduce(grad_mlp)

    def by_index(self, items):
        return jnp.stack(items)

    def share(self, mine):
        every = lax.all_gather(mine, "tensor")
        middle = 1 + lax.axis_index("dp") % 2
        return jnp.stack([every[0], every[self.groups - 1], lax.dynamic_index_in_dim(every, middle, 0, keepdims=False)])


def shards(images, counts, cotangent, query_w, query_b, key_w, value_w, value_b, out_w, out_b, norm1_gain, norm1_shift,
           norm2_gain, norm2_shift, expand_w, expand_b, shrink_w, shrink_b):
    slots, length, width = images.shape
    groups = lax.axis_size("tensor")
    d, z = lax.axis_index("dp"), lax.axis_index("tensor")
    cw, fw = query_w.shape[1], expand_w.shape[1]
    heads = cw // HD
    cut = fw // 128 * 128
    slot, used = slot_table(d, groups)
    live = jnp.where(used & (slot < counts[0]), 1.0, 0.0).astype(F32)
    pad = lambda a: jnp.pad(a, ((0, TOK - length), (0, 0)))

    x_low = pad(lax.dynamic_index_in_dim(images, slot, 0, keepdims=False))
    gout = pad(lax.dynamic_index_in_dim(cotangent, slot, 0, keepdims=False)) * live.astype(BF)
    gout_t = gout.T
    if (groups, lax.axis_size("dp")) == (4, 8):
        one = lambda a: a[None]
        blank = lambda n: jnp.zeros((n,), F32)
        bias_own = jnp.concatenate([query_b, blank(384 - cw), value_b, blank(384 - cw), expand_b, blank(1280 - fw)])
        deep = -fw % 16
        mlp_own = jnp.pad(jnp.stack([expand_w.T, shrink_w]), ((0, 0), (0, deep), (0, 0))).reshape(2 * (fw + deep), width)
        qkvs, atts, lses, (first_t, second, second_t, midway), attn_ws, mlp_ws, tops, bias_all = front(
            0, one(norm1_gain), one(norm1_shift), one(norm2_gain), one(norm2_shift), one(out_b), jnp.broadcast_to(bias_own, (8, 2048)),
            x_low, query_w.T, key_w.T, value_w.T, out_w, mlp_own, length)
        mine, sec, out_low, h1, h2, h3, geb, part_sum = middle(1, fw, live[None, None], one(shrink_b), bias_all, second, second_t, gout, gout_t, midway, mlp_own, *mlp_ws)
        out_high, in_all, sum_attn, sum_mlp, vec = back(
            2, one(norm1_gain), one(norm2_gain), live[None, None], geb, jnp.where(live > 0.0, tops[:, :, 0], -1e30)[:, None],
            gout, midway, sec, first_t, x_low, mine, part_sum, h1, h2, h3, qkvs, atts, lses, attn_ws, length)
        outputs = jnp.concatenate([out_low.reshape(3, -1, width), out_high.reshape(3, -1, width)], axis=1)[:, :length]
        input_grads = in_all.reshape(3, TOK, width)[:, :length].astype(F32)
        own = lax.dynamic_index_in_dim(vec, z, 0, keepdims=False)
        grad_query_b, grad_value_b, grad_expand_b, logit_top = own[:cw], own[384:384 + cw], own[768:768 + fw], own[1920:1920 + heads]
        tail = [vec[4 + i, :width] for i in range(6)]
    else:
        attn_own = jnp.concatenate([query_w, key_w, value_w, out_w.T], axis=1)
        shrink_t = shrink_w.T
        mlp_own = jnp.concatenate([expand_w[:, :cut], shrink_t[:, :cut], expand_w[:, cut:], shrink_t[:, cut:]], axis=1)
        net = General(groups, attn_own, mlp_own)
        biases = net.vectors(jnp.concatenate([query_b, value_b, expand_b]))

        x = x_low.astype(F32)
        normed1, inverse1 = normalize(x)
        first = (normed1 * norm1_gain + norm1_shift).astype(BF)
        first_t = first.T
        acc = x + out_b
        kept, tops = [], []
        for k in range(groups):
            b = biases[k]
            qkv, att, lse, top, acc = attn_fwd(first, net.attn[k], b[None, :cw], b[None, cw:2 * cw], acc, length)
            kept.append((qkv, att, lse))
            tops.append(top[:, 0])
        midway = acc
        normed2, inverse2 = normalize(midway)
        second = (normed2 * norm2_gain + norm2_shift).astype(BF)
        second_t = second.T
        mlp = midway + shrink_b
        sec = jnp.zeros((TOK, width), F32)
        grad_mlp, geb = [], []
        for k in range(groups):
            grad, g_b, mlp, sec = mlp_call(second, second_t, gout, gout_t, net.mlp[k], biases[k][None, 2 * cw:], mlp, sec)
            grad_mlp.append(grad)
            geb.append(g_b[0, :fw])
        back2, gn2g, gn2s = norm_back(sec, normed2, inverse2, norm2_gain)
        gout32 = gout.astype(F32)
        gmid = gout32 + back2
        gmid_low = gmid.astype(BF)
        gmid_t = gmid_low.T
        acc = jnp.zeros((TOK, width), F32)
        grad_attn, gqb, gvb = [None] * groups, [None] * groups, [None] * groups
        for k in reversed(range(groups)):
            grad, g_q, g_v, acc = attn_bwd(gmid_low, gmid_t, first_t, net.attn[k], *kept[k], acc, length)
            grad_attn[k], gqb[k], gvb[k] = grad, g_q[0], g_v[0]
        back1, gn1g, gn1s = norm_back(acc, normed1, inverse1, norm1_gain)
        input_grad = ((gmid + back1) * live)[:length].astype(BF)

        outputs = net.share((mlp[:length] * live).astype(BF))
        input_grads = net.share(input_grad).astype(F32)
        sum_attn, sum_mlp = net.collect(grad_attn, grad_mlp)
        flat = lambda items: net.by_index(items).reshape(-1)
        vector = jnp.concatenate([flat(gqb), flat(gvb), flat(geb), jnp.sum(gmid, axis=0), jnp.sum(gout32, axis=0), gn1g, gn1s, gn2g, gn2s])
        vector = lax.psum(vector, ("dp", "tensor"))
        part = lambda start, size: lax.dynamic_slice_in_dim(vector, start, size, 0)
        whole, hidden = cw * groups, fw * groups
        tail = [vector[2 * whole + hidden + i * width:][:width] for i in range(6)]
        logit_top = lax.pmax(jnp.where(live > 0.0, net.by_index(tops), -1e30), ("dp", "tensor"))
        logit_top = lax.dynamic_index_in_dim(logit_top, z, 0, keepdims=False)
        grad_query_b, grad_value_b, grad_expand_b = part(z * cw, cw), part(whole + z * cw, cw), part(2 * whole + z * fw, fw)
    factor = jnp.sqrt(clip_limit / jnp.maximum(logit_top, clip_limit))
    column_factor = jnp.repeat(factor, HD)
    clipped_query = (query_w.astype(F32) * column_factor).astype(BF)
    clipped_key = (key_w.astype(F32) * column_factor).astype(BF)
    unpack = lambda a, i: jnp.concatenate([a[:, i * cut:(i + 1) * cut], a[:, 2 * cut + i * (fw - cut):][:, :fw - cut]], axis=1)
    return (outputs, input_grads, sum_attn[:, :cw], grad_query_b, sum_attn[:, cw:2 * cw], sum_attn[:, 2 * cw:3 * cw], grad_value_b,
            sum_attn[:, 3 * cw:].T, tail[0], tail[2], tail[3], tail[4], tail[5], unpack(sum_mlp, 0), grad_expand_b, unpack(sum_mlp, 1).T,
            tail[1], clipped_query, clipped_key)


def solution(mesh):
    columns, rows, vector = P(None, "tensor"), P("tensor", None), P("tensor")
    whole = P("dp", None, None)
    return jax.shard_map(
        shards, mesh=mesh,
        in_specs=(whole, P("dp"), whole, columns, vector, columns, columns, vector, rows, P(), P(), P(), P(), P(), columns, vector, rows, P()),
        out_specs=(whole, whole, P("dp", "tensor"), vector, P("dp", "tensor"), P("dp", "tensor"), vector, P("tensor", "dp"), P(), P(), P(), P(), P(),
                   P("dp", "tensor"), vector, P("tensor", "dp"), P(), columns, columns),
        check_vma=False)
```

```python
import functools
import math

import jax
import jax.numpy as jnp
from jax import lax
from jax.experimental import pallas as pl
from jax.experimental.pallas import tpu as pltpu
from jax.sharding import PartitionSpec as P

HD = 72
TOK = 768
RT = 256
SC = 1 / math.sqrt(HD)
LOG2E = 1.4426950408889634
F32 = jnp.float32
BF = jnp.bfloat16
norm_eps = 1e-06
clip_limit = 3.0
tanh_coef = 0.7978845608028654
cube_coef = 0.044715
VM = pl.BlockSpec(memory_space=pltpu.VMEM)
HB = pl.BlockSpec(memory_space=pl.ANY)
MESH = pl.DeviceIdType.MESH


def nn(a, b):
    return jnp.dot(a, b, preferred_element_type=F32)


def nt(a, b):
    return lax.dot_general(a, b, (((1,), (1,)), ((), ())), preferred_element_type=F32)


def tn(a, b):
    return lax.dot_general(a, b, (((0,), (0,)), ((), ())), preferred_element_type=F32)


def shape(dims, dtype):
    return jax.ShapeDtypeStruct(dims, dtype)


def cut_rows(rows):
    first = (rows // 2 + 15) // 16 * 16
    return first, rows - first


def block_rows(lhs, rhs, half, write):
    if half is None:
        @pl.loop(0, lhs.shape[0] // 384)
        def _(t):
            place = pl.ds(pl.multiple_of(t * 384, 128), 384)
            write(place, nn(lhs[place, :], rhs[...]))
    else:
        rows = lhs.shape[0] // 8
        d = lax.axis_index("dp")

        @pl.loop(0, 2)
        def _(t):
            r = 4 * t + 1 - half
            both = [lhs[pl.ds(pl.multiple_of((d ^ q) * rows, 16), rows), :] for q in (r, r + 2)]
            write(pl.ds(pl.multiple_of(t * 2 * rows, 16), 2 * rows), nn(jnp.concatenate(both, axis=0), rhs[...]))


def attn_fwd_kernel(length, heads, first, qb, vb, acc_in, W, qkv, att, lse, tops, acc):
    cw = heads * HD

    @pl.loop(0, TOK // RT)
    def _(i):
        rows = pl.ds(pl.multiple_of(i * RT, RT), RT)
        t = nn(first[rows, :], W[:, :3 * cw])
        q = (t[:, :cw] + qb[...]).astype(BF)
        k = t[:, cw:2 * cw].astype(BF)
        v = (t[:, 2 * cw:] + vb[...]).astype(BF)
        for h in range(heads):
            qkv[h, rows, :] = q[:, h * HD:(h + 1) * HD]
            qkv[heads + h, rows, :] = k[:, h * HD:(h + 1) * HD]
            qkv[2 * heads + h, rows, :] = v[:, h * HD:(h + 1) * HD]

    tops[...] = jnp.full(tops.shape, -1e30, F32)

    @pl.loop(0, TOK // RT)
    def _(i):
        rows = pl.ds(pl.multiple_of(i * RT, RT), RT)
        rid = lax.broadcasted_iota(jnp.int32, (RT, 1), 0) + i * RT
        cid = lax.broadcasted_iota(jnp.int32, (1, TOK), 1)
        res = []
        for h in range(heads):
            s = nt(qkv[h, rows, :], qkv[heads + h])
            s = jnp.where(cid < length, s, -1e30)
            m = jnp.max(s, axis=1, keepdims=True)
            e = jnp.exp2((s - m) * (SC * LOG2E))
            l = jnp.sum(e, axis=1, keepdims=True)
            o = nn(e.astype(BF), qkv[2 * heads + h]) * (1.0 / l)
            res.append(o.astype(BF))
            lse[rows, h:h + 1] = m * (SC * LOG2E) + jnp.log2(l)
            tops[h:h + 1, :] = jnp.maximum(tops[h:h + 1, :], jnp.max(jnp.where(rid < length, m, -1e30)) * SC)
        a = jnp.concatenate(res, axis=1)
        att[rows, :] = a
        acc[rows, :] = acc_in[rows, :] + nt(a, W[:, 3 * cw:])


def attn_fwd(first, W, qb, vb, acc, length):
    D = first.shape[1]
    cw = W.shape[1] // 4
    heads = cw // HD
    return pl.pallas_call(
        functools.partial(attn_fwd_kernel, length, heads),
        out_shape=(shape((3 * heads, TOK, HD), BF), shape((TOK, cw), BF), shape((TOK, 128), F32), shape((heads, 128), F32), shape((TOK, D), F32)),
        in_specs=[VM] * 5,
        out_specs=(VM,) * 5,
        compiler_params=pltpu.CompilerParams(vmem_limit_bytes=44 * 2**20),
        cost_estimate=pl.CostEstimate(flops=2 * TOK * (D * cw * 4 + heads * 2 * TOK * HD * 6), bytes_accessed=25 * 2**20, transcendentals=heads * TOK * TOK),
        name="attn_fwd",
    )(first, qb, vb, acc, W)


def gelu_parts(u):
    u2 = u * u
    t = jnp.tanh(u * (tanh_coef + (tanh_coef * cube_coef) * u2))
    hu = 0.5 * (1.0 + t)
    return u * hu, hu + u * (0.5 * tanh_coef) * (1.0 - t * t) * (1.0 + (3.0 * cube_coef) * u2)


def mlp_kernel(fw, second, secondT, gout, goutT, eb, mlp_in, sec_in, W, G, geb, mlp, sec, E, ST, act_s, gpre_s):
    cut = fw // 128 * 128
    tail = fw - cut
    E[:, :cut] = W[:, :cut]
    ST[:, :cut] = W[:, cut:2 * cut]
    last = W[:, 2 * cut:]
    blank = jnp.zeros((last.shape[0], 128 - tail), BF)
    E[:, cut:] = jnp.concatenate([last[:, :tail], blank], axis=1)
    ST[:, cut:] = jnp.concatenate([last[:, tail:], blank], axis=1)
    geb[...] = jnp.zeros_like(geb)

    @pl.loop(0, TOK // RT)
    def _(i):
        rows = pl.ds(pl.multiple_of(i * RT, RT), RT)
        act, slope = gelu_parts(nn(second[rows, :], E[...]) + eb[...])
        act_s[rows, :] = act.astype(BF)
        gp = nn(gout[rows, :], ST[...]) * slope
        geb[...] += jnp.sum(gp, axis=0, keepdims=True)
        gpre_s[rows, :] = gp.astype(BF)
        mlp[rows, :] = mlp_in[rows, :] + nt(act_s[rows, :], ST[...])
        sec[rows, :] = sec_in[rows, :] + nt(gpre_s[rows, :], E[...])

    def write(lo, last):
        def put(place, v):
            v = v.astype(BF)
            G[place, lo:lo + cut] = v[:, :cut]
            G[place, last:last + tail] = v[:, cut:fw]
        return put

    block_rows(secondT, gpre_s, None, write(0, 2 * cut))
    block_rows(goutT, act_s, None, write(cut, 2 * cut + tail))


def mlp_call(second, secondT, gout, goutT, W, eb, mlp, sec):
    D = second.shape[1]
    fw = W.shape[1] // 2
    wide = fw // 128 * 128 + 128
    eb = jnp.pad(eb, ((0, 0), (0, wide - fw)))
    return pl.pallas_call(
        functools.partial(mlp_kernel, fw),
        out_shape=(shape((D, 2 * fw), BF), shape((1, wide), F32), shape((TOK, D), F32), shape((TOK, D), F32)),
        in_specs=[VM] * 8,
        out_specs=(VM,) * 4,
        scratch_shapes=[pltpu.VMEM((D, wide), BF)] * 2 + [pltpu.VMEM((TOK, wide), BF)] * 2,
        compiler_params=pltpu.CompilerParams(vmem_limit_bytes=56 * 2**20),
        cost_estimate=pl.CostEstimate(flops=2 * 9 * TOK * D * fw, bytes_accessed=35 * 2**20, transcendentals=TOK * fw),
        name="mlp",
    )(second, secondT, gout, goutT, eb, mlp, sec, W)


def attn_bwd_kernel(length, heads, gmid, gmidT, firstT, qkv, att, lse, acc_in, W, G, gqb, gvb, acc, ga_s, d_s, dk_s, dv_s):
    cw = heads * HD

    @pl.loop(0, TOK // RT)
    def _(i):
        rows = pl.ds(pl.multiple_of(i * RT, RT), RT)
        g = nn(gmid[rows, :], W[:, 3 * cw:]).astype(BF)
        for h in range(heads):
            ga_s[h, rows, :] = g[:, h * HD:(h + 1) * HD]

    gqb[...] = jnp.zeros_like(gqb)
    dk_s[...] = jnp.zeros_like(dk_s)
    dv_s[...] = jnp.zeros_like(dv_s)

    @pl.loop(0, TOK // RT)
    def _(i):
        rows = pl.ds(pl.multiple_of(i * RT, RT), RT)
        cid = lax.broadcasted_iota(jnp.int32, (1, TOK), 1)
        dqs = []
        for h in range(heads):
            q, k, v, g = qkv[h, rows, :], qkv[heads + h], qkv[2 * heads + h], ga_s[h, rows, :]
            s = nt(q, k)
            p = jnp.exp2(s * (SC * LOG2E) - lse[rows, h:h + 1])
            p = jnp.where(cid < length, p, 0.0)
            dp = nt(g, v)
            dd = jnp.sum(g.astype(F32) * att[rows, h * HD:(h + 1) * HD].astype(F32), axis=1, keepdims=True)
            ds = (p * (dp - dd)).astype(BF)
            dqs.append(nn(ds, k) * SC)
            dk_s[h] += tn(ds, q)
            dv_s[h] += tn(p.astype(BF), g)
        dq = jnp.concatenate(dqs, axis=1)
        gqb[...] += jnp.sum(dq, axis=0, keepdims=True)
        d_s[rows, :cw] = dq.astype(BF)

    dk = jnp.concatenate([dk_s[h] * SC for h in range(heads)], axis=1)
    d_s[:, cw:2 * cw] = dk.astype(BF)
    dv = jnp.concatenate([dv_s[h] for h in range(heads)], axis=1)
    gvb[...] = jnp.sum(dv, axis=0, keepdims=True)
    d_s[:, 2 * cw:] = dv.astype(BF)

    @pl.loop(0, TOK // RT)
    def _(i):
        rows = pl.ds(pl.multiple_of(i * RT, RT), RT)
        acc[rows, :] = acc_in[rows, :] + nt(d_s[rows, :], W[:, :3 * cw])

    def write(lo, hi):
        def put(place, v):
            G[place, lo:hi] = v.astype(BF)
        return put

    block_rows(firstT, d_s, None, write(0, 3 * cw))
    block_rows(gmidT, att, None, write(3 * cw, 4 * cw))


def attn_bwd(gmid, gmidT, firstT, W, qkv, att, lse, acc, length):
    D = gmid.shape[1]
    cw = W.shape[1] // 4
    heads = cw // HD
    return pl.pallas_call(
        functools.partial(attn_bwd_kernel, length, heads),
        out_shape=(shape((D, 4 * cw), BF), shape((1, cw), F32), shape((1, cw), F32), shape((TOK, D), F32)),
        in_specs=[VM] * 8,
        out_specs=(VM,) * 4,
        scratch_shapes=[pltpu.VMEM((heads, TOK, HD), BF), pltpu.VMEM((TOK, 3 * cw), BF), pltpu.VMEM((heads, TOK, HD), F32), pltpu.VMEM((heads, TOK, HD), F32)],
        compiler_params=pltpu.CompilerParams(vmem_limit_bytes=52 * 2**20),
        cost_estimate=pl.CostEstimate(flops=2 * TOK * (D * cw * 8 + heads * 5 * TOK * HD * 6), bytes_accessed=30 * 2**20, transcendentals=heads * TOK * TOK),
        name="attn_bwd",
    )(gmid, gmidT, firstT, qkv, att, lse, acc, W)


def normalize(values):
    centre = jnp.mean(values, axis=-1, keepdims=True)
    centred = values - centre
    spread = jnp.mean(centred * centred, axis=-1, keepdims=True)
    inverse = lax.rsqrt(spread + norm_eps)
    return centred * inverse, inverse


def norm_back(grad_norm, normed, inverse, gain):
    scaled = grad_norm * gain
    first_mean = jnp.mean(scaled, axis=-1, keepdims=True)
    second_mean = jnp.mean(scaled * normed, axis=-1, keepdims=True)
    grad_input = inverse * (scaled - first_mean - normed * second_mean)
    return grad_input, jnp.sum(grad_norm * normed, axis=0), jnp.sum(grad_norm, axis=0)


def slot_table(d, groups):
    z = lax.axis_index("tensor")
    middle = 1 + d % 2
    return jnp.where(z == 0, 0, jnp.where(z == groups - 1, 1, 2)), (z == 0) | (z == groups - 1) | (z == middle)


HOPS = {
    "u1": (1, ((0, None),)), "u2": (3, ((1, None),)), "u3": (1, ((2, None),)),
    "w1": (1, ((3, None),)), "w2": (3, ((2, None),)), "w3": (1, ((1, None),)),
    "v1": (3, ((1, 0), (2, 1))), "v2": (1, ((2, 0), (1, 1))), "v3": (1, ((1, 0), (2, 1))),
}
HOP_FROM = {"u1": "me", "u2": "u1", "u3": "u2", "w1": "me", "w2": "w1", "w3": "w2", "v1": "me", "v2": "v1", "v3": "me"}
NAMES = ("u1", "w1", "v1", "v3"), ("u2", "w2", "v2"), ("u3", "w3")
BEGIN = {"u": 0, "w": 1, "v": 2}


class Wires:
    def __init__(self, s_sem, r_sem):
        self.s, self.r, self.n = s_sem, r_sem, 0
        self.d, self.z = lax.axis_index("dp"), lax.axis_index("tensor")

    def local(self, src, dst, used):
        i = self.n
        self.n += 1
        make = lambda: pltpu.make_async_copy(src, dst, self.s.at[i])
        return (lambda: pl.when(used)(lambda: make().start())), (lambda: pl.when(used)(lambda: make().wait()))

    def swap(self, src, dst, dp=0, z=0, sends=None):
        i = self.n
        self.n += 1
        make = lambda: pltpu.make_async_remote_copy(src_ref=src, dst_ref=dst, send_sem=self.s.at[i], recv_sem=self.r.at[i], device_id=(self.d ^ dp, self.z ^ z), device_id_type=MESH)
        if sends is None:
            return (lambda: make().start()), (lambda: make().wait())

        def any_of(z_here):
            hit = None
            for zz, cc in sends:
                this = z_here == zz
                if cc is not None:
                    this = this & (self.d % 2 == cc)
                hit = this if hit is None else hit | this
            return hit

        def start():
            pl.when(any_of(self.z))(lambda: make().start())

        def wait():
            pl.when(any_of(self.z))(lambda: make().wait_send())
            pl.when(any_of(self.z ^ z))(lambda: make().wait_recv())

        return start, wait


def greet(d, z, masks):
    sem = pltpu.get_barrier_semaphore()
    for dp, t in masks:
        pl.semaphore_signal(sem, inc=1, device_id=(d ^ dp, z ^ t), device_id_type=MESH)
    pl.semaphore_wait(sem, len(masks))


class Summing:
    def __init__(self, wires, H, land):
        self.H = H
        self.rows = r = H.shape[0] // 4
        self.one, self.two = one, two = cut_rows(r)
        ax, by = land.at[pl.ds(0, 2 * one), :], land.at[pl.ds(2 * one, 2 * two), :]
        ay, bx = land.at[pl.ds(2 * r, one), :], land.at[pl.ds(2 * r + one, two), :]
        self.land = land
        h = lambda lo, n: H.at[pl.ds(lo, n), :]
        at = lambda ref, lo, n: ref.at[pl.ds(lo, n), :]
        self.c1 = [wires.swap(h(r, one), at(land, 0, one), dp=2), wires.swap(h(3 * r, one), at(land, one, one), dp=2),
                   wires.swap(h(2 * r + one, two), at(land, 2 * one, two), dp=4), wires.swap(h(3 * r + one, two), at(land, 2 * one + two, two), dp=4)]
        self.c2 = [wires.swap(h(2 * r, one), ay, dp=4), wires.swap(h(r + one, two), bx, dp=2)]

    def add(self, lo, n, *froms):
        total = self.H[lo:lo + n, :].astype(F32)
        for f in froms:
            total = total + self.land[f:f + n, :].astype(F32)
        self.H[lo:lo + n, :] = total.astype(BF)

    def step1(self):
        for s, _ in self.c1:
            s()

    def step2(self):
        r, one, two = self.rows, self.one, self.two
        for _, w in self.c1:
            w()
        self.add(2 * r, one, one)
        self.add(r + one, two, 2 * one + two)
        for s, _ in self.c2:
            s()

    def step3(self):
        r, one, two = self.rows, self.one, self.two
        for _, w in self.c2:
            w()
        self.add(0, one, 0, 2 * r)
        self.add(one, two, 2 * one, 2 * r + one)


ENDS = ((0, None), (3, None))
INNER = ((1, None), (2, None))


class LineSum:
    def __init__(self, wires, parts, land):
        self.parts, self.land = parts, land
        self.inner = (wires.z == 1) | (wires.z == 2)
        self.a = {k: wires.swap(parts[k], land.at[k - 1], z=1, sends=ENDS) for k in (1, 2, 3)}
        self.b = [wires.swap(parts[3], land.at[3], z=3, sends=INNER), wires.swap(parts[2], land.at[4], z=3, sends=INNER)]
        self.g = wires.swap(parts[1], land.at[0], z=1, sends=INNER)

    def alpha(self, k):
        self.a[k][0]()

    def add(self, k, i):
        @pl.when(self.inner)
        def _():
            self.parts[k][...] = (self.parts[k][...].astype(F32) + self.land[i].astype(F32)).astype(BF)

    def beta(self):
        self.a[2][1]()
        self.a[3][1]()
        self.add(3, 1)
        self.add(2, 2)
        for s, _ in self.b:
            s()

    def gamma(self):
        for _, w in self.b:
            w()
        self.a[1][1]()
        self.add(1, 4)
        self.g[0]()

    def total(self, own):
        self.g[1]()
        other = jnp.where(self.inner, self.land[3].astype(F32), 0.0)
        return own + self.land[0].astype(F32) + other


class Sharing:
    def __init__(self, wires, mine, O, chunks, base=0):
        self.stages = []
        stride = O.shape[0] // 3
        for lo, n in chunks:
            here = []
            for names in NAMES:
                row = []
                for name in names:
                    mask, sends = HOPS[name]
                    place = O.at[pl.ds(BEGIN[name[0]] * stride + lo - base, n), :]
                    row.append(wires.swap(mine.at[pl.ds(lo, n), :] if HOP_FROM[name] == "me" else place, place, z=mask, sends=sends))
                here.append(row)
            self.stages.append(here)

    def start(self, chunk, stage):
        for s, _ in self.stages[chunk][stage]:
            s()

    def wait(self, chunk, stage):
        for _, w in self.stages[chunk][stage]:
            w()

    def on(self, chunk, stage):
        self.wait(chunk, stage - 1)
        self.start(chunk, stage)


OUT_CHUNKS = ((0, 256), (256, 256), (512, 224))
IN_CHUNKS = ((0, 128), (128, 128), (256, 128), (384, 128), (512, 128), (640, 96))
MASKS = [(1, 0), (2, 0), (4, 0), (0, 1), (0, 2), (0, 3)]
COPIES = 180


LATE = 2


def back_kernel(length, heads, vectors, live, geb, tops, gout, midway, sec, firstT, x, mine, whole0, h1, h2, h3, O_low, *rest):
    gain1, gain2 = vectors[0:1, :], vectors[2:3, :]
    Ws, qkvs, atts, lses, rest = rest[:4], rest[4:8], rest[8:12], rest[12:16], rest[16:]
    (O_out, O_in, sum_a, sum_m, vec, g_s, gm_s, acc, gT, fT, x_s, W_s, qkv_s, att_s, lse_s, ga_s, d_s, dk_s, dv_s, out_s,
     Ha, La, Hm, Lm, za, zm, vr, w0_s, w1_s, l_sem, s_sem, r_sem) = rest
    cw = heads * HD
    D = g_s.shape[1]
    wires = Wires(s_sem, r_sem)
    d, z = wires.d, wires.z
    loads = {}
    order = [3, 2, 1, 0]
    names = iter(range(100))

    def load(key, src, dst):
        loads[key] = pltpu.make_async_copy(src, dst, l_sem.at[next(names)])

    load("midway", midway, acc)
    load("sec", sec, gm_s)
    load("gout", gout, g_s)
    load("firstT", firstT, fT)
    load("x", x, x_s)
    load("h2", h2, Hm.at[0])
    load("h3", h3, Hm.at[1])
    load("w0", whole0, w0_s)
    load("w1", h1, w1_s)
    for i, k in enumerate(order):
        b = i % 2
        load(f"W{i}", Ws[k], W_s.at[b])
        load(f"qkv{i}", qkvs[k], qkv_s.at[b])
        load(f"att{i}", atts[k], att_s.at[b])
        load(f"lse{i}", lses[k], lse_s.at[b])
    for key in ("midway", "sec", "gout", "h2", "h3", "w1", "w0", "firstT", "W0", "qkv0", "att0", "lse0", "x"):
        loads[key].start()
    slot = jnp.where(z == 0, 0, jnp.where(z == 3, 1, 2))
    own_place = pl.ds(pl.multiple_of(slot * TOK, 256), TOK)
    used = (z == 0) | (z == 3) | (z == 1 + d % 2)
    own_in = wires.local(g_s, O_in.at[own_place, :], used)
    share_out = Sharing(wires, mine, O_out, OUT_CHUNKS)
    share_in = Sharing(wires, g_s, O_in, IN_CHUNKS)
    sums = {"m2": Summing(wires, Hm.at[0], Lm.at[0]), "m3": Summing(wires, Hm.at[1], Lm.at[1])}
    for k in range(4):
        sums[f"b{k}"] = Summing(wires, Ha.at[k], La.at[k])
    r = sum_a.shape[0]
    top = pl.ds(0, r)
    line_m = LineSum(wires, [None, w1_s, Hm.at[0, top, :], Hm.at[1, top, :]], zm)
    line_b = LineSum(wires, [Ha.at[k, top, :] for k in range(4)], za)
    exchange = {k: wires.swap(out_s, Ha.at[k], dp=1) for k in range(4)}
    spread = [wires.swap(vec, vr.at[i], dp=dp, z=t) for i, (dp, t) in enumerate(((1, 0), (2, 0), (4, 0), (0, 1), (0, 2)))]
    greet(d, z, MASKS)

    todo = {
        -3: [lambda: share_out.start(0, 1), lambda: share_out.start(1, 1), lambda: share_out.start(2, 0)],
        -2: [lambda: loads["h2"].wait(), sums["m2"].step1, lambda: loads["w1"].wait(), lambda: line_m.alpha(1)],
        0: [lambda: loads["h3"].wait(), lambda: loads["w0"].wait()],
        5: [sums["m2"].step2, sums["m3"].step1],
        8: [lambda: share_out.on(0, 2), lambda: share_out.on(2, 1)],
        10: [sums["m2"].step3, lambda: line_m.alpha(2)],
        15: [sums["m3"].step2],
        18: [lambda: share_out.on(1, 2), sums["b3"].step2],
        20: [sums["m3"].step3, lambda: line_m.alpha(3)],
        22: [sums["b3"].step3, lambda: line_b.alpha(3)],
        25: [line_m.beta],
        28: [lambda: share_out.on(2, 2), sums["b2"].step2],
        33: [sums["b2"].step3, lambda: line_b.alpha(2)],
        38: [line_m.gamma],
    }

    def tick(t):
        for action in todo.get(t, ()):
            action()

    vec[...] = jnp.zeros_like(vec)
    for key in ("midway", "sec", "gout"):
        loads[key].wait()

    def total_of(row, value):
        vec[row:row + 1, :D] += jnp.sum(value, axis=0, keepdims=True)

    def put_row(where, lo, value):
        n = value.shape[1]
        hit = lax.broadcasted_iota(jnp.int32, (8, n), 0) == where
        vec[0:8, lo:lo + n] += jnp.where(hit, jnp.broadcast_to(value, (8, n)), 0.0)

    @pl.loop(0, TOK // RT)
    def _(i):
        for t in range(3):
            pl.when(i == t)(functools.partial(tick, t - 3))
        rows = pl.ds(pl.multiple_of(i * RT, RT), RT)
        normed, inverse = normalize(acc[rows, :])
        e = gm_s[rows, :]
        go = g_s[rows, :].astype(F32)
        scaled = e * gain2
        mean1 = jnp.mean(scaled, axis=-1, keepdims=True)
        mean2 = jnp.mean(scaled * normed, axis=-1, keepdims=True)
        gm = go + inverse * (scaled - mean1 - normed * mean2)
        total_of(4, gm)
        total_of(5, go)
        total_of(8, e * normed)
        total_of(9, e)
        gm_s[rows, :] = gm
        g_s[rows, :] = gm.astype(BF)
        gT[:, rows] = gm.T.astype(BF)

    def write(dst, lo, hi, add):
        def put(where, val):
            if add:
                val = val + dst[where, lo:hi].astype(F32)
            dst[where, lo:hi] = val.astype(BF)
        return put

    def give(i):
        k, b = order[i], i % 2
        block_rows(fT, d_s.at[b], 0, write(out_s, 0, 3 * cw, False))
        block_rows(gT, att_s.at[b], 0, write(out_s, 3 * cw, 4 * cw, False))
        exchange[k][0]()

    def keep(i):
        k, b = order[i], i % 2
        exchange[k][1]()
        block_rows(fT, d_s.at[b], 1, write(Ha.at[k], 0, 3 * cw, True))
        block_rows(gT, att_s.at[b], 1, write(Ha.at[k], 3 * cw, 4 * cw, True))

    loads["firstT"].wait()
    acc[...] = jnp.zeros_like(acc)
    for i, k in enumerate(order):
        base, b = 10 * i, i % 2
        W, qkv, att, lse, dd_s = W_s.at[b], qkv_s.at[b], att_s.at[b], lse_s.at[b], d_s.at[b]
        for key in ("W", "qkv", "att", "lse"):
            loads[f"{key}{i}"].wait()
        if i < 3:
            for key in ("W", "qkv", "lse"):
                loads[f"{key}{i + 1}"].start()
        tick(base)

        @pl.loop(0, TOK // RT)
        def _(t):
            rows = pl.ds(pl.multiple_of(t * RT, RT), RT)
            g = nt(g_s[rows, :], W[3 * cw:, :]).astype(BF)
            for h in range(heads):
                ga_s[h, rows, :] = g[:, h * HD:(h + 1) * HD]

        if 1 <= i <= LATE:
            keep(i - 1)
            sums[f"b{order[i - 1]}"].step1()
        if i < 3:
            loads[f"att{i + 1}"].start()
        tick(base + 1)
        dk_s[...] = jnp.zeros_like(dk_s)
        dv_s[...] = jnp.zeros_like(dv_s)
        place = z ^ k

        @pl.loop(0, TOK // RT)
        def _(t):
            for n in range(3):
                pl.when(t == n)(functools.partial(tick, base + 2 + n))
            rows = pl.ds(pl.multiple_of(t * RT, RT), RT)
            cid = lax.broadcasted_iota(jnp.int32, (1, TOK), 1)
            dqs = []
            for h in range(heads):
                q, kk, v, g = qkv[h, rows, :], qkv[heads + h], qkv[2 * heads + h], ga_s[h, rows, :]
                s = nt(q, kk)
                p = jnp.exp2(s * (SC * LOG2E) - lse[rows, h:h + 1])
                p = jnp.where(cid < length, p, 0.0)
                dp = nt(g, v)
                dd = jnp.sum(g.astype(F32) * att[rows, h * HD:(h + 1) * HD].astype(F32), axis=1, keepdims=True)
                ds = (p * (dp - dd)).astype(BF)
                dqs.append(nn(ds, kk) * SC)
                dk_s[h * HD:(h + 1) * HD, :] += tn(q, ds)
                dv_s[h * HD:(h + 1) * HD, :] += tn(g, p.astype(BF))
            dq = jnp.concatenate(dqs, axis=1)
            put_row(place, 0, jnp.sum(dq, axis=0, keepdims=True))
            dd_s[rows, :cw] = dq.astype(BF)

        dd_s[:, cw:2 * cw] = (dk_s[...].T[:, :cw] * SC).astype(BF)
        dv = dv_s[...].T[:, :cw]
        put_row(place, 384, jnp.sum(dv, axis=0, keepdims=True))
        dd_s[:, 2 * cw:] = dv.astype(BF)
        put_row(place, 768, geb[k])
        put_row(place, 1920, tops[k])
        tick(base + 5)

        if i < LATE:
            give(i)
        tick(base + 6)

        @pl.loop(0, TOK // RT)
        def _(t):
            rows = pl.ds(pl.multiple_of(t * RT, RT), RT)
            acc[rows, :] += nn(dd_s[rows, :], W[:3 * cw, :])

        tick(base + 7)
        tick(base + 8)

    loads["x"].wait()

    @pl.loop(0, TOK // RT)
    def _(i):
        rows = pl.ds(pl.multiple_of(i * RT, RT), RT)
        normed, inverse = normalize(x_s[rows, :].astype(F32))
        e = acc[rows, :]
        scaled = e * gain1
        mean1 = jnp.mean(scaled, axis=-1, keepdims=True)
        mean2 = jnp.mean(scaled * normed, axis=-1, keepdims=True)
        total_of(6, e * normed)
        total_of(7, e)
        g_s[rows, :] = ((gm_s[rows, :] + inverse * (scaled - mean1 - normed * mean2)) * live[...]).astype(BF)
        for t in range(3):
            @pl.when(i == t)
            def _():
                share_in.start(2 * t, 0)
                share_in.start(2 * t + 1, 0)

    own_in[0]()
    spread[0][0]()
    give(2)
    after = {
        0: [line_b.beta, lambda: keep(2), sums["b1"].step1, lambda: give(3)],
        1: [lambda: keep(3), sums["b0"].step1],
        2: [sums["b1"].step2],
        3: [sums["b1"].step3, lambda: line_b.alpha(1), sums["b0"].step2],
        4: [sums["b0"].step3],
        5: [line_b.gamma],
    }
    row = lax.broadcasted_iota(jnp.int32, vec.shape, 1)

    def fold(i):
        spread[i][1]()
        a, c = vec[...], vr[i]
        vec[...] = jnp.where(row < 1920, a + c, jnp.maximum(a, c))
        if i < 4:
            spread[i + 1][0]()

    n = len(IN_CHUNKS)
    for t in range(n + 2):
        if t < n:
            share_in.on(t, 1)
        for action in after.get(t, ()):
            action()
        if 1 <= t <= n:
            share_in.on(t - 1, 2)
        if 1 <= t <= 5:
            fold(t - 1)
    for c in range(len(OUT_CHUNKS)):
        share_out.wait(c, 2)
    own_in[1]()
    sum_m[...] = line_m.total(w0_s[...].astype(F32))
    sum_a[...] = line_b.total(Ha[0, :r, :].astype(F32))
    for c in range(n):
        share_in.wait(c, 2)


def back(number, vectors, live, geb, tops, gout, midway, sec, firstT, x, mine, whole0, h1, h2, h3, O_low, qkvs, atts, lses, Ws, length):
    D = gout.shape[1]
    cw = Ws[0].shape[0] // 4
    cm = h2.shape[1]
    heads = cw // HD
    r = D // 8
    vm = pltpu.VMEM
    dma = pltpu.SemaphoreType.DMA
    return pl.pallas_call(
        functools.partial(back_kernel, length, heads),
        out_shape=(shape((3 * TOK, D), BF), shape((3 * TOK, D), BF), shape((r, 4 * cw), F32), shape((r, cm), F32), shape((16, 2048), F32)),
        in_specs=[VM] * 4 + [HB] * 27,
        out_specs=(HB, HB, VM, VM, VM),
        input_output_aliases={14: 0},
        scratch_shapes=[vm((TOK, D), BF), vm((TOK, D), F32), vm((TOK, D), F32), vm((D, TOK), BF), vm((D, TOK), BF), vm((TOK, D), BF),
                        vm((2, 4 * cw, D), BF), vm((2, 3 * heads, TOK, HD), BF), vm((2, TOK, cw), BF), vm((2, TOK, 128), F32),
                        vm((heads, TOK, HD), BF), vm((2, TOK, 3 * cw), BF), vm((-(-cw // 128) * 128, TOK), F32), vm((-(-cw // 128) * 128, TOK), F32), vm((4 * r, 4 * cw), BF),
                        vm((4, 4 * r, 4 * cw), BF), vm((4, 3 * r, 4 * cw), BF), vm((2, 4 * r, cm), BF), vm((2, 3 * r, cm), BF),
                        vm((5, r, 4 * cw), BF), vm((5, r, cm), BF), vm((5, 16, 2048), F32), vm((r, cm), BF), vm((r, cm), BF),
                        dma((32,)), dma((COPIES,)), dma((COPIES,))],
        compiler_params=pltpu.CompilerParams(vmem_limit_bytes=63 * 2**20, collective_id=number, has_side_effects=True),
        cost_estimate=pl.CostEstimate(flops=4 * 2 * TOK * (D * cw * 8 + heads * 5 * TOK * HD * 6), bytes_accessed=60 * 2**20, transcendentals=4 * heads * TOK * TOK),
        name="back",
    )(vectors, live, geb, tops, gout, midway, sec, firstT, x, mine, whole0, h1, h2, h3, O_low, *Ws, *qkvs, *atts, *lses)


class Spreading:
    def __init__(self, wires, piece, W):
        rows = W.shape[0] // 8
        one, two = cut_rows(rows)
        d = wires.d
        at = lambda mask, lo=0, n=rows: W.at[pl.ds(pl.multiple_of((d ^ mask) * rows + lo, 16), n), :]
        self.own = wires.local(piece, at(0), d >= 0)
        self.s0 = [wires.swap(piece, at(0), dp=m) for m in (2, 4, 1)]
        self.s1 = [wires.swap(at(2, 0, one), at(2, 0, one), dp=4), wires.swap(at(4, one, two), at(4, one, two), dp=2)]
        self.s1c = [wires.swap(at(m), at(m), dp=1) for m in (2, 4)]
        self.s2 = wires.swap(at(6), at(6), dp=1)

    def step0(self):
        self.own[0]()
        for s, _ in self.s0:
            s()

    def landed(self):
        for _, w in self.s0 + [self.own]:
            w()

    def go_on(self):
        for s, _ in self.s1 + self.s1c:
            s()

    def step1(self):
        for _, w in self.s0:
            w()
        self.go_on()

    def step2(self):
        for _, w in self.s1:
            w()
        self.s2[0]()

    def finish(self, own=True):
        for _, w in self.s1c + [self.s2] + [self.own] * own:
            w()


class Moves:
    def __init__(self, sem):
        self.sem, self.made = sem, {}

    def add(self, key, src, dst):
        self.made[key] = pltpu.make_async_copy(src, dst, self.sem.at[len(self.made)])

    def start(self, *keys):
        for k in keys:
            self.made[k].start()

    def wait(self, *keys):
        for k in keys:
            self.made[k].wait()


def front_kernel(length, heads, vectors, live, bias_own, x, cot, qw, kw, vw, ow, mw, *rest):
    (qkv0, qkv1, qkv2, qkv3, att0, att1, att2, att3, lse0, lse1, lse2, lse3, firstT, second, secondT, midway, Wa0, Wa1, Wa2, Wa3, Wm1, Zm2, gout, goutT,
     tops, bias_all, gout_s, goutT_s, x_s, first_s, T_s, second_s, acc, W, Za, Zm1, qkv_s, att_s, lse_s, bias, l_sem, s_sem, r_sem) = rest
    cw = heads * HD
    D = x_s.shape[1]
    wires, moves = Wires(s_sem, r_sem), Moves(l_sem)
    d, z = wires.d, wires.z

    def own_rows(ref):
        n = ref.shape[0] // 8
        return pl.ds(pl.multiple_of(d * n, 16), n)

    for i, ref in enumerate((qw, kw, vw, ow)):
        moves.add(f"w{i}", ref, W.at[0, pl.ds(i * cw, cw), :])
    moves.add("x", x, x_s)
    moves.add("cot", cot, gout_s)
    moves.add("gout", gout_s, gout)
    moves.add("goutT", goutT_s, goutT)
    gain1, shift1, gain2, shift2, out_b = [vectors[n:n + 1, :] for n in range(5)]
    moves.add("oW0", W.at[0], Wa0)
    for k, (a, b, c) in enumerate(((qkv0, att0, lse0), (qkv1, att1, lse1), (qkv2, att2, lse2), (qkv3, att3, lse3))):
        moves.add(f"qkv{k}", qkv_s.at[k], a)
        moves.add(f"att{k}", att_s.at[k], b)
        moves.add(f"lse{k}", lse_s.at[k], c)
    for k, ref in enumerate((Wa1, Wa2, Wa3)):
        moves.add(f"oW{k + 1}", W.at[k + 1], ref)
    moves.add("firstT", T_s, firstT)
    moves.add("second", second_s, second)
    moves.add("secondT", T_s, secondT)
    moves.add("midway", acc, midway)
    moves.start("w0", "w1", "w2", "w3", "x", "cot")

    zb = [wires.swap(bias.at[0], bias.at[k], z=k) for k in (1, 2, 3)]
    a_piece, m_piece = W.at[0, own_rows(W.at[0]), :], mw.at[own_rows(mw), :]
    za = [wires.swap(a_piece, Za.at[0], z=1), wires.swap(a_piece, Za.at[1], z=2), wires.swap(Za.at[1], Za.at[2], z=1)]
    zm = [wires.swap(m_piece, Zm1, z=1), wires.swap(m_piece, Zm2, z=2)]
    ga = {k: Spreading(wires, Za.at[k - 1], W.at[k]) for k in (1, 2, 3)}
    gm = Spreading(wires, Zm1, Wm1)
    greet(d, z, MASKS)
    bias[0] = bias_own[...]
    for s, _ in zb:
        s()
    moves.wait("w0", "w1", "w2", "w3")
    za[0][0]()
    za[1][0]()
    moves.start("oW0")
    moves.wait("x")

    @pl.loop(0, TOK // RT)
    def _(i):
        part = pl.ds(pl.multiple_of(i * RT, RT), RT)
        xt = x_s[part, :].astype(F32)
        normed, _ = normalize(xt)
        f = normed * gain1 + shift1
        first_s[part, :] = f.astype(BF)
        T_s[:, part] = f.T.astype(BF)
        acc[part, :] = xt + out_b

    moves.start("firstT")
    for _, w in zb:
        w()
    bias_all[...] = bias[...]

    def turn_gout():
        moves.wait("cot")

        @pl.loop(0, TOK // RT)
        def _(i):
            part = pl.ds(pl.multiple_of(i * RT, RT), RT)
            g = gout_s[part, :].astype(F32) * live[...]
            gout_s[part, :] = g.astype(BF)
            goutT_s[:, part] = g.T.astype(BF)

        moves.start("gout", "goutT")

    def z_a3():
        za[1][1]()
        za[2][0]()

    todo = {
        0: [zm[0][0]],
        1: [za[0][1], ga[1].step0],
        5: [z_a3, ga[2].step0, turn_gout, ga[1].step1, ga[1].step2],
        10: [za[2][1], ga[3].step0],
        11: [zm[1][0]],
        13: [ga[2].step1],
        15: [ga[2].step2],
        20: [ga[3].step1, zm[0][1], gm.step0],
        23: [ga[3].step2],
        30: [],
    }

    def tick(t):
        for action in todo.get(t, ()):
            action()

    for k in range(4):
        base = 10 * k
        Wk, qkv, att, lse = W.at[k], qkv_s.at[k], att_s.at[k], lse_s.at[k]
        if k:
            ga[k].finish()
            moves.start(f"oW{k}")
        tick(base)
        qb, vb = bias[k, 0:1, :cw], bias[k, 0:1, 384:384 + cw]

        @pl.loop(0, TOK // RT)
        def _(i):
            part = pl.ds(pl.multiple_of(i * RT, RT), RT)
            t = nt(first_s[part, :], Wk[:3 * cw, :])
            q = (t[:, :cw] + qb).astype(BF)
            kk = t[:, cw:2 * cw].astype(BF)
            v = (t[:, 2 * cw:] + vb).astype(BF)
            for h in range(heads):
                qkv[h, part, :] = q[:, h * HD:(h + 1) * HD]
                qkv[heads + h, part, :] = kk[:, h * HD:(h + 1) * HD]
                qkv[2 * heads + h, part, :] = v[:, h * HD:(h + 1) * HD]

        tick(base + 1)
        moves.start(f"qkv{k}")
        tops[k] = jnp.full(tops.shape[1:], -1e30, F32)

        @pl.loop(0, TOK // RT)
        def _(i):
            for n in range(3):
                pl.when(i == n)(functools.partial(tick, base + 2 + n))
            part = pl.ds(pl.multiple_of(i * RT, RT), RT)
            rid = lax.broadcasted_iota(jnp.int32, (RT, 1), 0) + i * RT
            cid = lax.broadcasted_iota(jnp.int32, (1, TOK), 1)
            res = []
            for h in range(heads):
                s = nt(qkv[h, part, :], qkv[heads + h])
                s = jnp.where(cid < length, s, -1e30)
                m = jnp.max(s, axis=1, keepdims=True)
                e = jnp.exp2((s - m) * (SC * LOG2E))
                l = jnp.sum(e, axis=1, keepdims=True)
                o = nn(e.astype(BF), qkv[2 * heads + h]) * (1.0 / l)
                res.append(o.astype(BF))
                lse[part, h:h + 1] = m * (SC * LOG2E) + jnp.log2(l)
                tops[k, h:h + 1, :] = jnp.maximum(tops[k, h:h + 1, :], jnp.max(jnp.where(rid < length, m, -1e30)) * SC)
            a = jnp.concatenate(res, axis=1)
            att[part, :] = a
            acc[part, :] += nn(a, Wk[3 * cw:, :])

        moves.start(f"att{k}", f"lse{k}")
        tick(base + 5)

    moves.start("midway")
    moves.wait("firstT")

    @pl.loop(0, TOK // RT)
    def _(i):
        part = pl.ds(pl.multiple_of(i * RT, RT), RT)
        normed, _ = normalize(acc[part, :])
        f = normed * gain2 + shift2
        second_s[part, :] = f.astype(BF)
        T_s[:, part] = f.T.astype(BF)

    moves.start("second", "secondT")
    gm.landed()
    zm[1][1]()
    for k in range(4):
        moves.wait(f"qkv{k}", f"att{k}", f"lse{k}", f"oW{k}")
    moves.wait("second", "secondT", "midway", "gout", "goutT")


def front(number, vectors, live, bias_own, x, cot, qw, kw, vw, ow, mw, length):
    cw, D = qw.shape
    heads = cw // HD
    cm = mw.shape[0]
    vm = pltpu.VMEM
    dma = pltpu.SemaphoreType.DMA
    four = lambda s: (s,) * 4
    got = pl.pallas_call(
        functools.partial(front_kernel, length, heads),
        out_shape=(*four(shape((3 * heads, TOK, HD), BF)), *four(shape((TOK, cw), BF)), *four(shape((TOK, 128), F32)),
                   shape((D, TOK), BF), shape((TOK, D), BF), shape((D, TOK), BF), shape((TOK, D), F32), *four(shape((4 * cw, D), BF)),
                   shape((cm, D), BF), shape((cm // 8, D), BF), shape((TOK, D), BF), shape((D, TOK), BF), shape((4, heads, 128), F32), shape((4, 8, 2048), F32)),
        in_specs=[VM] * 3 + [HB] * 7,
        out_specs=(HB,) * 24 + (VM,) * 2,
        scratch_shapes=[vm((TOK, D), BF), vm((D, TOK), BF), vm((TOK, D), BF), vm((TOK, D), BF), vm((D, TOK), BF), vm((TOK, D), BF), vm((TOK, D), F32),
                        vm((4, 4 * cw, D), BF), vm((3, cw // 2, D), BF), vm((cm // 8, D), BF), vm((4, 3 * heads, TOK, HD), BF),
                        vm((4, TOK, cw), BF), vm((4, TOK, 128), F32), vm((4, 8, 2048), F32), dma((32,)), dma((64,)), dma((64,))],
        compiler_params=pltpu.CompilerParams(vmem_limit_bytes=62 * 2**20, collective_id=number, has_side_effects=True),
        cost_estimate=pl.CostEstimate(flops=4 * 2 * TOK * (D * cw * 4 + heads * 2 * TOK * HD * 6), bytes_accessed=60 * 2**20, transcendentals=4 * heads * TOK * TOK),
        name="front",
    )(vectors, live, bias_own, x, cot, qw, kw, vw, ow, mw)
    return got[:4], got[4:8], got[8:12], got[12:16], got[16:20], got[20:22], got[22:24], got[24], got[25]


def middle_kernel(fw, live, vectors, bias_all, second, secondT, gout, goutT, midway, Wm0, Wm1, Zm2, *rest):
    (mine, sec, O0, H1, H2, H3, geb, part_sum, Wg2, Wg3, Zm3, Wg1, second_s, secondT_s, gout_s, goutT_s, mlp, sec_s, mine_s, W, act_s, slope_s, gpre_s, out_s,
     Hm, Lm, l_sem, s_sem, r_sem) = rest
    D = second_s.shape[1]
    hid = W.shape[1] // 2
    cut = fw // 128 * 128
    tail = fw - cut
    r = D // 8
    wires, moves = Wires(s_sem, r_sem), Moves(l_sem)
    d, z = wires.d, wires.z
    Ws = (Wm0, Wg1, Wg2, Wg3)
    for key, a, b in (("second", second, second_s), ("secondT", secondT, secondT_s), ("gout", gout, gout_s), ("goutT", goutT, goutT_s), ("midway", midway, mlp)):
        moves.add(key, a, b)
    for k in range(4):
        moves.add(f"W{k}", Ws[k], W.at[k % 2])
    moves.add("mine", mine_s, mine)
    moves.add("sec", sec_s, sec)
    moves.add("h1", Hm.at[1, pl.ds(0, r), :], H1)
    moves.add("h2", Hm.at[2], H2)
    moves.add("h3", Hm.at[3], H3)
    slot = jnp.where(z == 0, 0, jnp.where(z == 3, 1, 2))
    used = (z == 0) | (z == 3) | (z == 1 + d % 2)
    own_out = wires.local(mine_s, O0.at[pl.ds(pl.multiple_of(slot * TOK, 256), TOK), :], used)
    share = Sharing(wires, mine_s, O0, OUT_CHUNKS)
    z3 = wires.swap(Zm2, Zm3, z=1)
    g1, g2, g3 = Spreading(wires, Zm2, Wg1), Spreading(wires, Zm2, Wg2), Spreading(wires, Zm3, Wg3)
    exchange = [wires.swap(out_s.at[k % 2], Hm.at[k], dp=1) for k in range(4)]
    sums = [Summing(wires, Hm.at[k], Lm.at[k]) for k in (0, 1)]
    moves.start("second", "W0", "midway", "gout", "goutT", "secondT")
    greet(d, z, MASKS)
    g1.go_on()
    z3[0]()
    sec_s[...] = jnp.zeros_like(sec_s)
    geb[...] = jnp.zeros_like(geb)
    moves.wait("second", "midway")

    def forward(k, tick):
        b = k % 2
        moves.wait(f"W{k}")
        eb = bias_all[k, 0:1, 768:768 + hid]

        @pl.loop(0, TOK // RT)
        def _(i):
            tick(i)
            rows = pl.ds(pl.multiple_of(i * RT, RT), RT)
            act, slope = gelu_parts(nt(second_s[rows, :], W[b, :hid, :]) + eb)
            act_s[b, rows, :] = act.astype(BF)
            slope_s[b, rows, :] = slope.astype(BF)
            mlp[rows, :] += nn(act_s[b, rows, :], W[b, hid:, :])

    def grads(k, half):
        b = k % 2
        for t in range(2):
            q = 4 * t + 1 - half
            lhs = lambda ref: jnp.concatenate([ref[pl.ds(pl.multiple_of((d ^ p) * r, 16), r), :] for p in (q, q + 2)], axis=0)
            place = pl.ds(t * 2 * r, 2 * r)
            ve, vs = nn(lhs(secondT_s), gpre_s[b]), nn(lhs(goutT_s), act_s[b])
            last = jnp.concatenate([ve[:, cut:fw], vs[:, cut:fw], jnp.zeros((2 * r, 128 - 2 * tail), F32)], axis=1)
            to = out_s.at[b] if half == 0 else Hm.at[k]
            for lo, v in ((0, ve[:, :cut]), (cut, vs[:, :cut]), (2 * cut, last)):
                n = v.shape[1]
                if half:
                    v = v + to[place, lo:lo + n].astype(F32)
                to[place, lo:lo + n] = v.astype(BF)

    def back_a(k, tick):
        b = k % 2

        @pl.loop(0, TOK // RT)
        def _(i):
            tick(i)
            rows = pl.ds(pl.multiple_of(i * RT, RT), RT)
            gp = nt(gout_s[rows, :], W[b, hid:, :]) * slope_s[b, rows, :].astype(F32)
            geb[k] += jnp.sum(gp, axis=0, keepdims=True)
            gpre_s[b, rows, :] = gp.astype(BF)

        grads(k, 0)
        exchange[k][0]()

        @pl.loop(0, TOK // RT)
        def _(i):
            tick(i + 3)
            rows = pl.ds(pl.multiple_of(i * RT, RT), RT)
            sec_s[rows, :] += nn(gpre_s[b, rows, :], W[b, :hid, :])

    def back_b(k):
        exchange[k][1]()
        grads(k, 1)

    def ticks(table):
        def tick(i):
            for n, actions in table.items():
                def run():
                    for a in actions:
                        a()
                pl.when(i == n)(run)
        return tick

    none = ticks({})
    forward(0, ticks({2: [g2.step0]}))
    moves.wait("gout", "goutT", "secondT")
    back_a(0, ticks({2: [g1.step2]}))
    g1.finish(False)
    moves.start("W1")
    forward(1, ticks({1: [g2.step1], 2: [z3[1], g3.step0]}))
    back_b(0)
    back_a(1, ticks({1: [g2.step2], 4: [g3.step1]}))
    g2.finish()
    moves.start("W2")
    forward(2, ticks({2: [g3.step2]}))
    back_b(1)
    g3.finish()
    moves.start("W3")
    sums[0].step1()
    forward(3, none)

    @pl.loop(0, TOK // RT)
    def _(i):
        rows = pl.ds(pl.multiple_of(i * RT, RT), RT)
        mine_s[rows, :] = ((mlp[rows, :] + vectors[5:6, :]) * live[...]).astype(BF)
        pl.when(i == 0)(lambda: share.start(0, 0))
        pl.when(i == 1)(lambda: share.start(1, 0))

    own_out[0]()
    moves.start("mine")
    sums[1].step1()
    back_a(2, ticks({4: [sums[0].step2]}))
    back_a(3, ticks({4: [sums[0].step3]}))
    sums[1].step2()
    moves.start("sec")
    back_b(2)
    moves.start("h2")
    back_b(3)
    moves.start("h3")
    sums[1].step3()
    moves.start("h1")
    part_sum[...] = Hm[0, :r, :]
    share.wait(0, 0)
    share.wait(1, 0)
    own_out[1]()
    moves.wait("h1", "h2", "h3", "sec", "mine")


def middle(number, fw, live, vectors, bias_all, second, secondT, gout, goutT, midway, Wm0, Wm1, Zm2):
    D = second.shape[1]
    cm, hid = Wm0.shape[0], Wm0.shape[0] // 2
    cg = fw // 128 * 256 + 128
    r = D // 8
    vm = pltpu.VMEM
    dma = pltpu.SemaphoreType.DMA
    got = pl.pallas_call(
        functools.partial(middle_kernel, fw),
        out_shape=(shape((TOK, D), BF), shape((TOK, D), F32), shape((3 * TOK, D), BF), shape((r, cg), BF), shape((4 * r, cg), BF), shape((4 * r, cg), BF), shape((4, 1, hid), F32), shape((r, cg), BF),
                   shape((cm, D), BF), shape((cm, D), BF), shape((cm // 8, D), BF), shape((cm, D), BF)),
        in_specs=[VM] * 3 + [HB] * 8,
        out_specs=(HB,) * 6 + (VM,) * 2 + (HB,) * 4,
        input_output_aliases={9: 11},
        scratch_shapes=[vm((TOK, D), BF), vm((D, TOK), BF), vm((TOK, D), BF), vm((D, TOK), BF), vm((TOK, D), F32), vm((TOK, D), F32), vm((TOK, D), BF), vm((2, cm, D), BF),
                        vm((2, TOK, hid), BF), vm((2, TOK, hid), BF), vm((2, TOK, hid), BF), vm((2, 4 * r, cg), BF),
                        vm((4, 4 * r, cg), BF), vm((2, 3 * r, cg), BF), dma((32,)), dma((72,)), dma((72,))],
        compiler_params=pltpu.CompilerParams(vmem_limit_bytes=63 * 2**20, collective_id=number, has_side_effects=True),
        cost_estimate=pl.CostEstimate(flops=4 * 2 * 9 * TOK * D * fw, bytes_accessed=60 * 2**20, transcendentals=4 * TOK * fw),
        name="middle",
    )(live, vectors, bias_all, second, secondT, gout, goutT, midway, Wm0, Wm1, Zm2)
    return got[:8]


class General:
    def __init__(self, groups, attn_own, mlp_own):
        self.groups = groups
        self.attn, self.mlp = self.spread(attn_own), self.spread(mlp_own)

    def vectors(self, own):
        every = lax.all_gather(own, "tensor")
        return [every[i] for i in range(self.groups)]

    def spread(self, own):
        d, count = lax.axis_index("dp"), lax.axis_size("dp")
        rows = own.shape[0] // count
        piece = lax.dynamic_slice_in_dim(own, d * rows, rows, 0)
        piece = lax.all_gather(piece, "tensor")
        whole = lax.all_gather(piece, "dp", axis=1, tiled=True)
        return [whole[i] for i in range(self.groups)]

    def reduce(self, parts):
        part = lax.psum_scatter(jnp.stack(parts), "dp", scatter_dimension=1, tiled=True)
        return lax.psum_scatter(part, "tensor", scatter_dimension=0, tiled=True)[0].astype(F32)

    def collect(self, grad_attn, grad_mlp):
        return self.reduce(grad_attn), self.reduce(grad_mlp)

    def by_index(self, items):
        return jnp.stack(items)

    def share(self, mine):
        every = lax.all_gather(mine, "tensor")
        middle = 1 + lax.axis_index("dp") % 2
        return jnp.stack([every[0], every[self.groups - 1], lax.dynamic_index_in_dim(every, middle, 0, keepdims=False)])


def shards(images, counts, cotangent, query_w, query_b, key_w, value_w, value_b, out_w, out_b, norm1_gain, norm1_shift,
           norm2_gain, norm2_shift, expand_w, expand_b, shrink_w, shrink_b):
    slots, length, width = images.shape
    groups = lax.axis_size("tensor")
    d, z = lax.axis_index("dp"), lax.axis_index("tensor")
    cw, fw = query_w.shape[1], expand_w.shape[1]
    heads = cw // HD
    cut = fw // 128 * 128
    slot, used = slot_table(d, groups)
    live = jnp.where(used & (slot < counts[0]), 1.0, 0.0).astype(F32)
    pad = lambda a: jnp.pad(a, ((0, TOK - length), (0, 0)))

    x_low = pad(lax.dynamic_index_in_dim(images, slot, 0, keepdims=False))
    cot_low = pad(lax.dynamic_index_in_dim(cotangent, slot, 0, keepdims=False))
    if (groups, lax.axis_size("dp")) == (4, 8):
        blank = lambda n: jnp.zeros((n,), F32)
        bias_own = jnp.concatenate([query_b, blank(384 - cw), value_b, blank(384 - cw), expand_b, blank(1280 - fw)])
        deep = -fw % 16
        mlp_own = jnp.pad(jnp.stack([expand_w.T, shrink_w]), ((0, 0), (0, deep), (0, 0))).reshape(2 * (fw + deep), width)
        vectors = jnp.stack([norm1_gain, norm1_shift, norm2_gain, norm2_shift, out_b, shrink_b, shrink_b, shrink_b])
        qkvs, atts, lses, (first_t, second, second_t, midway), attn_ws, mlp_ws, (gout, gout_t), tops, bias_all = front(
            0, vectors, live[None, None], jnp.broadcast_to(bias_own, (8, 2048)), x_low, cot_low, query_w.T, key_w.T, value_w.T, out_w, mlp_own, length)
        mine, sec, out_low, h1, h2, h3, geb, part_sum = middle(1, fw, live[None, None], vectors, bias_all, second, second_t, gout, gout_t, midway, mlp_own, *mlp_ws)
        out_all, in_all, sum_attn, sum_mlp, vec = back(
            2, vectors, live[None, None], geb, jnp.where(live > 0.0, tops[:, :, 0], -1e30)[:, None],
            gout, midway, sec, first_t, x_low, mine, part_sum, h1, h2, h3, out_low, qkvs, atts, lses, attn_ws, length)
        outputs = out_all.reshape(3, TOK, width)[:, :length]
        input_grads = in_all.reshape(3, TOK, width)[:, :length].astype(F32)
        own = lax.dynamic_index_in_dim(vec, z, 0, keepdims=False)
        grad_query_b, grad_value_b, grad_expand_b, logit_top = own[:cw], own[384:384 + cw], own[768:768 + fw], own[1920:1920 + heads]
        tail = [vec[4 + i, :width] for i in range(6)]
    else:
        gout = cot_low * live.astype(BF)
        gout_t = gout.T
        attn_own = jnp.concatenate([query_w, key_w, value_w, out_w.T], axis=1)
        shrink_t = shrink_w.T
        mlp_own = jnp.concatenate([expand_w[:, :cut], shrink_t[:, :cut], expand_w[:, cut:], shrink_t[:, cut:]], axis=1)
        net = General(groups, attn_own, mlp_own)
        biases = net.vectors(jnp.concatenate([query_b, value_b, expand_b]))

        x = x_low.astype(F32)
        normed1, inverse1 = normalize(x)
        first = (normed1 * norm1_gain + norm1_shift).astype(BF)
        first_t = first.T
        acc = x + out_b
        kept, tops = [], []
        for k in range(groups):
            b = biases[k]
            qkv, att, lse, top, acc = attn_fwd(first, net.attn[k], b[None, :cw], b[None, cw:2 * cw], acc, length)
            kept.append((qkv, att, lse))
            tops.append(top[:, 0])
        midway = acc
        normed2, inverse2 = normalize(midway)
        second = (normed2 * norm2_gain + norm2_shift).astype(BF)
        second_t = second.T
        mlp = midway + shrink_b
        sec = jnp.zeros((TOK, width), F32)
        grad_mlp, geb = [], []
        for k in range(groups):
            grad, g_b, mlp, sec = mlp_call(second, second_t, gout, gout_t, net.mlp[k], biases[k][None, 2 * cw:], mlp, sec)
            grad_mlp.append(grad)
            geb.append(g_b[0, :fw])
        back2, gn2g, gn2s = norm_back(sec, normed2, inverse2, norm2_gain)
        gout32 = gout.astype(F32)
        gmid = gout32 + back2
        gmid_low = gmid.astype(BF)
        gmid_t = gmid_low.T
        acc = jnp.zeros((TOK, width), F32)
        grad_attn, gqb, gvb = [None] * groups, [None] * groups, [None] * groups
        for k in reversed(range(groups)):
            grad, g_q, g_v, acc = attn_bwd(gmid_low, gmid_t, first_t, net.attn[k], *kept[k], acc, length)
            grad_attn[k], gqb[k], gvb[k] = grad, g_q[0], g_v[0]
        back1, gn1g, gn1s = norm_back(acc, normed1, inverse1, norm1_gain)
        input_grad = ((gmid + back1) * live)[:length].astype(BF)

        outputs = net.share((mlp[:length] * live).astype(BF))
        input_grads = net.share(input_grad).astype(F32)
        sum_attn, sum_mlp = net.collect(grad_attn, grad_mlp)
        flat = lambda items: net.by_index(items).reshape(-1)
        vector = jnp.concatenate([flat(gqb), flat(gvb), flat(geb), jnp.sum(gmid, axis=0), jnp.sum(gout32, axis=0), gn1g, gn1s, gn2g, gn2s])
        vector = lax.psum(vector, ("dp", "tensor"))
        part = lambda start, size: lax.dynamic_slice_in_dim(vector, start, size, 0)
        whole, hidden = cw * groups, fw * groups
        tail = [vector[2 * whole + hidden + i * width:][:width] for i in range(6)]
        logit_top = lax.pmax(jnp.where(live > 0.0, net.by_index(tops), -1e30), ("dp", "tensor"))
        logit_top = lax.dynamic_index_in_dim(logit_top, z, 0, keepdims=False)
        grad_query_b, grad_value_b, grad_expand_b = part(z * cw, cw), part(whole + z * cw, cw), part(2 * whole + z * fw, fw)
    factor = jnp.sqrt(clip_limit / jnp.maximum(logit_top, clip_limit))
    column_factor = jnp.repeat(factor, HD)
    clipped_query = (query_w.astype(F32) * column_factor).astype(BF)
    clipped_key = (key_w.astype(F32) * column_factor).astype(BF)
    unpack = lambda a, i: jnp.concatenate([a[:, i * cut:(i + 1) * cut], a[:, 2 * cut + i * (fw - cut):][:, :fw - cut]], axis=1)
    return (outputs, input_grads, sum_attn[:, :cw], grad_query_b, sum_attn[:, cw:2 * cw], sum_attn[:, 2 * cw:3 * cw], grad_value_b,
            sum_attn[:, 3 * cw:].T, tail[0], tail[2], tail[3], tail[4], tail[5], unpack(sum_mlp, 0), grad_expand_b, unpack(sum_mlp, 1).T,
            tail[1], clipped_query, clipped_key)


def solution(mesh):
    columns, rows, vector = P(None, "tensor"), P("tensor", None), P("tensor")
    whole = P("dp", None, None)
    return jax.shard_map(
        shards, mesh=mesh,
        in_specs=(whole, P("dp"), whole, columns, vector, columns, columns, vector, rows, P(), P(), P(), P(), P(), columns, vector, rows, P()),
        out_specs=(whole, whole, P("dp", "tensor"), vector, P("dp", "tensor"), P("dp", "tensor"), vector, P("tensor", "dp"), P(), P(), P(), P(), P(),
                   P("dp", "tensor"), vector, P("tensor", "dp"), P(), columns, columns),
        check_vma=False)
```

```python
import functools
import math

import jax
import jax.numpy as jnp
from jax import lax
from jax.experimental import pallas as pl
from jax.experimental.pallas import tpu as pltpu
from jax.sharding import PartitionSpec as P

HD = 72
TOK = 768
RT = 256
SC = 1 / math.sqrt(HD)
LOG2E = 1.4426950408889634
F32 = jnp.float32
BF = jnp.bfloat16
norm_eps = 1e-06
clip_limit = 3.0
tanh_coef = 0.7978845608028654
cube_coef = 0.044715
VM = pl.BlockSpec(memory_space=pltpu.VMEM)
HB = pl.BlockSpec(memory_space=pl.ANY)
MESH = pl.DeviceIdType.MESH


def nn(a, b):
    return jnp.dot(a, b, preferred_element_type=F32)


def nt(a, b):
    return lax.dot_general(a, b, (((1,), (1,)), ((), ())), preferred_element_type=F32)


def tn(a, b):
    return lax.dot_general(a, b, (((0,), (0,)), ((), ())), preferred_element_type=F32)


def shape(dims, dtype):
    return jax.ShapeDtypeStruct(dims, dtype)


def cut_rows(rows):
    first = (rows // 2 + 15) // 16 * 16
    return first, rows - first


def block_rows(lhs, rhs, half, write):
    if half is None:
        @pl.loop(0, lhs.shape[0] // 384)
        def _(t):
            place = pl.ds(pl.multiple_of(t * 384, 128), 384)
            write(place, nn(lhs[place, :], rhs[...]))
    else:
        rows = lhs.shape[0] // 8
        d = lax.axis_index("dp")

        @pl.loop(0, 2)
        def _(t):
            r = 4 * t + 1 - half
            both = [lhs[pl.ds(pl.multiple_of((d ^ q) * rows, 16), rows), :] for q in (r, r + 2)]
            write(pl.ds(pl.multiple_of(t * 2 * rows, 16), 2 * rows), nn(jnp.concatenate(both, axis=0), rhs[...]))


def attn_fwd_kernel(length, heads, first, qb, vb, acc_in, W, qkv, att, lse, tops, acc):
    cw = heads * HD

    @pl.loop(0, TOK // RT)
    def _(i):
        rows = pl.ds(pl.multiple_of(i * RT, RT), RT)
        t = nn(first[rows, :], W[:, :3 * cw])
        q = (t[:, :cw] + qb[...]).astype(BF)
        k = t[:, cw:2 * cw].astype(BF)
        v = (t[:, 2 * cw:] + vb[...]).astype(BF)
        for h in range(heads):
            qkv[h, rows, :] = q[:, h * HD:(h + 1) * HD]
            qkv[heads + h, rows, :] = k[:, h * HD:(h + 1) * HD]
            qkv[2 * heads + h, rows, :] = v[:, h * HD:(h + 1) * HD]

    tops[...] = jnp.full(tops.shape, -1e30, F32)

    @pl.loop(0, TOK // RT)
    def _(i):
        rows = pl.ds(pl.multiple_of(i * RT, RT), RT)
        rid = lax.broadcasted_iota(jnp.int32, (RT, 1), 0) + i * RT
        cid = lax.broadcasted_iota(jnp.int32, (1, TOK), 1)
        res = []
        for h in range(heads):
            s = nt(qkv[h, rows, :], qkv[heads + h])
            s = jnp.where(cid < length, s, -1e30)
            m = jnp.max(s, axis=1, keepdims=True)
            e = jnp.exp2((s - m) * (SC * LOG2E))
            l = jnp.sum(e, axis=1, keepdims=True)
            o = nn(e.astype(BF), qkv[2 * heads + h]) * (1.0 / l)
            res.append(o.astype(BF))
            lse[rows, h:h + 1] = m * (SC * LOG2E) + jnp.log2(l)
            tops[h:h + 1, :] = jnp.maximum(tops[h:h + 1, :], jnp.max(jnp.where(rid < length, m, -1e30)) * SC)
        a = jnp.concatenate(res, axis=1)
        att[rows, :] = a
        acc[rows, :] = acc_in[rows, :] + nt(a, W[:, 3 * cw:])


def attn_fwd(first, W, qb, vb, acc, length):
    D = first.shape[1]
    cw = W.shape[1] // 4
    heads = cw // HD
    return pl.pallas_call(
        functools.partial(attn_fwd_kernel, length, heads),
        out_shape=(shape((3 * heads, TOK, HD), BF), shape((TOK, cw), BF), shape((TOK, 128), F32), shape((heads, 128), F32), shape((TOK, D), F32)),
        in_specs=[VM] * 5,
        out_specs=(VM,) * 5,
        compiler_params=pltpu.CompilerParams(vmem_limit_bytes=44 * 2**20),
        cost_estimate=pl.CostEstimate(flops=2 * TOK * (D * cw * 4 + heads * 2 * TOK * HD * 6), bytes_accessed=25 * 2**20, transcendentals=heads * TOK * TOK),
        name="attn_fwd",
    )(first, qb, vb, acc, W)


def gelu_parts(u):
    u2 = u * u
    t = jnp.tanh(u * (tanh_coef + (tanh_coef * cube_coef) * u2))
    hu = 0.5 * (1.0 + t)
    return u * hu, hu + u * (0.5 * tanh_coef) * (1.0 - t * t) * (1.0 + (3.0 * cube_coef) * u2)


def mlp_kernel(fw, second, secondT, gout, goutT, eb, mlp_in, sec_in, W, G, geb, mlp, sec, E, ST, act_s, gpre_s):
    cut = fw // 128 * 128
    tail = fw - cut
    E[:, :cut] = W[:, :cut]
    ST[:, :cut] = W[:, cut:2 * cut]
    last = W[:, 2 * cut:]
    blank = jnp.zeros((last.shape[0], 128 - tail), BF)
    E[:, cut:] = jnp.concatenate([last[:, :tail], blank], axis=1)
    ST[:, cut:] = jnp.concatenate([last[:, tail:], blank], axis=1)
    geb[...] = jnp.zeros_like(geb)

    @pl.loop(0, TOK // RT)
    def _(i):
        rows = pl.ds(pl.multiple_of(i * RT, RT), RT)
        act, slope = gelu_parts(nn(second[rows, :], E[...]) + eb[...])
        act_s[rows, :] = act.astype(BF)
        gp = nn(gout[rows, :], ST[...]) * slope
        geb[...] += jnp.sum(gp, axis=0, keepdims=True)
        gpre_s[rows, :] = gp.astype(BF)
        mlp[rows, :] = mlp_in[rows, :] + nt(act_s[rows, :], ST[...])
        sec[rows, :] = sec_in[rows, :] + nt(gpre_s[rows, :], E[...])

    def write(lo, last):
        def put(place, v):
            v = v.astype(BF)
            G[place, lo:lo + cut] = v[:, :cut]
            G[place, last:last + tail] = v[:, cut:fw]
        return put

    block_rows(secondT, gpre_s, None, write(0, 2 * cut))
    block_rows(goutT, act_s, None, write(cut, 2 * cut + tail))


def mlp_call(second, secondT, gout, goutT, W, eb, mlp, sec):
    D = second.shape[1]
    fw = W.shape[1] // 2
    wide = fw // 128 * 128 + 128
    eb = jnp.pad(eb, ((0, 0), (0, wide - fw)))
    return pl.pallas_call(
        functools.partial(mlp_kernel, fw),
        out_shape=(shape((D, 2 * fw), BF), shape((1, wide), F32), shape((TOK, D), F32), shape((TOK, D), F32)),
        in_specs=[VM] * 8,
        out_specs=(VM,) * 4,
        scratch_shapes=[pltpu.VMEM((D, wide), BF)] * 2 + [pltpu.VMEM((TOK, wide), BF)] * 2,
        compiler_params=pltpu.CompilerParams(vmem_limit_bytes=56 * 2**20),
        cost_estimate=pl.CostEstimate(flops=2 * 9 * TOK * D * fw, bytes_accessed=35 * 2**20, transcendentals=TOK * fw),
        name="mlp",
    )(second, secondT, gout, goutT, eb, mlp, sec, W)


def attn_bwd_kernel(length, heads, gmid, gmidT, firstT, qkv, att, lse, acc_in, W, G, gqb, gvb, acc, ga_s, d_s, dk_s, dv_s):
    cw = heads * HD

    @pl.loop(0, TOK // RT)
    def _(i):
        rows = pl.ds(pl.multiple_of(i * RT, RT), RT)
        g = nn(gmid[rows, :], W[:, 3 * cw:]).astype(BF)
        for h in range(heads):
            ga_s[h, rows, :] = g[:, h * HD:(h + 1) * HD]

    gqb[...] = jnp.zeros_like(gqb)
    dk_s[...] = jnp.zeros_like(dk_s)
    dv_s[...] = jnp.zeros_like(dv_s)

    @pl.loop(0, TOK // RT)
    def _(i):
        rows = pl.ds(pl.multiple_of(i * RT, RT), RT)
        cid = lax.broadcasted_iota(jnp.int32, (1, TOK), 1)
        dqs = []
        for h in range(heads):
            q, k, v, g = qkv[h, rows, :], qkv[heads + h], qkv[2 * heads + h], ga_s[h, rows, :]
            s = nt(q, k)
            p = jnp.exp2(s * (SC * LOG2E) - lse[rows, h:h + 1])
            p = jnp.where(cid < length, p, 0.0)
            dp = nt(g, v)
            dd = jnp.sum(g.astype(F32) * att[rows, h * HD:(h + 1) * HD].astype(F32), axis=1, keepdims=True)
            ds = (p * (dp - dd)).astype(BF)
            dqs.append(nn(ds, k) * SC)
            dk_s[h] += tn(ds, q)
            dv_s[h] += tn(p.astype(BF), g)
        dq = jnp.concatenate(dqs, axis=1)
        gqb[...] += jnp.sum(dq, axis=0, keepdims=True)
        d_s[rows, :cw] = dq.astype(BF)

    dk = jnp.concatenate([dk_s[h] * SC for h in range(heads)], axis=1)
    d_s[:, cw:2 * cw] = dk.astype(BF)
    dv = jnp.concatenate([dv_s[h] for h in range(heads)], axis=1)
    gvb[...] = jnp.sum(dv, axis=0, keepdims=True)
    d_s[:, 2 * cw:] = dv.astype(BF)

    @pl.loop(0, TOK // RT)
    def _(i):
        rows = pl.ds(pl.multiple_of(i * RT, RT), RT)
        acc[rows, :] = acc_in[rows, :] + nt(d_s[rows, :], W[:, :3 * cw])

    def write(lo, hi):
        def put(place, v):
            G[place, lo:hi] = v.astype(BF)
        return put

    block_rows(firstT, d_s, None, write(0, 3 * cw))
    block_rows(gmidT, att, None, write(3 * cw, 4 * cw))


def attn_bwd(gmid, gmidT, firstT, W, qkv, att, lse, acc, length):
    D = gmid.shape[1]
    cw = W.shape[1] // 4
    heads = cw // HD
    return pl.pallas_call(
        functools.partial(attn_bwd_kernel, length, heads),
        out_shape=(shape((D, 4 * cw), BF), shape((1, cw), F32), shape((1, cw), F32), shape((TOK, D), F32)),
        in_specs=[VM] * 8,
        out_specs=(VM,) * 4,
        scratch_shapes=[pltpu.VMEM((heads, TOK, HD), BF), pltpu.VMEM((TOK, 3 * cw), BF), pltpu.VMEM((heads, TOK, HD), F32), pltpu.VMEM((heads, TOK, HD), F32)],
        compiler_params=pltpu.CompilerParams(vmem_limit_bytes=52 * 2**20),
        cost_estimate=pl.CostEstimate(flops=2 * TOK * (D * cw * 8 + heads * 5 * TOK * HD * 6), bytes_accessed=30 * 2**20, transcendentals=heads * TOK * TOK),
        name="attn_bwd",
    )(gmid, gmidT, firstT, qkv, att, lse, acc, W)


def normalize(values):
    centre = jnp.mean(values, axis=-1, keepdims=True)
    centred = values - centre
    spread = jnp.mean(centred * centred, axis=-1, keepdims=True)
    inverse = lax.rsqrt(spread + norm_eps)
    return centred * inverse, inverse


def norm_back(grad_norm, normed, inverse, gain):
    scaled = grad_norm * gain
    first_mean = jnp.mean(scaled, axis=-1, keepdims=True)
    second_mean = jnp.mean(scaled * normed, axis=-1, keepdims=True)
    grad_input = inverse * (scaled - first_mean - normed * second_mean)
    return grad_input, jnp.sum(grad_norm * normed, axis=0), jnp.sum(grad_norm, axis=0)


def slot_table(d, groups):
    z = lax.axis_index("tensor")
    middle = 1 + d % 2
    return jnp.where(z == 0, 0, jnp.where(z == groups - 1, 1, 2)), (z == 0) | (z == groups - 1) | (z == middle)


HOPS = {
    "u1": (1, ((0, None),)), "u2": (3, ((1, None),)), "u3": (1, ((2, None),)),
    "w1": (1, ((3, None),)), "w2": (3, ((2, None),)), "w3": (1, ((1, None),)),
    "v1": (3, ((1, 0), (2, 1))), "v2": (1, ((2, 0), (1, 1))), "v3": (1, ((1, 0), (2, 1))),
}
HOP_FROM = {"u1": "me", "u2": "u1", "u3": "u2", "w1": "me", "w2": "w1", "w3": "w2", "v1": "me", "v2": "v1", "v3": "me"}
NAMES = ("u1", "w1", "v1", "v3"), ("u2", "w2", "v2"), ("u3", "w3")
BEGIN = {"u": 0, "w": 1, "v": 2}


class Wires:
    def __init__(self, s_sem, r_sem):
        self.s, self.r, self.n = s_sem, r_sem, 0
        self.d, self.z = lax.axis_index("dp"), lax.axis_index("tensor")

    def local(self, src, dst, used):
        i = self.n
        self.n += 1
        make = lambda: pltpu.make_async_copy(src, dst, self.s.at[i])
        return (lambda: pl.when(used)(lambda: make().start())), (lambda: pl.when(used)(lambda: make().wait()))

    def swap(self, src, dst, dp=0, z=0, sends=None):
        i = self.n
        self.n += 1
        make = lambda: pltpu.make_async_remote_copy(src_ref=src, dst_ref=dst, send_sem=self.s.at[i], recv_sem=self.r.at[i], device_id=(self.d ^ dp, self.z ^ z), device_id_type=MESH)
        if sends is None:
            return (lambda: make().start()), (lambda: make().wait())

        def any_of(z_here):
            hit = None
            for zz, cc in sends:
                this = z_here == zz
                if cc is not None:
                    this = this & (self.d % 2 == cc)
                hit = this if hit is None else hit | this
            return hit

        def start():
            pl.when(any_of(self.z))(lambda: make().start())

        def wait():
            pl.when(any_of(self.z))(lambda: make().wait_send())
            pl.when(any_of(self.z ^ z))(lambda: make().wait_recv())

        return start, wait


def greet(d, z, masks):
    sem = pltpu.get_barrier_semaphore()
    for dp, t in masks:
        pl.semaphore_signal(sem, inc=1, device_id=(d ^ dp, z ^ t), device_id_type=MESH)
    pl.semaphore_wait(sem, len(masks))


class Summing:
    def __init__(self, wires, H, land):
        self.H = H
        self.rows = r = H.shape[0] // 4
        self.one, self.two = one, two = cut_rows(r)
        ax, by = land.at[pl.ds(0, 2 * one), :], land.at[pl.ds(2 * one, 2 * two), :]
        ay, bx = land.at[pl.ds(2 * r, one), :], land.at[pl.ds(2 * r + one, two), :]
        self.land = land
        h = lambda lo, n: H.at[pl.ds(lo, n), :]
        at = lambda ref, lo, n: ref.at[pl.ds(lo, n), :]
        self.c1 = [wires.swap(h(r, one), at(land, 0, one), dp=2), wires.swap(h(3 * r, one), at(land, one, one), dp=2),
                   wires.swap(h(2 * r + one, two), at(land, 2 * one, two), dp=4), wires.swap(h(3 * r + one, two), at(land, 2 * one + two, two), dp=4)]
        self.c2 = [wires.swap(h(2 * r, one), ay, dp=4), wires.swap(h(r + one, two), bx, dp=2)]

    def add(self, lo, n, *froms):
        total = self.H[lo:lo + n, :].astype(F32)
        for f in froms:
            total = total + self.land[f:f + n, :].astype(F32)
        self.H[lo:lo + n, :] = total.astype(BF)

    def step1(self):
        for s, _ in self.c1:
            s()

    def step2(self):
        r, one, two = self.rows, self.one, self.two
        for _, w in self.c1:
            w()
        self.add(2 * r, one, one)
        self.add(r + one, two, 2 * one + two)
        for s, _ in self.c2:
            s()

    def step3(self):
        r, one, two = self.rows, self.one, self.two
        for _, w in self.c2:
            w()
        self.add(0, one, 0, 2 * r)
        self.add(one, two, 2 * one, 2 * r + one)


ENDS = ((0, None), (3, None))
INNER = ((1, None), (2, None))


class LineSum:
    def __init__(self, wires, parts, land):
        self.parts, self.land = parts, land
        self.inner = (wires.z == 1) | (wires.z == 2)
        self.a = {k: wires.swap(parts[k], land.at[k - 1], z=1, sends=ENDS) for k in (1, 2, 3)}
        self.b = [wires.swap(parts[3], land.at[3], z=3, sends=INNER), wires.swap(parts[2], land.at[4], z=3, sends=INNER)]
        self.g = wires.swap(parts[1], land.at[0], z=1, sends=INNER)

    def alpha(self, k):
        self.a[k][0]()

    def add(self, k, i):
        @pl.when(self.inner)
        def _():
            self.parts[k][...] = (self.parts[k][...].astype(F32) + self.land[i].astype(F32)).astype(BF)

    def beta(self):
        self.a[2][1]()
        self.a[3][1]()
        self.add(3, 1)
        self.add(2, 2)
        for s, _ in self.b:
            s()

    def gamma(self):
        for _, w in self.b:
            w()
        self.a[1][1]()
        self.add(1, 4)
        self.g[0]()

    def total(self, own):
        self.g[1]()
        other = jnp.where(self.inner, self.land[3].astype(F32), 0.0)
        return own + self.land[0].astype(F32) + other


class Sharing:
    def __init__(self, wires, mine, O, chunks, base=0):
        self.stages = []
        stride = O.shape[0] // 3
        for lo, n in chunks:
            here = []
            for names in NAMES:
                row = []
                for name in names:
                    mask, sends = HOPS[name]
                    place = O.at[pl.ds(BEGIN[name[0]] * stride + lo - base, n), :]
                    row.append(wires.swap(mine.at[pl.ds(lo, n), :] if HOP_FROM[name] == "me" else place, place, z=mask, sends=sends))
                here.append(row)
            self.stages.append(here)

    def start(self, chunk, stage):
        for s, _ in self.stages[chunk][stage]:
            s()

    def wait(self, chunk, stage):
        for _, w in self.stages[chunk][stage]:
            w()

    def on(self, chunk, stage):
        self.wait(chunk, stage - 1)
        self.start(chunk, stage)


OUT_CHUNKS = ((0, 256), (256, 256), (512, 224))
IN_CHUNKS = ((0, 128), (128, 128), (256, 128), (384, 128), (512, 128), (640, 96))
MASKS = [(1, 0), (2, 0), (4, 0), (0, 1), (0, 2), (0, 3)]
COPIES = 180


LATE = 2


def back_kernel(length, heads, vectors, live, geb, tops, gout, midway, sec, firstT, x, mine, whole0, h1, h2, h3, O_low, *rest):
    gain1, gain2 = vectors[0:1, :], vectors[2:3, :]
    Ws, qkvs, atts, lses, rest = rest[:4], rest[4:8], rest[8:12], rest[12:16], rest[16:]
    (O_out, O_in, sum_a, sum_m, vec, g_s, gm_s, acc, gT, fT, x_s, W_s, qkv_s, att_s, lse_s, ga_s, d_s, dk_s, dv_s, out_s,
     Ha, La, Hm, Lm, za, zm, vr, w0_s, w1_s, l_sem, s_sem, r_sem) = rest
    cw = heads * HD
    D = g_s.shape[1]
    wires = Wires(s_sem, r_sem)
    d, z = wires.d, wires.z
    loads = {}
    order = [3, 2, 1, 0]
    names = iter(range(100))

    def load(key, src, dst):
        loads[key] = pltpu.make_async_copy(src, dst, l_sem.at[next(names)])

    load("midway", midway, acc)
    load("sec", sec, gm_s)
    load("gout", gout, g_s)
    load("firstT", firstT, fT)
    load("x", x, x_s)
    load("h2", h2, Hm.at[0])
    load("h3", h3, Hm.at[1])
    load("w0", whole0, w0_s)
    load("w1", h1, w1_s)
    for i, k in enumerate(order):
        b = i % 2
        load(f"W{i}", Ws[k], W_s.at[b])
        load(f"qkv{i}", qkvs[k], qkv_s.at[b])
        load(f"att{i}", atts[k], att_s.at[b])
        load(f"lse{i}", lses[k], lse_s.at[b])
    for key in ("midway", "sec", "gout", "h2", "h3", "w1", "w0", "firstT", "W0", "qkv0", "att0", "lse0", "x"):
        loads[key].start()
    slot = jnp.where(z == 0, 0, jnp.where(z == 3, 1, 2))
    own_place = pl.ds(pl.multiple_of(slot * TOK, 256), TOK)
    used = (z == 0) | (z == 3) | (z == 1 + d % 2)
    own_in = wires.local(g_s, O_in.at[own_place, :], used)
    share_out = Sharing(wires, mine, O_out, OUT_CHUNKS)
    share_in = Sharing(wires, g_s, O_in, IN_CHUNKS)
    sums = {"m2": Summing(wires, Hm.at[0], Lm.at[0]), "m3": Summing(wires, Hm.at[1], Lm.at[1])}
    for k in range(4):
        sums[f"b{k}"] = Summing(wires, Ha.at[k], La.at[k])
    r = sum_a.shape[0]
    top = pl.ds(0, r)
    line_m = LineSum(wires, [None, w1_s, Hm.at[0, top, :], Hm.at[1, top, :]], zm)
    line_b = LineSum(wires, [Ha.at[k, top, :] for k in range(4)], za)
    exchange = {k: wires.swap(out_s, Ha.at[k], dp=1) for k in range(4)}
    spread = [wires.swap(vec, vr.at[i], dp=dp, z=t) for i, (dp, t) in enumerate(((1, 0), (2, 0), (4, 0), (0, 1), (0, 2)))]
    greet(d, z, MASKS)

    todo = {
        -3: [lambda: share_out.start(0, 1), lambda: share_out.start(1, 1), lambda: share_out.start(2, 0)],
        -2: [lambda: loads["h2"].wait(), sums["m2"].step1, lambda: loads["w1"].wait(), lambda: line_m.alpha(1)],
        0: [lambda: loads["h3"].wait(), lambda: loads["w0"].wait()],
        5: [sums["m2"].step2, sums["m3"].step1],
        8: [lambda: share_out.on(0, 2), lambda: share_out.on(2, 1)],
        10: [sums["m2"].step3, lambda: line_m.alpha(2)],
        15: [sums["m3"].step2],
        18: [lambda: share_out.on(1, 2), sums["b3"].step2],
        20: [sums["m3"].step3, lambda: line_m.alpha(3)],
        22: [sums["b3"].step3, lambda: line_b.alpha(3)],
        25: [line_m.beta],
        28: [lambda: share_out.on(2, 2), sums["b2"].step2],
        33: [sums["b2"].step3, lambda: line_b.alpha(2)],
        38: [line_m.gamma],
    }

    def tick(t):
        for action in todo.get(t, ()):
            action()

    vec[...] = jnp.zeros_like(vec)
    for key in ("midway", "sec", "gout"):
        loads[key].wait()

    def total_of(row, value):
        vec[row:row + 1, :D] += jnp.sum(value, axis=0, keepdims=True)

    def put_row(where, lo, value):
        n = value.shape[1]
        hit = lax.broadcasted_iota(jnp.int32, (8, n), 0) == where
        vec[0:8, lo:lo + n] += jnp.where(hit, jnp.broadcast_to(value, (8, n)), 0.0)

    @pl.loop(0, TOK // RT)
    def _(i):
        for t in range(3):
            pl.when(i == t)(functools.partial(tick, t - 3))
        rows = pl.ds(pl.multiple_of(i * RT, RT), RT)
        normed, inverse = normalize(acc[rows, :])
        e = gm_s[rows, :]
        go = g_s[rows, :].astype(F32)
        scaled = e * gain2
        mean1 = jnp.mean(scaled, axis=-1, keepdims=True)
        mean2 = jnp.mean(scaled * normed, axis=-1, keepdims=True)
        gm = go + inverse * (scaled - mean1 - normed * mean2)
        total_of(4, gm)
        total_of(5, go)
        total_of(8, e * normed)
        total_of(9, e)
        gm_s[rows, :] = gm
        g_s[rows, :] = gm.astype(BF)
        gT[:, rows] = gm.T.astype(BF)

    def write(dst, lo, hi, add):
        def put(where, val):
            if add:
                val = val + dst[where, lo:hi].astype(F32)
            dst[where, lo:hi] = val.astype(BF)
        return put

    def give(i):
        k, b = order[i], i % 2
        block_rows(fT, d_s.at[b], 0, write(out_s, 0, 3 * cw, False))
        block_rows(gT, att_s.at[b], 0, write(out_s, 3 * cw, 4 * cw, False))
        exchange[k][0]()

    def keep(i):
        k, b = order[i], i % 2
        exchange[k][1]()
        block_rows(fT, d_s.at[b], 1, write(Ha.at[k], 0, 3 * cw, True))
        block_rows(gT, att_s.at[b], 1, write(Ha.at[k], 3 * cw, 4 * cw, True))

    loads["firstT"].wait()
    acc[...] = jnp.zeros_like(acc)
    for i, k in enumerate(order):
        base, b = 10 * i, i % 2
        W, qkv, att, lse, dd_s = W_s.at[b], qkv_s.at[b], att_s.at[b], lse_s.at[b], d_s.at[b]
        for key in ("W", "qkv", "att", "lse"):
            loads[f"{key}{i}"].wait()
        if i < 3:
            for key in ("W", "qkv", "lse"):
                loads[f"{key}{i + 1}"].start()
        tick(base)

        @pl.loop(0, TOK // RT)
        def _(t):
            rows = pl.ds(pl.multiple_of(t * RT, RT), RT)
            g = nt(g_s[rows, :], W[3 * cw:, :]).astype(BF)
            for h in range(heads):
                ga_s[h, rows, :] = g[:, h * HD:(h + 1) * HD]

        if 1 <= i <= LATE:
            keep(i - 1)
            sums[f"b{order[i - 1]}"].step1()
        if i < 3:
            loads[f"att{i + 1}"].start()
        tick(base + 1)
        dk_s[...] = jnp.zeros_like(dk_s)
        dv_s[...] = jnp.zeros_like(dv_s)
        place = z ^ k

        @pl.loop(0, TOK // RT)
        def _(t):
            for n in range(3):
                pl.when(t == n)(functools.partial(tick, base + 2 + n))
            rows = pl.ds(pl.multiple_of(t * RT, RT), RT)
            cid = lax.broadcasted_iota(jnp.int32, (1, TOK), 1)
            dqs = []
            for h in range(heads):
                q, kk, v, g = qkv[h, rows, :], qkv[heads + h], qkv[2 * heads + h], ga_s[h, rows, :]
                s = nt(q, kk)
                p = jnp.exp2(s * (SC * LOG2E) - lse[rows, h:h + 1])
                p = jnp.where(cid < length, p, 0.0)
                dp = nt(g, v)
                dd = jnp.sum(g.astype(F32) * att[rows, h * HD:(h + 1) * HD].astype(F32), axis=1, keepdims=True)
                ds = (p * (dp - dd)).astype(BF)
                dqs.append(nn(ds, kk) * SC)
                dk_s[h * HD:(h + 1) * HD, :] += tn(q, ds)
                dv_s[h * HD:(h + 1) * HD, :] += tn(g, p.astype(BF))
            dq = jnp.concatenate(dqs, axis=1)
            put_row(place, 0, jnp.sum(dq, axis=0, keepdims=True))
            dd_s[rows, :cw] = dq.astype(BF)

        dd_s[:, cw:2 * cw] = (dk_s[...].T[:, :cw] * SC).astype(BF)
        dv = dv_s[...].T[:, :cw]
        put_row(place, 384, jnp.sum(dv, axis=0, keepdims=True))
        dd_s[:, 2 * cw:] = dv.astype(BF)
        put_row(place, 768, geb[k])
        put_row(place, 1920, tops[k])
        tick(base + 5)

        if i < LATE:
            give(i)
        tick(base + 6)

        @pl.loop(0, TOK // RT)
        def _(t):
            rows = pl.ds(pl.multiple_of(t * RT, RT), RT)
            acc[rows, :] += nn(dd_s[rows, :], W[:3 * cw, :])

        tick(base + 7)
        tick(base + 8)

    loads["x"].wait()

    @pl.loop(0, TOK // RT)
    def _(i):
        rows = pl.ds(pl.multiple_of(i * RT, RT), RT)
        normed, inverse = normalize(x_s[rows, :].astype(F32))
        e = acc[rows, :]
        scaled = e * gain1
        mean1 = jnp.mean(scaled, axis=-1, keepdims=True)
        mean2 = jnp.mean(scaled * normed, axis=-1, keepdims=True)
        total_of(6, e * normed)
        total_of(7, e)
        g_s[rows, :] = ((gm_s[rows, :] + inverse * (scaled - mean1 - normed * mean2)) * live[...]).astype(BF)
        for t in range(3):
            @pl.when(i == t)
            def _():
                share_in.start(2 * t, 0)
                share_in.start(2 * t + 1, 0)

    own_in[0]()
    spread[0][0]()
    give(2)
    after = {
        0: [line_b.beta, lambda: keep(2), sums["b1"].step1, lambda: give(3)],
        1: [lambda: keep(3), sums["b0"].step1],
        2: [sums["b1"].step2],
        3: [sums["b1"].step3, lambda: line_b.alpha(1), sums["b0"].step2],
        4: [sums["b0"].step3],
        5: [line_b.gamma],
    }
    row = lax.broadcasted_iota(jnp.int32, vec.shape, 1)

    def fold(i):
        spread[i][1]()
        a, c = vec[...], vr[i]
        vec[...] = jnp.where(row < 1920, a + c, jnp.maximum(a, c))
        if i < 4:
            spread[i + 1][0]()

    n = len(IN_CHUNKS)
    for t in range(n + 2):
        if t < n:
            share_in.on(t, 1)
        for action in after.get(t, ()):
            action()
        if 1 <= t <= n:
            share_in.on(t - 1, 2)
        if 1 <= t <= 5:
            fold(t - 1)
    for c in range(len(OUT_CHUNKS)):
        share_out.wait(c, 2)
    own_in[1]()
    sum_m[...] = line_m.total(w0_s[...].astype(F32))
    sum_a[...] = line_b.total(Ha[0, :r, :].astype(F32))
    for c in range(n):
        share_in.wait(c, 2)


def back(number, vectors, live, geb, tops, gout, midway, sec, firstT, x, mine, whole0, h1, h2, h3, O_low, qkvs, atts, lses, Ws, length):
    D = gout.shape[1]
    cw = Ws[0].shape[0] // 4
    cm = h2.shape[1]
    heads = cw // HD
    r = D // 8
    vm = pltpu.VMEM
    dma = pltpu.SemaphoreType.DMA
    return pl.pallas_call(
        functools.partial(back_kernel, length, heads),
        out_shape=(shape((3 * TOK, D), BF), shape((3 * TOK, D), BF), shape((r, 4 * cw), F32), shape((r, cm), F32), shape((16, 2048), F32)),
        in_specs=[VM] * 4 + [HB] * 27,
        out_specs=(HB, HB, VM, VM, VM),
        input_output_aliases={14: 0},
        scratch_shapes=[vm((TOK, D), BF), vm((TOK, D), F32), vm((TOK, D), F32), vm((D, TOK), BF), vm((D, TOK), BF), vm((TOK, D), BF),
                        vm((2, 4 * cw, D), BF), vm((2, 3 * heads, TOK, HD), BF), vm((2, TOK, cw), BF), vm((2, TOK, 128), F32),
                        vm((heads, TOK, HD), BF), vm((2, TOK, 3 * cw), BF), vm((-(-cw // 128) * 128, TOK), F32), vm((-(-cw // 128) * 128, TOK), F32), vm((4 * r, 4 * cw), BF),
                        vm((4, 4 * r, 4 * cw), BF), vm((4, 3 * r, 4 * cw), BF), vm((2, 4 * r, cm), BF), vm((2, 3 * r, cm), BF),
                        vm((5, r, 4 * cw), BF), vm((5, r, cm), BF), vm((5, 16, 2048), F32), vm((r, cm), BF), vm((r, cm), BF),
                        dma((32,)), dma((COPIES,)), dma((COPIES,))],
        compiler_params=pltpu.CompilerParams(vmem_limit_bytes=63 * 2**20, collective_id=number, has_side_effects=True),
        cost_estimate=pl.CostEstimate(flops=4 * 2 * TOK * (D * cw * 8 + heads * 5 * TOK * HD * 6), bytes_accessed=60 * 2**20, transcendentals=4 * heads * TOK * TOK),
        name="back",
    )(vectors, live, geb, tops, gout, midway, sec, firstT, x, mine, whole0, h1, h2, h3, O_low, *Ws, *qkvs, *atts, *lses)


class Spreading:
    def __init__(self, wires, piece, W):
        rows = W.shape[0] // 8
        one, two = cut_rows(rows)
        d = wires.d
        at = lambda mask, lo=0, n=rows: W.at[pl.ds(pl.multiple_of((d ^ mask) * rows + lo, 16), n), :]
        self.own = wires.local(piece, at(0), d >= 0)
        self.s0 = [wires.swap(piece, at(0), dp=m) for m in (2, 4, 1)]
        self.s1 = [wires.swap(at(2, 0, one), at(2, 0, one), dp=4), wires.swap(at(4, one, two), at(4, one, two), dp=2)]
        self.s1c = [wires.swap(at(m), at(m), dp=1) for m in (2, 4)]
        self.s2 = wires.swap(at(6), at(6), dp=1)

    def step0(self):
        self.own[0]()
        for s, _ in self.s0:
            s()

    def landed(self):
        for _, w in self.s0 + [self.own]:
            w()

    def go_on(self):
        for s, _ in self.s1 + self.s1c:
            s()

    def step1(self):
        for _, w in self.s0:
            w()
        self.go_on()

    def step2(self):
        for _, w in self.s1:
            w()
        self.s2[0]()

    def finish(self, own=True):
        for _, w in self.s1c + [self.s2] + [self.own] * own:
            w()


class Moves:
    def __init__(self, sem):
        self.sem, self.made = sem, {}

    def add(self, key, src, dst):
        self.made[key] = pltpu.make_async_copy(src, dst, self.sem.at[len(self.made)])

    def start(self, *keys):
        for k in keys:
            self.made[k].start()

    def wait(self, *keys):
        for k in keys:
            self.made[k].wait()


def front_kernel(length, heads, vectors, live, bias_own, x, cot, qw, kw, vw, ow, mw, *rest):
    (qkv0, qkv1, qkv2, qkv3, att0, att1, att2, att3, lse0, lse1, lse2, lse3, firstT, second, secondT, midway, Wa0, Wa1, Wa2, Wa3, Wm1, Zm2, gout, goutT,
     tops, bias_all, gout_s, goutT_s, x_s, first_s, T_s, second_s, acc, W, Za, Zm1, qkv_s, att_s, lse_s, bias, l_sem, s_sem, r_sem) = rest
    cw = heads * HD
    D = x_s.shape[1]
    wires, moves = Wires(s_sem, r_sem), Moves(l_sem)
    d, z = wires.d, wires.z

    def own_rows(ref):
        n = ref.shape[0] // 8
        return pl.ds(pl.multiple_of(d * n, 16), n)

    for i, ref in enumerate((qw, kw, vw, ow)):
        moves.add(f"w{i}", ref, W.at[0, pl.ds(i * cw, cw), :])
    moves.add("x", x, x_s)
    moves.add("cot", cot, gout_s)
    moves.add("gout", gout_s, gout)
    moves.add("goutT", goutT_s, goutT)
    gain1, shift1, gain2, shift2, out_b = [vectors[n:n + 1, :] for n in range(5)]
    moves.add("oW0", W.at[0], Wa0)
    for k, (a, b, c) in enumerate(((qkv0, att0, lse0), (qkv1, att1, lse1), (qkv2, att2, lse2), (qkv3, att3, lse3))):
        moves.add(f"qkv{k}", qkv_s.at[k], a)
        moves.add(f"att{k}", att_s.at[k], b)
        moves.add(f"lse{k}", lse_s.at[k], c)
    for k, ref in enumerate((Wa1, Wa2, Wa3)):
        moves.add(f"oW{k + 1}", W.at[k + 1], ref)
    moves.add("firstT", T_s, firstT)
    moves.add("second", second_s, second)
    moves.add("secondT", T_s, secondT)
    moves.add("midway", acc, midway)
    moves.start("w0", "w1", "w2", "w3", "x", "cot")

    zb = [wires.swap(bias.at[0], bias.at[k], z=k) for k in (1, 2, 3)]
    a_piece, m_piece = W.at[0, own_rows(W.at[0]), :], mw.at[own_rows(mw), :]
    za = [wires.swap(a_piece, Za.at[0], z=1), wires.swap(a_piece, Za.at[1], z=2), wires.swap(Za.at[1], Za.at[2], z=1)]
    zm = [wires.swap(m_piece, Zm1, z=1), wires.swap(m_piece, Zm2, z=2)]
    ga = {k: Spreading(wires, Za.at[k - 1], W.at[k]) for k in (1, 2, 3)}
    gm = Spreading(wires, Zm1, Wm1)
    greet(d, z, MASKS)
    bias[0] = bias_own[...]
    for s, _ in zb:
        s()
    moves.wait("w0", "w1", "w2", "w3")
    za[0][0]()
    za[1][0]()
    moves.start("oW0")
    moves.wait("x")

    @pl.loop(0, TOK // RT)
    def _(i):
        part = pl.ds(pl.multiple_of(i * RT, RT), RT)
        xt = x_s[part, :].astype(F32)
        normed, _ = normalize(xt)
        f = normed * gain1 + shift1
        first_s[part, :] = f.astype(BF)
        T_s[:, part] = f.T.astype(BF)
        acc[part, :] = xt + out_b

    moves.start("firstT")
    for _, w in zb:
        w()
    bias_all[...] = bias[...]

    def turn_gout():
        moves.wait("cot")

        @pl.loop(0, TOK // RT)
        def _(i):
            part = pl.ds(pl.multiple_of(i * RT, RT), RT)
            g = gout_s[part, :].astype(F32) * live[...]
            gout_s[part, :] = g.astype(BF)
            goutT_s[:, part] = g.T.astype(BF)

        moves.start("gout", "goutT")

    def z_a3():
        za[1][1]()
        za[2][0]()

    todo = {
        0: [zm[0][0]],
        1: [za[0][1], ga[1].step0],
        5: [z_a3, ga[2].step0, turn_gout, ga[1].step1, ga[1].step2],
        10: [za[2][1], ga[3].step0],
        11: [],
        13: [ga[2].step1],
        15: [ga[2].step2, zm[1][0]],
        20: [ga[3].step1, zm[0][1], gm.step0],
        23: [ga[3].step2],
        30: [],
    }

    def tick(t):
        for action in todo.get(t, ()):
            action()

    for k in range(4):
        base = 10 * k
        Wk, qkv, att, lse = W.at[k], qkv_s.at[k], att_s.at[k], lse_s.at[k]
        if k:
            ga[k].finish()
            moves.start(f"oW{k}")
        tick(base)
        qb, vb = bias[k, 0:1, :cw], bias[k, 0:1, 384:384 + cw]

        @pl.loop(0, TOK // RT)
        def _(i):
            part = pl.ds(pl.multiple_of(i * RT, RT), RT)
            t = nt(first_s[part, :], Wk[:3 * cw, :])
            q = (t[:, :cw] + qb).astype(BF)
            kk = t[:, cw:2 * cw].astype(BF)
            v = (t[:, 2 * cw:] + vb).astype(BF)
            for h in range(heads):
                qkv[h, part, :] = q[:, h * HD:(h + 1) * HD]
                qkv[heads + h, part, :] = kk[:, h * HD:(h + 1) * HD]
                qkv[2 * heads + h, part, :] = v[:, h * HD:(h + 1) * HD]

        tick(base + 1)
        moves.start(f"qkv{k}")
        tops[k] = jnp.full(tops.shape[1:], -1e30, F32)

        @pl.loop(0, TOK // RT)
        def _(i):
            for n in range(3):
                pl.when(i == n)(functools.partial(tick, base + 2 + n))
            part = pl.ds(pl.multiple_of(i * RT, RT), RT)
            rid = lax.broadcasted_iota(jnp.int32, (RT, 1), 0) + i * RT
            cid = lax.broadcasted_iota(jnp.int32, (1, TOK), 1)
            res = []
            for h in range(heads):
                s = nt(qkv[h, part, :], qkv[heads + h])
                s = jnp.where(cid < length, s, -1e30)
                m = jnp.max(s, axis=1, keepdims=True)
                e = jnp.exp2((s - m) * (SC * LOG2E))
                l = jnp.sum(e, axis=1, keepdims=True)
                o = nn(e.astype(BF), qkv[2 * heads + h]) * (1.0 / l)
                res.append(o.astype(BF))
                lse[part, h:h + 1] = m * (SC * LOG2E) + jnp.log2(l)
                tops[k, h:h + 1, :] = jnp.maximum(tops[k, h:h + 1, :], jnp.max(jnp.where(rid < length, m, -1e30)) * SC)
            a = jnp.concatenate(res, axis=1)
            att[part, :] = a
            acc[part, :] += nn(a, Wk[3 * cw:, :])

        moves.start(f"att{k}", f"lse{k}")
        tick(base + 5)

    moves.start("midway")
    moves.wait("firstT")

    @pl.loop(0, TOK // RT)
    def _(i):
        part = pl.ds(pl.multiple_of(i * RT, RT), RT)
        normed, _ = normalize(acc[part, :])
        f = normed * gain2 + shift2
        second_s[part, :] = f.astype(BF)
        T_s[:, part] = f.T.astype(BF)

    moves.start("second", "secondT")
    gm.landed()
    zm[1][1]()
    for k in range(4):
        moves.wait(f"qkv{k}", f"att{k}", f"lse{k}", f"oW{k}")
    moves.wait("second", "secondT", "midway", "gout", "goutT")


def front(number, vectors, live, bias_own, x, cot, qw, kw, vw, ow, mw, length):
    cw, D = qw.shape
    heads = cw // HD
    cm = mw.shape[0]
    vm = pltpu.VMEM
    dma = pltpu.SemaphoreType.DMA
    four = lambda s: (s,) * 4
    got = pl.pallas_call(
        functools.partial(front_kernel, length, heads),
        out_shape=(*four(shape((3 * heads, TOK, HD), BF)), *four(shape((TOK, cw), BF)), *four(shape((TOK, 128), F32)),
                   shape((D, TOK), BF), shape((TOK, D), BF), shape((D, TOK), BF), shape((TOK, D), F32), *four(shape((4 * cw, D), BF)),
                   shape((cm, D), BF), shape((cm // 8, D), BF), shape((TOK, D), BF), shape((D, TOK), BF), shape((4, heads, 128), F32), shape((4, 8, 2048), F32)),
        in_specs=[VM] * 3 + [HB] * 7,
        out_specs=(HB,) * 24 + (VM,) * 2,
        scratch_shapes=[vm((TOK, D), BF), vm((D, TOK), BF), vm((TOK, D), BF), vm((TOK, D), BF), vm((D, TOK), BF), vm((TOK, D), BF), vm((TOK, D), F32),
                        vm((4, 4 * cw, D), BF), vm((3, cw // 2, D), BF), vm((cm // 8, D), BF), vm((4, 3 * heads, TOK, HD), BF),
                        vm((4, TOK, cw), BF), vm((4, TOK, 128), F32), vm((4, 8, 2048), F32), dma((32,)), dma((64,)), dma((64,))],
        compiler_params=pltpu.CompilerParams(vmem_limit_bytes=62 * 2**20, collective_id=number, has_side_effects=True),
        cost_estimate=pl.CostEstimate(flops=4 * 2 * TOK * (D * cw * 4 + heads * 2 * TOK * HD * 6), bytes_accessed=60 * 2**20, transcendentals=4 * heads * TOK * TOK),
        name="front",
    )(vectors, live, bias_own, x, cot, qw, kw, vw, ow, mw)
    return got[:4], got[4:8], got[8:12], got[12:16], got[16:20], got[20:22], got[22:24], got[24], got[25]


def middle_kernel(fw, live, vectors, bias_all, second, secondT, gout, goutT, midway, Wm0, Wm1, Zm2, *rest):
    (mine, sec, O0, H1, H2, H3, geb, part_sum, Wg2, Wg3, Zm3, Wg1, second_s, secondT_s, gout_s, goutT_s, mlp, sec_s, mine_s, W, act_s, slope_s, gpre_s, out_s,
     Hm, Lm, l_sem, s_sem, r_sem) = rest
    D = second_s.shape[1]
    hid = W.shape[1] // 2
    cut = fw // 128 * 128
    tail = fw - cut
    r = D // 8
    wires, moves = Wires(s_sem, r_sem), Moves(l_sem)
    d, z = wires.d, wires.z
    Ws = (Wm0, Wg1, Wg2, Wg3)
    for key, a, b in (("second", second, second_s), ("secondT", secondT, secondT_s), ("gout", gout, gout_s), ("goutT", goutT, goutT_s), ("midway", midway, mlp)):
        moves.add(key, a, b)
    for k in range(4):
        moves.add(f"W{k}", Ws[k], W.at[k % 2])
    moves.add("mine", mine_s, mine)
    moves.add("sec", sec_s, sec)
    moves.add("h1", Hm.at[1, pl.ds(0, r), :], H1)
    moves.add("h2", Hm.at[2], H2)
    moves.add("h3", Hm.at[3], H3)
    slot = jnp.where(z == 0, 0, jnp.where(z == 3, 1, 2))
    used = (z == 0) | (z == 3) | (z == 1 + d % 2)
    own_out = wires.local(mine_s, O0.at[pl.ds(pl.multiple_of(slot * TOK, 256), TOK), :], used)
    share = Sharing(wires, mine_s, O0, OUT_CHUNKS)
    z3 = wires.swap(Zm2, Zm3, z=1)
    g1, g2, g3 = Spreading(wires, Zm2, Wg1), Spreading(wires, Zm2, Wg2), Spreading(wires, Zm3, Wg3)
    exchange = [wires.swap(out_s.at[k % 2], Hm.at[k], dp=1) for k in range(4)]
    sums = [Summing(wires, Hm.at[k], Lm.at[k]) for k in (0, 1)]
    moves.start("second", "W0", "midway", "gout", "goutT", "secondT")
    greet(d, z, MASKS)
    g1.go_on()
    z3[0]()
    sec_s[...] = jnp.zeros_like(sec_s)
    geb[...] = jnp.zeros_like(geb)
    moves.wait("second", "midway")

    def forward(k, tick):
        b = k % 2
        moves.wait(f"W{k}")
        eb = bias_all[k, 0:1, 768:768 + hid]

        @pl.loop(0, TOK // RT)
        def _(i):
            tick(i)
            rows = pl.ds(pl.multiple_of(i * RT, RT), RT)
            act, slope = gelu_parts(nt(second_s[rows, :], W[b, :hid, :]) + eb)
            act_s[b, rows, :] = act.astype(BF)
            slope_s[b, rows, :] = slope.astype(BF)
            mlp[rows, :] += nn(act_s[b, rows, :], W[b, hid:, :])

    def grads(k, half):
        b = k % 2
        for t in range(2):
            q = 4 * t + 1 - half
            lhs = lambda ref: jnp.concatenate([ref[pl.ds(pl.multiple_of((d ^ p) * r, 16), r), :] for p in (q, q + 2)], axis=0)
            place = pl.ds(t * 2 * r, 2 * r)
            ve, vs = nn(lhs(secondT_s), gpre_s[b]), nn(lhs(goutT_s), act_s[b])
            last = jnp.concatenate([ve[:, cut:fw], vs[:, cut:fw], jnp.zeros((2 * r, 128 - 2 * tail), F32)], axis=1)
            to = out_s.at[b] if half == 0 else Hm.at[k]
            for lo, v in ((0, ve[:, :cut]), (cut, vs[:, :cut]), (2 * cut, last)):
                n = v.shape[1]
                if half:
                    v = v + to[place, lo:lo + n].astype(F32)
                to[place, lo:lo + n] = v.astype(BF)

    def back_a(k, tick):
        b = k % 2

        @pl.loop(0, TOK // RT)
        def _(i):
            tick(i)
            rows = pl.ds(pl.multiple_of(i * RT, RT), RT)
            gp = nt(gout_s[rows, :], W[b, hid:, :]) * slope_s[b, rows, :].astype(F32)
            geb[k] += jnp.sum(gp, axis=0, keepdims=True)
            gpre_s[b, rows, :] = gp.astype(BF)

        grads(k, 0)
        exchange[k][0]()

        @pl.loop(0, TOK // RT)
        def _(i):
            tick(i + 3)
            rows = pl.ds(pl.multiple_of(i * RT, RT), RT)
            sec_s[rows, :] += nn(gpre_s[b, rows, :], W[b, :hid, :])

    def back_b(k):
        exchange[k][1]()
        grads(k, 1)

    def ticks(table):
        def tick(i):
            for n, actions in table.items():
                def run():
                    for a in actions:
                        a()
                pl.when(i == n)(run)
        return tick

    none = ticks({})
    forward(0, ticks({2: [g2.step0]}))
    moves.wait("gout", "goutT", "secondT")
    back_a(0, ticks({2: [g1.step2]}))
    g1.finish(False)
    moves.start("W1")
    forward(1, ticks({1: [g2.step1], 2: [z3[1], g3.step0]}))
    back_b(0)
    back_a(1, ticks({1: [g2.step2], 4: [g3.step1]}))
    g2.finish()
    moves.start("W2")
    forward(2, ticks({2: [g3.step2]}))
    back_b(1)
    g3.finish()
    moves.start("W3")
    sums[0].step1()
    forward(3, none)

    @pl.loop(0, TOK // RT)
    def _(i):
        rows = pl.ds(pl.multiple_of(i * RT, RT), RT)
        mine_s[rows, :] = ((mlp[rows, :] + vectors[5:6, :]) * live[...]).astype(BF)
        pl.when(i == 0)(lambda: share.start(0, 0))
        pl.when(i == 1)(lambda: share.start(1, 0))

    own_out[0]()
    moves.start("mine")
    sums[1].step1()
    back_a(2, none)
    sums[0].step2()
    back_a(3, none)
    moves.start("sec")
    back_b(2)
    moves.start("h2")
    sums[0].step3()
    sums[1].step2()
    back_b(3)
    moves.start("h3")
    sums[1].step3()
    moves.start("h1")
    part_sum[...] = Hm[0, :r, :]
    share.wait(0, 0)
    share.wait(1, 0)
    own_out[1]()
    moves.wait("h1", "h2", "h3", "sec", "mine")


def middle(number, fw, live, vectors, bias_all, second, secondT, gout, goutT, midway, Wm0, Wm1, Zm2):
    D = second.shape[1]
    cm, hid = Wm0.shape[0], Wm0.shape[0] // 2
    cg = fw // 128 * 256 + 128
    r = D // 8
    vm = pltpu.VMEM
    dma = pltpu.SemaphoreType.DMA
    got = pl.pallas_call(
        functools.partial(middle_kernel, fw),
        out_shape=(shape((TOK, D), BF), shape((TOK, D), F32), shape((3 * TOK, D), BF), shape((r, cg), BF), shape((4 * r, cg), BF), shape((4 * r, cg), BF), shape((4, 1, hid), F32), shape((r, cg), BF),
                   shape((cm, D), BF), shape((cm, D), BF), shape((cm // 8, D), BF), shape((cm, D), BF)),
        in_specs=[VM] * 3 + [HB] * 8,
        out_specs=(HB,) * 6 + (VM,) * 2 + (HB,) * 4,
        input_output_aliases={9: 11},
        scratch_shapes=[vm((TOK, D), BF), vm((D, TOK), BF), vm((TOK, D), BF), vm((D, TOK), BF), vm((TOK, D), F32), vm((TOK, D), F32), vm((TOK, D), BF), vm((2, cm, D), BF),
                        vm((2, TOK, hid), BF), vm((2, TOK, hid), BF), vm((2, TOK, hid), BF), vm((2, 4 * r, cg), BF),
                        vm((4, 4 * r, cg), BF), vm((2, 3 * r, cg), BF), dma((32,)), dma((72,)), dma((72,))],
        compiler_params=pltpu.CompilerParams(vmem_limit_bytes=63 * 2**20, collective_id=number, has_side_effects=True),
        cost_estimate=pl.CostEstimate(flops=4 * 2 * 9 * TOK * D * fw, bytes_accessed=60 * 2**20, transcendentals=4 * TOK * fw),
        name="middle",
    )(live, vectors, bias_all, second, secondT, gout, goutT, midway, Wm0, Wm1, Zm2)
    return got[:8]


class General:
    def __init__(self, groups, attn_own, mlp_own):
        self.groups = groups
        self.attn, self.mlp = self.spread(attn_own), self.spread(mlp_own)

    def vectors(self, own):
        every = lax.all_gather(own, "tensor")
        return [every[i] for i in range(self.groups)]

    def spread(self, own):
        d, count = lax.axis_index("dp"), lax.axis_size("dp")
        rows = own.shape[0] // count
        piece = lax.dynamic_slice_in_dim(own, d * rows, rows, 0)
        piece = lax.all_gather(piece, "tensor")
        whole = lax.all_gather(piece, "dp", axis=1, tiled=True)
        return [whole[i] for i in range(self.groups)]

    def reduce(self, parts):
        part = lax.psum_scatter(jnp.stack(parts), "dp", scatter_dimension=1, tiled=True)
        return lax.psum_scatter(part, "tensor", scatter_dimension=0, tiled=True)[0].astype(F32)

    def collect(self, grad_attn, grad_mlp):
        return self.reduce(grad_attn), self.reduce(grad_mlp)

    def by_index(self, items):
        return jnp.stack(items)

    def share(self, mine):
        every = lax.all_gather(mine, "tensor")
        middle = 1 + lax.axis_index("dp") % 2
        return jnp.stack([every[0], every[self.groups - 1], lax.dynamic_index_in_dim(every, middle, 0, keepdims=False)])


def shards(images, counts, cotangent, query_w, query_b, key_w, value_w, value_b, out_w, out_b, norm1_gain, norm1_shift,
           norm2_gain, norm2_shift, expand_w, expand_b, shrink_w, shrink_b):
    slots, length, width = images.shape
    groups = lax.axis_size("tensor")
    d, z = lax.axis_index("dp"), lax.axis_index("tensor")
    cw, fw = query_w.shape[1], expand_w.shape[1]
    heads = cw // HD
    cut = fw // 128 * 128
    slot, used = slot_table(d, groups)
    live = jnp.where(used & (slot < counts[0]), 1.0, 0.0).astype(F32)
    pad = lambda a: jnp.pad(a, ((0, TOK - length), (0, 0)))

    x_low = pad(lax.dynamic_index_in_dim(images, slot, 0, keepdims=False))
    cot_low = pad(lax.dynamic_index_in_dim(cotangent, slot, 0, keepdims=False))
    if (groups, lax.axis_size("dp")) == (4, 8):
        blank = lambda n: jnp.zeros((n,), F32)
        bias_own = jnp.concatenate([query_b, blank(384 - cw), value_b, blank(384 - cw), expand_b, blank(1280 - fw)])
        deep = -fw % 16
        mlp_own = jnp.pad(jnp.stack([expand_w.T, shrink_w]), ((0, 0), (0, deep), (0, 0))).reshape(2 * (fw + deep), width)
        vectors = jnp.stack([norm1_gain, norm1_shift, norm2_gain, norm2_shift, out_b, shrink_b, shrink_b, shrink_b])
        qkvs, atts, lses, (first_t, second, second_t, midway), attn_ws, mlp_ws, (gout, gout_t), tops, bias_all = front(
            0, vectors, live[None, None], jnp.broadcast_to(bias_own, (8, 2048)), x_low, cot_low, query_w.T, key_w.T, value_w.T, out_w, mlp_own, length)
        mine, sec, out_low, h1, h2, h3, geb, part_sum = middle(1, fw, live[None, None], vectors, bias_all, second, second_t, gout, gout_t, midway, mlp_own, *mlp_ws)
        out_all, in_all, sum_attn, sum_mlp, vec = back(
            2, vectors, live[None, None], geb, jnp.where(live > 0.0, tops[:, :, 0], -1e30)[:, None],
            gout, midway, sec, first_t, x_low, mine, part_sum, h1, h2, h3, out_low, qkvs, atts, lses, attn_ws, length)
        outputs = out_all.reshape(3, TOK, width)[:, :length]
        input_grads = in_all.reshape(3, TOK, width)[:, :length].astype(F32)
        own = lax.dynamic_index_in_dim(vec, z, 0, keepdims=False)
        grad_query_b, grad_value_b, grad_expand_b, logit_top = own[:cw], own[384:384 + cw], own[768:768 + fw], own[1920:1920 + heads]
        tail = [vec[4 + i, :width] for i in range(6)]
    else:
        gout = cot_low * live.astype(BF)
        gout_t = gout.T
        attn_own = jnp.concatenate([query_w, key_w, value_w, out_w.T], axis=1)
        shrink_t = shrink_w.T
        mlp_own = jnp.concatenate([expand_w[:, :cut], shrink_t[:, :cut], expand_w[:, cut:], shrink_t[:, cut:]], axis=1)
        net = General(groups, attn_own, mlp_own)
        biases = net.vectors(jnp.concatenate([query_b, value_b, expand_b]))

        x = x_low.astype(F32)
        normed1, inverse1 = normalize(x)
        first = (normed1 * norm1_gain + norm1_shift).astype(BF)
        first_t = first.T
        acc = x + out_b
        kept, tops = [], []
        for k in range(groups):
            b = biases[k]
            qkv, att, lse, top, acc = attn_fwd(first, net.attn[k], b[None, :cw], b[None, cw:2 * cw], acc, length)
            kept.append((qkv, att, lse))
            tops.append(top[:, 0])
        midway = acc
        normed2, inverse2 = normalize(midway)
        second = (normed2 * norm2_gain + norm2_shift).astype(BF)
        second_t = second.T
        mlp = midway + shrink_b
        sec = jnp.zeros((TOK, width), F32)
        grad_mlp, geb = [], []
        for k in range(groups):
            grad, g_b, mlp, sec = mlp_call(second, second_t, gout, gout_t, net.mlp[k], biases[k][None, 2 * cw:], mlp, sec)
            grad_mlp.append(grad)
            geb.append(g_b[0, :fw])
        back2, gn2g, gn2s = norm_back(sec, normed2, inverse2, norm2_gain)
        gout32 = gout.astype(F32)
        gmid = gout32 + back2
        gmid_low = gmid.astype(BF)
        gmid_t = gmid_low.T
        acc = jnp.zeros((TOK, width), F32)
        grad_attn, gqb, gvb = [None] * groups, [None] * groups, [None] * groups
        for k in reversed(range(groups)):
            grad, g_q, g_v, acc = attn_bwd(gmid_low, gmid_t, first_t, net.attn[k], *kept[k], acc, length)
            grad_attn[k], gqb[k], gvb[k] = grad, g_q[0], g_v[0]
        back1, gn1g, gn1s = norm_back(acc, normed1, inverse1, norm1_gain)
        input_grad = ((gmid + back1) * live)[:length].astype(BF)

        outputs = net.share((mlp[:length] * live).astype(BF))
        input_grads = net.share(input_grad).astype(F32)
        sum_attn, sum_mlp = net.collect(grad_attn, grad_mlp)
        flat = lambda items: net.by_index(items).reshape(-1)
        vector = jnp.concatenate([flat(gqb), flat(gvb), flat(geb), jnp.sum(gmid, axis=0), jnp.sum(gout32, axis=0), gn1g, gn1s, gn2g, gn2s])
        vector = lax.psum(vector, ("dp", "tensor"))
        part = lambda start, size: lax.dynamic_slice_in_dim(vector, start, size, 0)
        whole, hidden = cw * groups, fw * groups
        tail = [vector[2 * whole + hidden + i * width:][:width] for i in range(6)]
        logit_top = lax.pmax(jnp.where(live > 0.0, net.by_index(tops), -1e30), ("dp", "tensor"))
        logit_top = lax.dynamic_index_in_dim(logit_top, z, 0, keepdims=False)
        grad_query_b, grad_value_b, grad_expand_b = part(z * cw, cw), part(whole + z * cw, cw), part(2 * whole + z * fw, fw)
    factor = jnp.sqrt(clip_limit / jnp.maximum(logit_top, clip_limit))
    column_factor = jnp.repeat(factor, HD)
    clipped_query = (query_w.astype(F32) * column_factor).astype(BF)
    clipped_key = (key_w.astype(F32) * column_factor).astype(BF)
    unpack = lambda a, i: jnp.concatenate([a[:, i * cut:(i + 1) * cut], a[:, 2 * cut + i * (fw - cut):][:, :fw - cut]], axis=1)
    return (outputs, input_grads, sum_attn[:, :cw], grad_query_b, sum_attn[:, cw:2 * cw], sum_attn[:, 2 * cw:3 * cw], grad_value_b,
            sum_attn[:, 3 * cw:].T, tail[0], tail[2], tail[3], tail[4], tail[5], unpack(sum_mlp, 0), grad_expand_b, unpack(sum_mlp, 1).T,
            tail[1], clipped_query, clipped_key)


def solution(mesh):
    columns, rows, vector = P(None, "tensor"), P("tensor", None), P("tensor")
    whole = P("dp", None, None)
    return jax.shard_map(
        shards, mesh=mesh,
        in_specs=(whole, P("dp"), whole, columns, vector, columns, columns, vector, rows, P(), P(), P(), P(), P(), columns, vector, rows, P()),
        out_specs=(whole, whole, P("dp", "tensor"), vector, P("dp", "tensor"), P("dp", "tensor"), vector, P("tensor", "dp"), P(), P(), P(), P(), P(),
                   P("dp", "tensor"), vector, P("tensor", "dp"), P(), columns, columns),
        check_vma=False)
```
